32 devices in a mesh: dp: 4 (over y, x), fsdp: 8 (over z, core).
Axes of the slice: x: 2, y: 2, z: 4, core: 2. Of those that a mesh axis runs over, the one named last changes fastest.
Arguments:
- tokens: bfloat16 [2, 96, 128, 768], P(None, ('dp', 'fsdp')), may hold values from -6 to 6
- timesteps: int32 [2, 96], P(None, ('dp', 'fsdp')), may hold values from 0 to 999
- segments: int32 [2, 96, 128], P(None, ('dp', 'fsdp')), may hold values from 0 to 7, never falling along the last dimension, each value on 1 to 32 neighbouring positions
- padding: int32 [2, 96, 128], P(None, ('dp', 'fsdp')), may hold values 0 or 1
- cotangent: bfloat16 [2, 96, 128, 768], P(None, ('dp', 'fsdp')), may hold values from -6 to 6
- step_table: bfloat16 [1000, 768], P(None, 'fsdp'), may hold values from -6 to 6
- triple_weight: bfloat16 [768, 2304], P('fsdp'), may hold values from -0.21875 to 0.21875
- query_bias: bfloat16 [768], P('fsdp'), may hold values from -3 to 3
- value_bias: bfloat16 [768], P('fsdp'), may hold values from -3 to 3
- output_weight: bfloat16 [768, 768], P('fsdp'), may hold values from -0.875 to 0.875
- output_bias: bfloat16 [768], P('fsdp'), may hold values from -3 to 3
- first_gain: bfloat16 [768], P('fsdp'), may hold values from 0.5 to 1.5
- first_shift: bfloat16 [768], P('fsdp'), may hold values from -3 to 3
- second_gain: bfloat16 [768], P('fsdp'), may hold values from 0.5 to 1.5
- second_shift: bfloat16 [768], P('fsdp'), may hold values from -3 to 3
- hidden_weight: bfloat16 [768, 3072], P('fsdp'), may hold values from -0.21875 to 0.21875
- hidden_bias: bfloat16 [3072], P('fsdp'), may hold values from -3 to 3
- down_weight: bfloat16 [3072, 768], P('fsdp'), may hold values from -0.109375 to 0.109375
- down_bias: bfloat16 [768], P('fsdp'), may hold values from -3 to 3
Outputs:
- result_rows: bfloat16 [2, 96, 128, 768], P(None, ('dp', 'fsdp'))
- input_grad: bfloat16 [2, 96, 128, 768], P(None, ('dp', 'fsdp'))
- table_grad: float32 [1000, 768], P(None, 'fsdp')
- triple_grad: float32 [768, 2304], P('fsdp')
- query_bias_grad: float32 [768], P('fsdp')
- value_bias_grad: float32 [768], P('fsdp')
- output_weight_grad: float32 [768, 768], P('fsdp')
- output_bias_grad: float32 [768], P('fsdp')
- first_gain_grad: float32 [768], P('fsdp')
- first_shift_grad: float32 [768], P('fsdp')
- second_gain_grad: float32 [768], P('fsdp')
- second_shift_grad: float32 [768], P('fsdp')
- hidden_weight_grad: float32 [768, 3072], P('fsdp')
- hidden_bias_grad: float32 [3072], P('fsdp')
- down_weight_grad: float32 [3072, 768], P('fsdp')
- down_bias_grad: float32 [768], P('fsdp')
The draws below stay inside these ranges and needn't reach their ends.
Inputs may be any that keep to these rules, and one draw needn't show every extreme that they name: `segments`: within each row of 128 tokens the numbers never fall; each sentence holds 1 to 32 tokens. 1 marks a padding token.
All inputs are finite; a program needn't handle non-finite values. No bound on the sum of `padding` on one device may be relied on, other than what follows from the above.
Results may differ from the reference program's by a relative error of at most 0.012.
The reference program's roundings to bfloat16 on the way count: a program that leaves them out, or rounds other values in their place, can miss the bound.
Values may be sent and summed in bfloat16 or wider, within the bound.
No kernel may reach another device: no remote copies, remote signals or barrier semaphores. Data moves between devices by JAX's collectives and lax.ppermute only.
A program may use at most 192 MiB of HBM per device.

```python
import math
import jax
import jax.numpy as jnp
import numpy as np
from jax import lax

D = 768
HEADS = 12
HD = 64
FF = 3072
TSTEPS = 1000
L = 128
MB = 2
ROWS = 96


def with_ends(array, key, smallest, high):
    place = [jax.random.randint(jax.random.fold_in(key, axis), (), 0, length) for axis, length in enumerate(array.shape)]
    widest = array.shape.index(max(array.shape))
    neighbour = place[:widest] + [(place[widest] + 1) % array.shape[widest]] + place[widest + 1:]
    return array.at[tuple(place)].set(smallest).at[tuple(neighbour)].set(high)


def spiked(values, rng, source, target, parts, factor):
    owner, partner = [(jnp.arange(values.shape[axis_at]) // (values.shape[axis_at] // parts)).reshape([-1 if axis == axis_at else 1 for axis in range(values.ndim)]) for axis_at in (source, target)]
    chosen = jax.random.permutation(rng, parts)[partner]
    strong = (owner == chosen) | (owner == (partner + parts // 2) % parts)
    return jnp.where(strong, factor * values, values)


def block_scale(stream_key, shape, cuts, low, top_value):
    factor_of, own = 1.0, jax.random.fold_in(stream_key, 6)
    for position, parts in cuts:
        steps = jnp.exp(jax.random.uniform(jax.random.fold_in(own, position), (parts,), jnp.float32, low / len(cuts), top_value / len(cuts)))
        factor_of = factor_of * jnp.repeat(steps, shape[position] // parts).reshape([-1 if axis == position else 1 for axis in range(len(shape))])
    return factor_of


def length_profile(count, total, reach, slope):
    weights = [(1 << 20) // math.isqrt(standing ** slope) + 1 for standing in range(2, count + 1)]
    surplus, counts = total - reach - (count - 1), [1] * (count - 1)
    while surplus > 0:
        movable = [i for i in range(count - 1) if counts[i] < reach]
        mass, budget = sum([weights[i] for i in movable]), surplus
        for i in movable:
            extra = min(reach - counts[i], max(1, budget * weights[i] // mass), surplus)
            counts[i] = counts[i] + extra
            surplus = surplus - extra
    return np.array([reach] + counts)


def ragged_sizes(key, number_of, total, bound, lean):
    if number_of == 2:
        one = jax.random.randint(key, (), max(1, total - bound), min(bound, total - 1) + 1)
        return jnp.stack([one, total - one])
    sizes = jnp.asarray(length_profile(number_of, total, bound, lean), jnp.int32)
    twos = (number_of - 1) // 2
    giver, receiver = sizes[1:1 + 2 * twos:2], sizes[2:2 + 2 * twos:2]
    margin = jnp.minimum(giver - 1, bound - receiver)
    moved = jax.random.randint(jax.random.fold_in(key, 1), (twos,), 0, 1 << 20) % (margin + 1)
    sizes = sizes.at[1:1 + 2 * twos:2].set(giver - moved).at[2:2 + 2 * twos:2].set(receiver + moved)
    return sizes[jax.random.permutation(jax.random.fold_in(key, 2), number_of)]


def normal_values(key, dims, width, bound, cuts=(), kind=jnp.bfloat16):
    factor_of = block_scale(key, dims, cuts, -0.22, 0.18) if cuts else 1.0
    entries = jax.random.normal(key, dims, jnp.float32) * width * factor_of
    return jnp.minimum(jnp.maximum(entries, -bound), bound).astype(kind)


def bell_draw_with(rng, dims, spread, reach, pieces, heavy, kind=jnp.bfloat16):
    entries = spread * jax.random.normal(rng, dims, jnp.float32)
    if pieces:
        entries = entries * block_scale(rng, dims, pieces, -0.22, 0.18)
    return jnp.clip(spiked(entries, jax.random.fold_in(rng, 3), *heavy), -reach, reach).astype(kind)


def setup_inputs(seed: int = 0) -> dict:
    splits = jax.random.split(jax.random.key(seed), 20)
    tokens = bell_draw_with(splits[0], (MB, ROWS, L, D), 1.0, 6.0, ((1, 32),), (1, 3, 32, 2.75))
    timesteps = with_ends(jax.random.randint(splits[1], (MB, ROWS), 0, TSTEPS), jax.random.fold_in(splits[1], 1), 0, TSTEPS - 1).astype(jnp.int32)
    segments = jax.vmap(lambda own: jnp.searchsorted(jnp.cumsum(ragged_sizes(own, 8, L, L // 4, 1)), jnp.arange(L), side="right"))(jax.random.split(splits[2], MB * ROWS)).reshape((MB, ROWS, L)).astype(jnp.int32)
    padding = with_ends((jax.random.randint(splits[3], (MB, ROWS, L), 0, 8) < 1).astype(jnp.int32), jax.random.fold_in(splits[3], 1), 0, 1)
    cotangent = bell_draw_with(splits[4], (MB, ROWS, L, D), 1.0, 6.0, ((1, 32),), (1, 3, 32, 2.75))
    step_table = normal_values(splits[5], (TSTEPS, D), 1.0, 6.0, ((1, 8),))
    triple_weight = normal_values(splits[6], (D, 3 * D), D ** -0.5, 0.21875, ((0, 8),))
    query_bias = normal_values(splits[7], (D,), 0.5, 3.0, ((0, 8),))
    value_bias = normal_values(splits[8], (D,), 0.5, 3.0, ((0, 8),))
    output_weight = normal_values(splits[9], (D, D), (D // 16) ** -0.5, 0.875, ((0, 8),))
    output_bias = normal_values(splits[10], (D,), 0.5, 3.0, ((0, 8),))
    first_gain = jnp.clip(1.0 + 0.1 * jax.random.normal(splits[11], (D,), jnp.float32), 0.5, 1.5).astype(jnp.bfloat16)
    first_shift = normal_values(splits[12], (D,), 0.5, 3.0, ((0, 8),))
    second_gain = jnp.clip(1.0 + 0.1 * jax.random.normal(splits[13], (D,), jnp.float32), 0.5, 1.5).astype(jnp.bfloat16)
    second_shift = normal_values(splits[14], (D,), 0.5, 3.0, ((0, 8),))
    hidden_weight = normal_values(splits[15], (D, FF), D ** -0.5, 0.21875, ((0, 8),))
    hidden_bias = normal_values(splits[16], (FF,), 0.5, 3.0, ((0, 8),))
    down_weight = normal_values(splits[17], (FF, D), FF ** -0.5, 0.109375, ((0, 8),))
    down_bias = normal_values(splits[18], (D,), 0.5, 3.0, ((0, 8),))
    return dict(tokens=tokens, timesteps=timesteps, segments=segments, padding=padding, cotangent=cotangent, step_table=step_table, triple_weight=triple_weight, query_bias=query_bias, value_bias=value_bias, output_weight=output_weight, output_bias=output_bias, first_gain=first_gain, first_shift=first_shift, second_gain=second_gain, second_shift=second_shift, hidden_weight=hidden_weight, hidden_bias=hidden_bias, down_weight=down_weight, down_bias=down_bias)


@jax.custom_vjp
def low(v):
    return lax.optimization_barrier(v.astype(jnp.bfloat16)).astype(jnp.float32)

@jax.custom_vjp
def low_back(v):
    return v

def low_keep(v):
    return (low(v), None)

def low_pass(kept, grad):
    return (grad,)

def back_keep(v):
    return (v, None)

def back_low(kept, grad):
    return (low(grad),)
low.defvjp(low_keep, low_pass)
low_back.defvjp(back_keep, back_low)
highest = lax.Precision.HIGHEST
norm_eps = 1e-05
masked_score = -1e+30

def layer_norm(values, gain, shift):
    average = lax.optimization_barrier(jnp.mean(values, axis=-1, keepdims=True))
    centered = values - average
    variance = lax.optimization_barrier(jnp.mean(centered * centered, axis=-1, keepdims=True))
    return centered * lax.rsqrt(variance + norm_eps) * gain + shift

def smooth_gate(values):
    return jax.nn.gelu(values, approximate=True)

def widen(array_in):
    return array_in.astype(jnp.float32)

def block_forward(weight_set, tokens_block, steps_block, segment_block, padding_block):
    table_full, triple_full, query_add, value_add, output_full, output_add, first_scale, first_offset, second_scale, second_offset, hidden_full, hidden_add, down_full, down_add = weight_set
    row_count, length, model_width = tokens_block.shape
    residual_in = tokens_block + jnp.take(table_full, steps_block, axis=0)[:, None, :]
    normed = low(layer_norm(residual_in, first_scale, first_offset))
    triple = jnp.einsum('rld,de->rle', normed, triple_full, precision=highest)
    triple = triple + jnp.concatenate([query_add, jnp.zeros_like(query_add), value_add])
    triple = low(low_back(triple))
    heads = triple.reshape(row_count, length, 3, HEADS, HD)
    queries = heads[:, :, 0]
    key_heads = heads[:, :, 1]
    values = heads[:, :, 2]
    scores = jnp.einsum('rqhd,rkhd->rhqk', queries, key_heads, precision=highest) * (1.0 / math.sqrt(HD))
    scores = low_back(scores)
    same_segment = segment_block[:, :, None] == segment_block[:, None, :]
    diagonal = jnp.eye(length, dtype=bool)
    allowed = same_segment & ((padding_block[:, None, :] == 0) | diagonal[None])
    scores = jnp.where(allowed[:, None], scores, masked_score)
    largest = lax.optimization_barrier(jnp.max(scores, axis=-1, keepdims=True))
    exponent = jnp.exp(scores - largest)
    attention = exponent / lax.optimization_barrier(jnp.sum(exponent, axis=-1, keepdims=True))
    attended = jnp.einsum('rhqk,rkhd->rqhd', low(attention), values, precision=highest)
    attended = low(low_back(attended.reshape(row_count, length, model_width)))
    branch = jnp.einsum('rlc,cd->rld', attended, output_full, precision=highest) + output_add
    branch = low_back(branch)
    middle = residual_in + branch
    normed_two = low(layer_norm(middle, second_scale, second_offset))
    hidden = jnp.einsum('rld,df->rlf', normed_two, hidden_full, precision=highest) + hidden_add
    hidden = low_back(hidden)
    active = low(smooth_gate(hidden))
    down_part = jnp.einsum('rlf,fd->rld', active, down_full, precision=highest) + down_add
    down_part = low_back(down_part)
    return middle + down_part

def reference(tokens, timesteps, segments, padding, cotangent, step_table, triple_weight, query_bias, value_bias, output_weight, output_bias, first_gain, first_shift, second_gain, second_shift, hidden_weight, hidden_bias, down_weight, down_bias):
    weight_set = tuple(map(widen, (step_table, triple_weight, query_bias, value_bias, output_weight, output_bias, first_gain, first_shift, second_gain, second_shift, hidden_weight, hidden_bias, down_weight, down_bias)))
    group_rows = math.gcd(ROWS, max(1, 4096 // L))
    block_count = MB * ROWS // group_rows
    int_pieces = (timesteps.reshape(block_count, group_rows), segments.reshape(block_count, group_rows, L), padding.reshape(block_count, group_rows, L))
    checked = jax.checkpoint(block_forward)

    def forward_all(weights_in, tokens_in):

        def one_block(state_carry, block_items):
            return (state_carry, checked(weights_in, block_items[0], block_items[1], block_items[2], block_items[3]))
        blocks_in = (tokens_in.reshape(block_count, group_rows, L, D),) + int_pieces
        unused_carry, outputs = lax.scan(one_block, None, blocks_in)
        return outputs.reshape(MB, ROWS, L, D)
    outputs, pull_back = jax.vjp(forward_all, weight_set, widen(tokens))
    weight_grads, token_grads = pull_back(widen(cotangent))
    return (outputs.astype(jnp.bfloat16), token_grads.astype(jnp.bfloat16), weight_grads[0], weight_grads[1], weight_grads[2], weight_grads[3], weight_grads[4], weight_grads[5], weight_grads[6], weight_grads[7], weight_grads[8], weight_grads[9], weight_grads[10], weight_grads[11], weight_grads[12], weight_grads[13])
```

```python
import functools
import math

import jax
import jax.numpy as jnp
from jax import lax
from jax.experimental import pallas as pl
from jax.experimental.pallas import tpu as pltpu
from jax.sharding import PartitionSpec as P

HEADS = 12
HD = 64
EPS = 1e-05
MASKED = -1e30
SCALE = 1.0 / math.sqrt(HD)
GELU_C = math.sqrt(2.0 / math.pi)
GELU_A = 0.044715
VMEM_LIMIT = 60 * 1024 * 1024
highest = lax.Precision.HIGHEST
f32 = jnp.float32
bf16 = jnp.bfloat16

NB = 8


def mm(a, b):
    return lax.dot_general(a, b, (((1,), (0,)), ((), ())), preferred_element_type=f32)


def mm_nt(a, b):
    return lax.dot_general(a, b, (((1,), (1,)), ((), ())), preferred_element_type=f32)


def mm_tn(a, b):
    return lax.dot_general(a, b, (((0,), (0,)), ((), ())), preferred_element_type=f32)


def moments(v):
    average = jnp.mean(v, axis=-1, keepdims=True)
    centered = v - average
    variance = jnp.mean(centered * centered, axis=-1, keepdims=True)
    inv = lax.rsqrt(variance + EPS)
    return centered * inv, inv


def ln_back(e, xhat, inv):
    return (e - jnp.mean(e, -1, keepdims=True) - xhat * jnp.mean(e * xhat, -1, keepdims=True)) * inv


def load_blocks(slots_ref, pieces, layout, w_ref, sem):
    copies = []
    for piece, first, count in layout:
        for t in range(count):
            i = len(copies)
            copies.append(
                pltpu.make_async_copy(pieces[piece].at[first + t], w_ref.at[slots_ref[i]], sem.at[i])
            )
    for cp in copies:
        cp.start()
    for cp in copies:
        cp.wait()


def square(w_ref, j):
    part = w_ref[NB * j : NB * (j + 1)]
    return part.reshape(part.shape[0] * part.shape[1], part.shape[2])


def put_pair(gpos_ref, at, keep_ref, send_ref, even, odd):
    idx = gpos_ref[at]
    side = gpos_ref[16]

    @pl.when(side == 0)
    def _():
        keep_ref[idx] = even
        send_ref[idx] = odd

    @pl.when(side != 0)
    def _():
        keep_ref[idx] = odd
        send_ref[idx] = even


def half_mask(rows, width):
    lane = lax.broadcasted_iota(jnp.int32, (rows, width), 1)
    return lane < HD


def both(x2, first):
    zero = jnp.zeros_like(x2)
    return jnp.concatenate([jnp.where(first, x2, zero), jnp.where(first, zero, x2)], axis=0)


def residual_of(tok_ref, emb_ref, step, rb, length):
    parts = []
    for r in range(rb):
        rows = tok_ref[r * length : (r + 1) * length].astype(f32)
        parts.append(rows + emb_ref[pl.ds(step * rb + r, 1), :])
    return jnp.concatenate(parts, axis=0) if rb > 1 else parts[0]


def f1_kernel(layout, rb, length, slots, tok_ref, emb_ref, seg_ref, pad_ref, vec_ref, *rest):
    n = max(l[0] for l in layout) + 1
    pieces = rest[:n]
    normed_ref, triple_ref, att_ref, attended_ref, middle_ref, n2_ref, w_ref, sem = rest[n:]
    step = pl.program_id(0)

    @pl.when(step == 0)
    def _():
        load_blocks(slots, pieces, layout, w_ref, sem)

    x = residual_of(tok_ref, emb_ref, step, rb, length)
    xhat, _inv = moments(x)
    normed = (xhat * vec_ref[3:4, :] + vec_ref[4:5, :]).astype(bf16)
    normed_ref[...] = normed
    width = normed.shape[1]
    for q, row in ((0, 0), (1, None), (2, 1)):
        t = mm(normed, square(w_ref, q))
        if row is not None:
            t = t + vec_ref[row : row + 1, :]
        triple_ref[q] = t.astype(bf16)
    eye = lax.broadcasted_iota(jnp.int32, (length, length), 0) == lax.broadcasted_iota(
        jnp.int32, (length, length), 1
    )
    first = half_mask(length, 2 * HD)
    for r in range(rb):
        seg = jnp.broadcast_to(seg_ref[pl.ds(step * rb + r, 1), :], (length, length))
        pad = jnp.broadcast_to(pad_ref[pl.ds(step * rb + r, 1), :], (length, length))
        same = seg == seg.T
        allowed = same & ((pad == 0.0) | eye)
        allowed = jnp.where(allowed, 1.0, 0.0)
        allowed = jnp.concatenate([allowed, allowed], axis=0) > 0.5
        rows = slice(r * length, (r + 1) * length)
        for hp in range(width // (2 * HD)):
            lanes = slice(hp * 2 * HD, (hp + 1) * 2 * HD)
            qs = both(triple_ref[0, rows, lanes], first)
            s = mm_nt(qs, triple_ref[1, rows, lanes]) * SCALE
            s = jnp.where(allowed, s, MASKED)
            top = jnp.max(s, axis=-1, keepdims=True)
            e = jnp.exp(s - top)
            p = (e / jnp.sum(e, axis=-1, keepdims=True)).astype(bf16)
            att_ref[r * (width // (2 * HD)) + hp] = p
            wide = jnp.concatenate([p[:length], p[length:]], axis=1)
            o = mm(wide, both(triple_ref[2, rows, lanes], first))
            attended_ref[rows, lanes] = o.astype(bf16)
    branch = mm(attended_ref[...], square(w_ref, 3)) + vec_ref[2:3, :]
    middle = x + branch
    middle_ref[...] = middle
    xhat2, _inv2 = moments(middle)
    n2_ref[...] = (xhat2 * vec_ref[5:6, :] + vec_ref[6:7, :]).astype(bf16)


def f2_kernel(layout, chunk, slots, gpos, n2_ref, cot_ref, hb_ref, *rest):
    n = max(l[0] for l in layout) + 1
    pieces = rest[:n]
    active_ref, gp_ref, keep_ref, send_ref, w_ref, h_ref, sem = rest[n:]
    j = pl.program_id(0)

    @pl.when(j == 0)
    def _():
        load_blocks(slots, pieces, layout, w_ref, sem)

    tokens, width = n2_ref.shape
    w = w_ref[pl.ds(j * NB, NB)].reshape(width, width)
    bias = hb_ref[pl.ds(j, 1), :]
    sub = 32
    for m in range(tokens // chunk):
        h_ref[...] = mm(n2_ref[m * chunk : (m + 1) * chunk], w)
        for s in range(chunk // sub):
            v = h_ref[s * sub : (s + 1) * sub] + bias
            v2 = v * v
            t = jnp.tanh((GELU_C * v) * (1.0 + GELU_A * v2))
            half = 0.5 * (1.0 + t)
            at = slice(m * chunk + s * sub, m * chunk + (s + 1) * sub)
            active_ref[at] = (v * half).astype(bf16)
            slope = half + (0.5 * GELU_C) * v * (1.0 - t * t) * (1.0 + (3.0 * GELU_A) * v2)
            gp_ref[at] = slope.astype(bf16)
    cot = cot_ref[...]
    hw = width // 2
    ev = mm_tn(active_ref[:, :hw], cot).astype(bf16)
    od = mm_tn(active_ref[:, hw:], cot).astype(bf16)
    b = width // NB
    for q in range(4):
        put_pair(gpos, q * 4 + j, keep_ref, send_ref, ev[q * b : (q + 1) * b], od[q * b : (q + 1) * b])


def b1_kernel(layout, chunk, slots, gpos, n2_ref, cot_ref, gp_ref, *rest):
    n = max(l[0] for l in layout) + 1
    pieces = rest[:n]
    dh_ref, hb_ref, db_ref, keep_ref, send_ref, w_ref, nt_ref, h_ref, sem = rest[n:]
    j = pl.program_id(0)
    tokens, width = n2_ref.shape

    @pl.when(j == 0)
    def _():
        load_blocks(slots, pieces, layout, w_ref, sem)
        nt_ref[...] = n2_ref[...].T
        db_ref[...] = jnp.zeros_like(db_ref)
        db_ref[0:1] = jnp.sum(cot_ref[...].astype(f32), axis=0, keepdims=True)
        hb_ref[...] = jnp.zeros_like(hb_ref)

    w = w_ref[pl.ds(j * NB, NB)].reshape(width, width)
    sub = 32
    total = jnp.zeros((8, width), f32)
    for m in range(tokens // chunk):
        h_ref[...] = mm_nt(cot_ref[m * chunk : (m + 1) * chunk], w)
        for s in range(chunk // sub):
            at = slice(m * chunk + s * sub, m * chunk + (s + 1) * sub)
            dh = (h_ref[s * sub : (s + 1) * sub] * gp_ref[at].astype(f32)).astype(bf16)
            dh_ref[at] = dh
            total = total + jnp.sum(dh.astype(f32).reshape(sub // 8, 8, width), axis=0)
    hb_ref[pl.ds(j, 1), :] = jnp.sum(total, axis=0, keepdims=True)
    b = width // NB
    dh_all = dh_ref[...]
    for zf in range(4):
        g = mm(nt_ref[zf * 2 * b : (zf + 1) * 2 * b], dh_all).astype(bf16)
        put_pair(gpos, j * 4 + zf, keep_ref, send_ref, g[:b], g[b:])


def b2_kernel(
    layout_a, layout_b, rb, length, slots_a, slots_b, gpos,
    dh_ref, cot_ref, middle_ref, triple_ref, att_ref, attended_ref, normed_ref, vec_ref, *rest
):
    na = max(l[0] for l in layout_a) + 1
    nb = max(l[0] for l in layout_b) + 1
    pieces_a, pieces_b, rest = rest[:na], rest[na : na + nb], rest[na + nb :]
    dmid_ref, dt_ref, sums_ref, keep_ref, send_ref, wa_ref, wb_ref, dbr_ref, dts_ref, sem_a, sem_b = rest
    step = pl.program_id(0)
    block = rb * length
    width = cot_ref.shape[1]

    @pl.when(step == 0)
    def _():
        load_blocks(slots_b, pieces_b, layout_b, wb_ref, sem_b)
        load_blocks(slots_a, pieces_a, layout_a, wa_ref, sem_a)
        sums_ref[...] = jnp.zeros_like(sums_ref)

    d_n2 = mm_nt(dh_ref[0], square(wb_ref, 0))
    for j in range(1, 4):
        d_n2 = d_n2 + mm_nt(dh_ref[j], square(wb_ref, j))
    xhat, inv = moments(middle_ref[...])
    sums_ref[0:1] += jnp.sum(d_n2 * xhat, axis=0, keepdims=True)
    sums_ref[1:2] += jnp.sum(d_n2, axis=0, keepdims=True)
    d_middle = cot_ref[...].astype(f32) + ln_back(d_n2 * vec_ref[5:6, :], xhat, inv)
    dmid_ref[...] = d_middle
    d_branch = d_middle.astype(bf16)
    base = pl.multiple_of(step * block, block)
    dbr_ref[pl.ds(base, block)] = d_branch
    sums_ref[2:3] += jnp.sum(d_branch.astype(f32), axis=0, keepdims=True)
    d_att = mm_nt(d_branch, square(wa_ref, 3)).astype(bf16)
    first = half_mask(length, 2 * HD)
    pairs = width // (2 * HD)
    for r in range(rb):
        rows = slice(r * length, (r + 1) * length)
        for hp in range(pairs):
            lanes = slice(hp * 2 * HD, (hp + 1) * 2 * HD)
            dos = both(d_att[rows, lanes], first)
            p_low = att_ref[r * pairs + hp]
            p = p_low.astype(f32)
            d_a = mm_nt(dos, triple_ref[2, rows, lanes])
            inner = jnp.sum(p * d_a, axis=-1, keepdims=True)
            ds = (p * (d_a - inner)).astype(bf16)
            wide = jnp.concatenate([ds[:length], ds[length:]], axis=1)
            dt_ref[0, rows, lanes] = (mm(wide, both(triple_ref[1, rows, lanes], first)) * SCALE).astype(bf16)
            dt_ref[1, rows, lanes] = (mm_tn(ds, both(triple_ref[0, rows, lanes], first)) * SCALE).astype(bf16)
            dt_ref[2, rows, lanes] = mm_tn(p_low, dos).astype(bf16)
    sums_ref[3:4] += jnp.sum(dt_ref[0].astype(f32), axis=0, keepdims=True)
    sums_ref[4:5] += jnp.sum(dt_ref[2].astype(f32), axis=0, keepdims=True)
    for q in range(3):
        dts_ref[q, pl.ds(base, block)] = dt_ref[q]

    @pl.when(step == pl.num_programs(0) - 1)
    def _():
        b = width // NB
        hw = width // 2
        for h in range(2):
            cols = slice(h * hw, (h + 1) * hw)
            for q in range(4):
                if q < 3:
                    g = mm_tn(normed_ref[:, cols], dts_ref[q])
                else:
                    g = mm_tn(attended_ref[:, cols], dbr_ref[...])
                g = g.astype(bf16)
                for zz in range(2):
                    put_pair(
                        gpos, q * 4 + 2 * h + zz, keep_ref, send_ref,
                        g[2 * zz * b : (2 * zz + 1) * b], g[(2 * zz + 1) * b : (2 * zz + 2) * b],
                    )


def b4_kernel(layout, rb, length, slots, tok_ref, emb_ref, dmid_ref, dt_ref, vec_ref, *rest):
    n = max(l[0] for l in layout) + 1
    pieces = rest[:n]
    ig_ref, rs_ref, sums_ref, w_ref, sem = rest[n:]
    step = pl.program_id(0)

    @pl.when(step == 0)
    def _():
        load_blocks(slots, pieces, layout, w_ref, sem)
        sums_ref[...] = jnp.zeros_like(sums_ref)
        rs_ref[...] = jnp.zeros_like(rs_ref)

    d_n = mm_nt(dt_ref[0], square(w_ref, 0))
    for q in range(1, 3):
        d_n = d_n + mm_nt(dt_ref[q], square(w_ref, q))
    xhat, inv = moments(residual_of(tok_ref, emb_ref, step, rb, length))
    sums_ref[0:1] += jnp.sum(d_n * xhat, axis=0, keepdims=True)
    sums_ref[1:2] += jnp.sum(d_n, axis=0, keepdims=True)
    d_start = dmid_ref[...] + ln_back(d_n * vec_ref[3:4, :], xhat, inv)
    ig_ref[...] = d_start.astype(bf16)
    for r in range(rb):
        rs_ref[pl.ds(step * rb + r, 1), :] = jnp.sum(d_start[r * length : (r + 1) * length], axis=0, keepdims=True)


def f3_kernel(layout, slots, act_ref, middle_ref, vec_ref, *rest):
    n = max(l[0] for l in layout) + 1
    pieces = rest[:n]
    out_ref, w_ref, sem = rest[n:]

    @pl.when(pl.program_id(0) == 0)
    def _():
        load_blocks(slots, pieces, layout, w_ref, sem)

    acc = mm(act_ref[0], square(w_ref, 0))
    for j in range(1, 4):
        acc = acc + mm(act_ref[j], square(w_ref, j))
    out_ref[...] = (middle_ref[...] + (acc + vec_ref[7:8, :])).astype(bf16)


def sds(shape, dtype):
    return jax.ShapeDtypeStruct(shape, dtype)


def full(shape):
    zeros = (0,) * len(shape)
    return pl.BlockSpec(shape, lambda i: zeros)


smem = pl.BlockSpec(memory_space=pltpu.SMEM)
hbm = pl.BlockSpec(memory_space=pl.ANY)


def call(kernel, grid, in_specs, out_shape, out_specs, scratch, flops, nbytes, args):
    return pl.pallas_call(
        kernel,
        grid=grid,
        in_specs=in_specs,
        out_shape=out_shape,
        out_specs=out_specs,
        scratch_shapes=scratch,
        compiler_params=pltpu.CompilerParams(
            dimension_semantics=("arbitrary",), vmem_limit_bytes=VMEM_LIMIT
        ),
        cost_estimate=pl.CostEstimate(flops=flops, bytes_accessed=nbytes, transcendentals=0),
    )(*args)


class Group:
    def __init__(self, arrays, layout, slots):
        self.arrays, self.layout, self.slots = arrays, layout, slots


def compute_f1(tok, emb, seg, pad, vecs, group, rows, length):
    n, width = tok.shape
    rb = 2 if rows % 2 == 0 else 1
    block = rb * length
    pairs = width // (2 * HD)
    b = width // NB
    return call(
        functools.partial(f1_kernel, group.layout, rb, length),
        (rows // rb,),
        [smem, pl.BlockSpec((block, width), lambda i: (i, 0)), full(emb.shape), full(seg.shape), full(pad.shape), full(vecs.shape)]
        + [hbm] * len(group.arrays),
        [sds((n, width), bf16), sds((3, n, width), bf16), sds((rows * pairs, 2 * length, length), bf16),
         sds((n, width), bf16), sds((n, width), f32), sds((n, width), bf16)],
        [pl.BlockSpec((block, width), lambda i: (i, 0)), pl.BlockSpec((3, block, width), lambda i: (0, i, 0)),
         pl.BlockSpec((rb * pairs, 2 * length, length), lambda i: (i, 0, 0)),
         pl.BlockSpec((block, width), lambda i: (i, 0)), pl.BlockSpec((block, width), lambda i: (i, 0)),
         pl.BlockSpec((block, width), lambda i: (i, 0))],
        [pltpu.VMEM((32, b, width), bf16), pltpu.SemaphoreType.DMA((32,))],
        2 * n * width * width * 4 * 3, 20 << 20,
        [group.slots, tok, emb, seg, pad, vecs, *group.arrays],
    )


def compute_f2(n2, cot, hb, group, gpos):
    n, width = n2.shape
    b = width // NB
    chunk = 256 if n % 256 == 0 else n
    return call(
        functools.partial(f2_kernel, group.layout, chunk),
        (4,),
        [smem, smem, full(n2.shape), full(cot.shape), full(hb.shape)] + [hbm] * len(group.arrays),
        [sds((4, n, width), bf16), sds((4, n, width), bf16), sds((16, b, width), bf16), sds((16, b, width), bf16)],
        [pl.BlockSpec((None, n, width), lambda i: (i, 0, 0)), pl.BlockSpec((None, n, width), lambda i: (i, 0, 0)),
         full((16, b, width)), full((16, b, width))],
        [pltpu.VMEM((32, b, width), bf16), pltpu.VMEM((chunk, width), f32), pltpu.SemaphoreType.DMA((32,))],
        2 * n * width * width * 8 * 2, 20 << 20,
        [group.slots, gpos, n2, cot, hb, *group.arrays],
    )


def compute_b1(n2, cot, gp, group, gpos):
    n, width = n2.shape
    b = width // NB
    chunk = 256 if n % 256 == 0 else n
    return call(
        functools.partial(b1_kernel, group.layout, chunk),
        (4,),
        [smem, smem, full(n2.shape), full(cot.shape), pl.BlockSpec((None, n, width), lambda i: (i, 0, 0))]
        + [hbm] * len(group.arrays),
        [sds((4, n, width), bf16), sds((8, width), f32), sds((8, width), f32), sds((16, b, width), bf16), sds((16, b, width), bf16)],
        [pl.BlockSpec((None, n, width), lambda i: (i, 0, 0)), full((8, width)), full((8, width)),
         full((16, b, width)), full((16, b, width))],
        [pltpu.VMEM((32, b, width), bf16), pltpu.VMEM((width, n), bf16), pltpu.VMEM((chunk, width), f32),
         pltpu.SemaphoreType.DMA((32,))],
        2 * n * width * width * 8 * 2, 20 << 20,
        [group.slots, gpos, n2, cot, gp, *group.arrays],
    )


def compute_b2(dh, cot, middle, triple, att, attended, normed, vecs, ga, gb, gpos, rows, length):
    n, width = cot.shape
    rb = 2 if rows % 2 == 0 else 1
    block = rb * length
    pairs = width // (2 * HD)
    b = width // NB
    return call(
        functools.partial(b2_kernel, ga.layout, gb.layout, rb, length),
        (rows // rb,),
        [smem, smem, smem, pl.BlockSpec((4, block, width), lambda i: (0, i, 0)), pl.BlockSpec((block, width), lambda i: (i, 0)),
         pl.BlockSpec((block, width), lambda i: (i, 0)), pl.BlockSpec((3, block, width), lambda i: (0, i, 0)),
         pl.BlockSpec((rb * pairs, 2 * length, length), lambda i: (i, 0, 0)), full(attended.shape), full(normed.shape),
         full(vecs.shape)] + [hbm] * (len(ga.arrays) + len(gb.arrays)),
        [sds((n, width), f32), sds((3, n, width), bf16), sds((8, width), f32), sds((16, b, width), bf16), sds((16, b, width), bf16)],
        [pl.BlockSpec((block, width), lambda i: (i, 0)), pl.BlockSpec((3, block, width), lambda i: (0, i, 0)), full((8, width)),
         full((16, b, width)), full((16, b, width))],
        [pltpu.VMEM((32, b, width), bf16), pltpu.VMEM((32, b, width), bf16), pltpu.VMEM((n, width), bf16),
         pltpu.VMEM((3, n, width), bf16), pltpu.SemaphoreType.DMA((32,)), pltpu.SemaphoreType.DMA((32,))],
        2 * n * width * width * 16, 40 << 20,
        [ga.slots, gb.slots, gpos, dh, cot, middle, triple, att, attended, normed, vecs, *ga.arrays, *gb.arrays],
    )


def compute_b4(tok, emb, dmid, dt, vecs, group, rows, length):
    n, width = tok.shape
    rb = 2 if rows % 2 == 0 else 1
    block = rb * length
    b = width // NB
    return call(
        functools.partial(b4_kernel, group.layout, rb, length),
        (rows // rb,),
        [smem, pl.BlockSpec((block, width), lambda i: (i, 0)), full(emb.shape), pl.BlockSpec((block, width), lambda i: (i, 0)),
         pl.BlockSpec((3, block, width), lambda i: (0, i, 0)), full(vecs.shape)] + [hbm] * len(group.arrays),
        [sds((n, width), bf16), sds((8 * ((rows + 7) // 8), width), f32), sds((8, width), f32)],
        [pl.BlockSpec((block, width), lambda i: (i, 0)), full((8 * ((rows + 7) // 8), width)), full((8, width))],
        [pltpu.VMEM((32, b, width), bf16), pltpu.SemaphoreType.DMA((32,))],
        2 * n * width * width * 3 * 2, 12 << 20,
        [group.slots, tok, emb, dmid, dt, vecs, *group.arrays],
    )


def compute_f3(active, middle, vecs, group):
    n, width = middle.shape
    b = width // NB
    block = 256 if n % 256 == 0 else n
    return call(
        functools.partial(f3_kernel, group.layout),
        (n // block,),
        [smem, pl.BlockSpec((4, block, width), lambda i: (0, i, 0)), pl.BlockSpec((block, width), lambda i: (i, 0)), full(vecs.shape)]
        + [hbm] * len(group.arrays),
        sds((n, width), bf16),
        pl.BlockSpec((block, width), lambda i: (i, 0)),
        [pltpu.VMEM((32, b, width), bf16), pltpu.SemaphoreType.DMA((32,))],
        2 * n * width * width * 4 * 2, 12 << 20,
        [group.slots, active, middle, vecs, *group.arrays],
    )


def plain_groups(own_a, own_b, own_c, small):
    width = own_a.shape[2]
    slots = jnp.arange(32, dtype=jnp.int32)

    def group(whole):
        return Group([whole.reshape(32, width // NB, width)], [(0, 0, 32)], slots)

    a = lax.all_gather(own_a, "fsdp", axis=1, tiled=True)
    b = lax.all_gather(own_b, "fsdp", axis=1, tiled=True)
    c = lax.all_gather(own_c, "fsdp", axis=0, tiled=True)
    vec = [lax.all_gather(v, "fsdp", axis=0, tiled=True) for v in small]
    return group(a), group(b), group(c), jnp.stack(vec[:8]).astype(f32), vec[8].astype(f32).reshape(4, width)


def plain_scatter(keep, send, rows_first):
    b, width = keep.shape[1:]
    g = jnp.stack([keep.reshape(4, 4, b, width), send.reshape(4, 4, b, width)], axis=2)
    if rows_first:
        g = g.transpose(1, 2, 0, 3, 4).reshape(32 * b, width)
        s = lax.psum_scatter(g.astype(f32), "fsdp", scatter_dimension=0, tiled=True)
        return lax.psum(s, "dp")
    g = g.reshape(4, NB * b, width)
    s = lax.psum_scatter(g.astype(f32), "fsdp", scatter_dimension=1, tiled=True)
    return lax.psum(s, "dp")


def pick(stacked, i):
    return lax.dynamic_index_in_dim(stacked, i, axis=0, keepdims=False)


def xor_perm(n, k):
    return [(i, i ^ k) for i in range(n)]


def core_swap(v):
    return lax.ppermute(v, "fsdp", xor_perm(8, 1))


def x_swap(v):
    return lax.ppermute(v, "dp", xor_perm(4, 1))


def y_swap(v):
    return lax.ppermute(v, "dp", xor_perm(4, 2))


def z_shift(v, k):
    return lax.ppermute(v, "fsdp", [(i, (i + 2 * k) % 8) for i in range(8)])


def fast_slots(d, z, c, rows_first):
    table = []

    def add(delta, k, e):
        q = d ^ delta
        f = 2 * lax.rem(z - k + 4, 4) + (c ^ e)
        table.append(f * 4 + q if rows_first else q * NB + f)

    for e in (0, 1):
        for delta in (0, 1, 2):
            for k in range(4):
                add(delta, k, e)
        for k in range(4):
            add(3, k, e)
    return jnp.stack(table).astype(jnp.int32)


def fast_gather(own, d, z, c, rows_first, extra=None):
    b = own.shape[0]
    sent = own if extra is None else jnp.concatenate([own, extra], axis=0)
    got = [sent] + [z_shift(sent, k) for k in (1, 2, 3)]
    s0 = jnp.stack([g[:b] for g in got])
    xs, ys = x_swap(s0), y_swap(s0)
    d1, d2 = y_swap(xs[:2]), x_swap(ys[2:])
    mine = [s0, xs, ys, d1, d2]
    arrays = mine + [core_swap(v) for v in mine]
    layout = []
    for e in range(2):
        layout += [(5 * e, 0, 4), (5 * e + 1, 0, 4), (5 * e + 2, 0, 4), (5 * e + 3, 0, 2), (5 * e + 4, 0, 2)]
    group = Group(arrays, layout, fast_slots(d, z, c, rows_first))
    if extra is None:
        return group
    e0 = jnp.stack([g[b:] for g in got])
    return group, e0, core_swap(e0)


def fast_small(e0, e1, z, c, width):
    pair = jnp.stack([jnp.where(c == 0, e0, e1), jnp.where(c == 0, e1, e0)], axis=1)[:, :, :2]
    rows = jnp.stack([pick(pair, lax.rem(z - i + 4, 4)) for i in range(4)])
    rows = rows.reshape(8, 2, width).astype(f32)
    vecs = rows[:, 0].reshape(8, 8, width // 8).transpose(1, 0, 2).reshape(8, width)
    hb = rows[:, 1, : width // 2].reshape(4, width)
    return vecs, hb


def fast_scatter(keep, send):
    b, width = keep.shape[1:]
    got = core_swap(send)

    def add(u, v):
        return (u.astype(f32) + v.astype(f32)).astype(bf16)

    keep = keep.reshape(4, 4, b, width)
    got = got.reshape(4, 4, b, width)

    def part(deltas, half):
        ks = slice(2 * half, 2 * half + 2)
        return jnp.stack([add(keep[dl, ks], got[dl, ks]) for dl in deltas])

    rx = x_swap(part((1, 3), 0))
    ry = y_swap(part((2, 3), 1))
    h2a = add(part((0, 2), 0), rx)
    h2b = add(part((0, 1), 1), ry)
    ra = y_swap(h2a[1])
    rb = x_swap(h2b[1])
    h3 = jnp.concatenate([add(h2a[0], ra), add(h2b[0], rb)], axis=0)
    parts = [h3[0]] + [z_shift(h3[k], k) for k in (1, 2, 3)]
    total = sum(p.astype(f32) for p in parts)
    return total.astype(bf16)


def fast_spread(mine, d):
    got = jnp.stack([mine, x_swap(mine), y_swap(mine), lax.ppermute(mine, "dp", xor_perm(4, 3))])
    return jnp.stack([pick(got, d ^ q) for q in range(4)]).astype(f32)


def per_device(
    fast, tokens, timesteps, segments, padding, cotangent, step_table,
    triple_weight, query_bias, value_bias, output_weight, output_bias,
    first_gain, first_shift, second_gain, second_shift,
    hidden_weight, hidden_bias, down_weight, down_bias,
):
    micro, local_rows, length, width = tokens.shape
    rows = micro * local_rows
    n = rows * length
    nd, nf = lax.axis_size("dp"), lax.axis_size("fsdp")
    d, f = lax.axis_index("dp"), lax.axis_index("fsdp")
    z, c = f // 2, lax.rem(f, 2)
    tok = tokens.reshape(n, width)
    cot = cotangent.reshape(n, width)
    seg = segments.reshape(rows, length).astype(f32)
    pad = padding.reshape(rows, length).astype(f32)

    ids = lax.all_gather(timesteps.reshape(1, rows), ("dp", "fsdp"), axis=0, tiled=True)
    here = lax.dynamic_slice_in_dim(ids, d * nf, nf, axis=0).reshape(nf * rows)
    steps = lax.iota(jnp.int32, step_table.shape[0])
    onehot = (here[:, None] == steps[None, :]).astype(bf16)
    looked = jnp.dot(onehot, step_table, preferred_element_type=f32).astype(bf16)
    looked = looked.reshape(nf, rows, width // nf)
    emb = lax.all_to_all(looked, "fsdp", 0, 0, tiled=True)
    emb = emb.transpose(1, 0, 2).reshape(rows, width).astype(f32)

    q4 = [triple_weight[:, i * width : (i + 1) * width] for i in range(3)] + [output_weight]
    h4 = [hidden_weight[:, i * width : (i + 1) * width] for i in range(4)]
    vec_args = (query_bias, value_bias, output_bias, first_gain, first_shift, second_gain, second_shift, down_bias)
    if fast:
        b = width // NB
        own_a = pick(jnp.stack(q4), d)
        own_b = pick(jnp.stack(h4), d)
        own_c = lax.dynamic_slice_in_dim(down_weight, d * b, b, axis=0)
        hb_row = jnp.concatenate([hidden_bias, jnp.zeros_like(hidden_bias)])
        small = jnp.stack([jnp.concatenate(vec_args), hb_row])
        small = jnp.concatenate([small, jnp.zeros((14, width), bf16)], axis=0)
        ga, e0, e1 = fast_gather(own_a, d, z, c, False, small)
        gb = fast_gather(own_b, d, z, c, False)
        gc = fast_gather(own_c, d, z, c, True)
        vecs, hb = fast_small(e0, e1, z, c, width)
        gpos = [(q ^ d) * 4 + lax.rem(zf - z + 4, 4) for q in range(4) for zf in range(4)] + [c]
        gpos = jnp.stack(gpos).astype(jnp.int32)
    else:
        ga, gb, gc, vecs, hb = plain_groups(
            jnp.stack(q4), jnp.stack(h4), down_weight, vec_args + (hidden_bias,)
        )
        gpos = jnp.concatenate([jnp.arange(16, dtype=jnp.int32), jnp.zeros((1,), jnp.int32)])

    normed, triple, att, attended, middle, n2 = compute_f1(tok, emb, seg, pad, vecs, ga, rows, length)
    active, gp, keep_c, send_c = compute_f2(n2, cot, hb, gb, gpos)
    dh, hb_sum, db_sum, keep_b, send_b = compute_b1(n2, cot, gp, gc, gpos)
    dmid, dt, sums2, keep_a, send_a = compute_b2(
        dh, cot, middle, triple, att, attended, normed, vecs, ga, gb, gpos, rows, length
    )
    result = compute_f3(active, middle, vecs, gc)
    input_grad, row_sums, sums4 = compute_b4(tok, emb, dmid, dt, vecs, ga, rows, length)
    row_sums = row_sums[:rows]

    if fast:
        out_c = fast_spread(fast_scatter(keep_c, send_c), d)
        out_b = fast_spread(fast_scatter(keep_b, send_b), d)
        out_a = fast_spread(fast_scatter(keep_a, send_a), d)
        down_grad = out_c.reshape(4 * b, width)
    else:
        out_b = plain_scatter(keep_b, send_b, False)
        out_a = plain_scatter(keep_a, send_a, False)
        down_grad = plain_scatter(keep_c, send_c, True)
    hidden_grad = jnp.concatenate([out_b[i] for i in range(4)], axis=1)
    triple_grad = jnp.concatenate([out_a[i] for i in range(3)], axis=1)
    output_grad = out_a[3]

    part = width // nf
    sums = jnp.concatenate(
        [row_sums, sums2[3:5], sums2[2:3], sums4[0:2], sums2[0:2], db_sum[0:1]], axis=0
    )
    lanes = sums.reshape(rows + 8, nf, part).transpose(1, 0, 2).reshape(nf, (rows + 8) * part)
    payload = jnp.concatenate([lanes, hb_sum[:4].reshape(nf, 4 * part)], axis=1)
    moved = lax.all_to_all(payload, "fsdp", 0, 0, tiled=True)
    moved = lax.all_gather(moved, "dp", axis=0, tiled=True)
    table_rows = moved[:, : rows * part].reshape(nd * nf * rows, part)
    all_hot = (steps[:, None] == ids.reshape(1, nd * nf * rows)).astype(f32)
    table_grad = jnp.dot(all_hot, table_rows, precision=highest)
    vec_sums = jnp.sum(moved[:, rows * part :], axis=0)
    v = [vec_sums[i * part : (i + 1) * part] for i in range(8)]
    hidden_bias_grad = vec_sums[8 * part :]
    shape = tokens.shape
    return (
        result.reshape(shape), input_grad.reshape(shape), table_grad, triple_grad, v[0], v[1], output_grad, v[2],
        v[3], v[4], v[5], v[6], hidden_grad, hidden_bias_grad, down_grad, v[7],
    )


def solution(mesh):
    fast = mesh.shape["dp"] == 4 and mesh.shape["fsdp"] == 8
    batch = ("dp", "fsdp")
    vec, mat, tab = P("fsdp"), P("fsdp", None), P(None, "fsdp")
    tokens_spec = P(None, batch, None, None)
    return jax.shard_map(
        functools.partial(per_device, fast),
        mesh=mesh,
        in_specs=(
            tokens_spec, P(None, batch), P(None, batch, None), P(None, batch, None), tokens_spec,
            tab, mat, vec, vec, mat, vec, vec, vec, vec, vec, mat, vec, mat, vec,
        ),
        out_specs=(
            tokens_spec, tokens_spec, tab, mat, vec, vec, mat, vec, vec, vec, vec, vec, mat, vec, mat, vec,
        ),
        check_vma=False,
    )
```

```python
import functools
import math

import jax
import jax.numpy as jnp
from jax import lax
from jax.experimental import pallas as pl
from jax.experimental.pallas import tpu as pltpu
from jax.sharding import PartitionSpec as P

HEADS = 12
HD = 64
EPS = 1e-05
MASKED = -1e30
SCALE = 1.0 / math.sqrt(HD)
GELU_C = math.sqrt(2.0 / math.pi)
GELU_A = 0.044715
VMEM_LIMIT = 60 * 1024 * 1024
highest = lax.Precision.HIGHEST
f32 = jnp.float32
bf16 = jnp.bfloat16

NB = 8


def mm(a, b):
    return lax.dot_general(a, b, (((1,), (0,)), ((), ())), preferred_element_type=f32)


def mm_nt(a, b):
    return lax.dot_general(a, b, (((1,), (1,)), ((), ())), preferred_element_type=f32)


def mm_tn(a, b):
    return lax.dot_general(a, b, (((0,), (0,)), ((), ())), preferred_element_type=f32)


def moments(v):
    average = jnp.mean(v, axis=-1, keepdims=True)
    centered = v - average
    variance = jnp.mean(centered * centered, axis=-1, keepdims=True)
    inv = lax.rsqrt(variance + EPS)
    return centered * inv, inv


def ln_back(e, xhat, inv):
    return (e - jnp.mean(e, -1, keepdims=True) - xhat * jnp.mean(e * xhat, -1, keepdims=True)) * inv


def start_blocks(slots_ref, pieces, layout, w_ref, sem):
    i = 0
    for piece, first, count in layout:
        for t in range(count):
            slot = slots_ref[i]
            pltpu.make_async_copy(pieces[piece].at[first + t], w_ref.at[slot], sem.at[slot]).start()
            i += 1


def wait_blocks(w_ref, sem, first, count):
    def one(t, carry):
        pltpu.make_async_copy(w_ref.at[first + t], w_ref.at[first + t], sem.at[first + t]).wait()
        return carry

    lax.fori_loop(0, count, one, 0)


def load_blocks(slots_ref, pieces, layout, w_ref, sem):
    start_blocks(slots_ref, pieces, layout, w_ref, sem)
    wait_blocks(w_ref, sem, 0, 32)


def square(w_ref, j):
    part = w_ref[NB * j : NB * (j + 1)]
    return part.reshape(part.shape[0] * part.shape[1], part.shape[2])


def put_pair(gpos_ref, at, keep_ref, send_ref, even, odd):
    idx = gpos_ref[at]
    side = gpos_ref[16]

    @pl.when(side == 0)
    def _():
        keep_ref[idx] = even
        send_ref[idx] = odd

    @pl.when(side != 0)
    def _():
        keep_ref[idx] = odd
        send_ref[idx] = even


def half_mask(rows, width):
    lane = lax.broadcasted_iota(jnp.int32, (rows, width), 1)
    return lane < HD


def both(x2, first):
    zero = jnp.zeros_like(x2)
    return jnp.concatenate([jnp.where(first, x2, zero), jnp.where(first, zero, x2)], axis=0)


def residual_of(tok_ref, emb_ref, step, rb, length):
    parts = []
    for r in range(rb):
        rows = tok_ref[r * length : (r + 1) * length].astype(f32)
        parts.append(rows + emb_ref[pl.ds(step * rb + r, 1), :])
    return jnp.concatenate(parts, axis=0) if rb > 1 else parts[0]


def f1_kernel(layout, rb, length, slots, tok_ref, emb_ref, seg_ref, pad_ref, vec_ref, *rest):
    n = max(l[0] for l in layout) + 1
    pieces = rest[:n]
    normed_ref, triple_ref, att_ref, attended_ref, middle_ref, n2_ref, w_ref, sem = rest[n:]
    step = pl.program_id(0)

    @pl.when(step == 0)
    def _():
        load_blocks(slots, pieces, layout, w_ref, sem)

    x = residual_of(tok_ref, emb_ref, step, rb, length)
    xhat, _inv = moments(x)
    normed = (xhat * vec_ref[3:4, :] + vec_ref[4:5, :]).astype(bf16)
    normed_ref[...] = normed
    width = normed.shape[1]
    for q, row in ((0, 0), (1, None), (2, 1)):
        t = mm(normed, square(w_ref, q))
        if row is not None:
            t = t + vec_ref[row : row + 1, :]
        triple_ref[q] = t.astype(bf16)
    eye = lax.broadcasted_iota(jnp.int32, (length, length), 0) == lax.broadcasted_iota(
        jnp.int32, (length, length), 1
    )
    first = half_mask(length, 2 * HD)
    for r in range(rb):
        seg = jnp.broadcast_to(seg_ref[pl.ds(step * rb + r, 1), :], (length, length))
        pad = jnp.broadcast_to(pad_ref[pl.ds(step * rb + r, 1), :], (length, length))
        same = seg == seg.T
        allowed = same & ((pad == 0.0) | eye)
        allowed = jnp.where(allowed, 1.0, 0.0)
        allowed = jnp.concatenate([allowed, allowed], axis=0) > 0.5
        rows = slice(r * length, (r + 1) * length)
        for hp in range(width // (2 * HD)):
            lanes = slice(hp * 2 * HD, (hp + 1) * 2 * HD)
            qs = both(triple_ref[0, rows, lanes], first)
            s = mm_nt(qs, triple_ref[1, rows, lanes]) * SCALE
            s = jnp.where(allowed, s, MASKED)
            top = jnp.max(s, axis=-1, keepdims=True)
            e = jnp.exp(s - top)
            p = (e / jnp.sum(e, axis=-1, keepdims=True)).astype(bf16)
            att_ref[r * (width // (2 * HD)) + hp] = p
            wide = jnp.concatenate([p[:length], p[length:]], axis=1)
            o = mm(wide, both(triple_ref[2, rows, lanes], first))
            attended_ref[rows, lanes] = o.astype(bf16)
    branch = mm(attended_ref[...], square(w_ref, 3)) + vec_ref[2:3, :]
    middle = x + branch
    middle_ref[...] = middle
    xhat2, _inv2 = moments(middle)
    n2_ref[...] = (xhat2 * vec_ref[5:6, :] + vec_ref[6:7, :]).astype(bf16)


def f2_kernel(layout, chunk, slots, gpos, n2_ref, cot_ref, hb_ref, *rest):
    n = max(l[0] for l in layout) + 1
    pieces = rest[:n]
    active_ref, gp_ref, keep_ref, send_ref, w_ref, h_ref, sem = rest[n:]
    j = pl.program_id(0)

    @pl.when(j == 0)
    def _():
        start_blocks(slots, pieces, layout, w_ref, sem)

    wait_blocks(w_ref, sem, j * NB, NB)
    tokens, width = n2_ref.shape
    w = w_ref[pl.ds(j * NB, NB)].reshape(width, width)
    bias = hb_ref[pl.ds(j, 1), :]
    sub = 32
    for m in range(tokens // chunk):
        h_ref[...] = mm(n2_ref[m * chunk : (m + 1) * chunk], w)
        for s in range(chunk // sub):
            v = h_ref[s * sub : (s + 1) * sub] + bias
            v2 = v * v
            t = jnp.tanh((GELU_C * v) * (1.0 + GELU_A * v2))
            half = 0.5 * (1.0 + t)
            at = slice(m * chunk + s * sub, m * chunk + (s + 1) * sub)
            active_ref[at] = (v * half).astype(bf16)
            slope = half + (0.5 * GELU_C) * v * (1.0 - t * t) * (1.0 + (3.0 * GELU_A) * v2)
            gp_ref[at] = slope.astype(bf16)
    cot = cot_ref[...]
    hw = width // 2
    ev = mm_tn(active_ref[:, :hw], cot).astype(bf16)
    od = mm_tn(active_ref[:, hw:], cot).astype(bf16)
    b = width // NB
    for q in range(4):
        put_pair(gpos, q * 4 + j, keep_ref, send_ref, ev[q * b : (q + 1) * b], od[q * b : (q + 1) * b])


def b1_kernel(layout, chunk, slots, gpos, n2_ref, cot_ref, gp_ref, *rest):
    n = max(l[0] for l in layout) + 1
    pieces = rest[:n]
    dh_ref, hb_ref, db_ref, keep_ref, send_ref, w_ref, nt_ref, h_ref, sem = rest[n:]
    j = pl.program_id(0)
    tokens, width = n2_ref.shape

    @pl.when(j == 0)
    def _():
        start_blocks(slots, pieces, layout, w_ref, sem)
        nt_ref[...] = n2_ref[...].T
        db_ref[...] = jnp.zeros_like(db_ref)
        db_ref[0:1] = jnp.sum(cot_ref[...].astype(f32), axis=0, keepdims=True)
        hb_ref[...] = jnp.zeros_like(hb_ref)

    wait_blocks(w_ref, sem, j * NB, NB)
    w = w_ref[pl.ds(j * NB, NB)].reshape(width, width)
    sub = 32
    total = jnp.zeros((8, width), f32)
    for m in range(tokens // chunk):
        h_ref[...] = mm_nt(cot_ref[m * chunk : (m + 1) * chunk], w)
        for s in range(chunk // sub):
            at = slice(m * chunk + s * sub, m * chunk + (s + 1) * sub)
            dh = (h_ref[s * sub : (s + 1) * sub] * gp_ref[at].astype(f32)).astype(bf16)
            dh_ref[at] = dh
            total = total + jnp.sum(dh.astype(f32).reshape(sub // 8, 8, width), axis=0)
    hb_ref[pl.ds(j, 1), :] = jnp.sum(total, axis=0, keepdims=True)
    b = width // NB
    dh_all = dh_ref[...]
    for zf in range(4):
        g = mm(nt_ref[zf * 2 * b : (zf + 1) * 2 * b], dh_all).astype(bf16)
        put_pair(gpos, j * 4 + zf, keep_ref, send_ref, g[:b], g[b:])


def b2_kernel(layout_a, layout_b, slots_a, slots_b, dh_ref, cot_ref, middle_ref, vec_ref, *rest):
    na = max(l[0] for l in layout_a) + 1
    nb = max(l[0] for l in layout_b) + 1
    pieces_a, pieces_b, rest = rest[:na], rest[na : na + nb], rest[na + nb :]
    dmid_ref, dbr_ref, datt_ref, sums_ref, wa_ref, wb_ref, sem_a, sem_b = rest

    @pl.when(pl.program_id(0) == 0)
    def _():
        start_blocks(slots_b, pieces_b, layout_b, wb_ref, sem_b)
        start_blocks(slots_a, pieces_a, layout_a, wa_ref, sem_a)
        sums_ref[...] = jnp.zeros_like(sums_ref)
        wait_blocks(wb_ref, sem_b, 0, 32)

    d_n2 = mm_nt(dh_ref[0], square(wb_ref, 0))
    for j in range(1, 4):
        d_n2 = d_n2 + mm_nt(dh_ref[j], square(wb_ref, j))
    xhat, inv = moments(middle_ref[...])
    sums_ref[0:1] += jnp.sum(d_n2 * xhat, axis=0, keepdims=True)
    sums_ref[1:2] += jnp.sum(d_n2, axis=0, keepdims=True)
    d_middle = cot_ref[...].astype(f32) + ln_back(d_n2 * vec_ref[5:6, :], xhat, inv)
    dmid_ref[...] = d_middle
    d_branch = d_middle.astype(bf16)
    dbr_ref[...] = d_branch
    sums_ref[2:3] += jnp.sum(d_branch.astype(f32), axis=0, keepdims=True)

    @pl.when(pl.program_id(0) == 0)
    def _():
        wait_blocks(wa_ref, sem_a, 0, 32)

    datt_ref[...] = mm_nt(d_branch, square(wa_ref, 3)).astype(bf16)


def b3_kernel(rb, length, datt_ref, triple_ref, att_ref, dt_ref, sums_ref):
    width = datt_ref.shape[1]

    @pl.when(pl.program_id(0) == 0)
    def _():
        sums_ref[...] = jnp.zeros_like(sums_ref)

    first = half_mask(length, 2 * HD)
    pairs = width // (2 * HD)
    for r in range(rb):
        rows = slice(r * length, (r + 1) * length)
        for hp in range(pairs):
            lanes = slice(hp * 2 * HD, (hp + 1) * 2 * HD)
            dos = both(datt_ref[rows, lanes], first)
            p_low = att_ref[r * pairs + hp]
            p = p_low.astype(f32)
            d_a = mm_nt(dos, triple_ref[2, rows, lanes])
            inner = jnp.sum(p * d_a, axis=-1, keepdims=True)
            ds = (p * (d_a - inner)).astype(bf16)
            wide = jnp.concatenate([ds[:length], ds[length:]], axis=1)
            dt_ref[0, rows, lanes] = (mm(wide, both(triple_ref[1, rows, lanes], first)) * SCALE).astype(bf16)
            dt_ref[1, rows, lanes] = (mm_tn(ds, both(triple_ref[0, rows, lanes], first)) * SCALE).astype(bf16)
            dt_ref[2, rows, lanes] = mm_tn(p_low, dos).astype(bf16)
    sums_ref[0:1] += jnp.sum(dt_ref[0].astype(f32), axis=0, keepdims=True)
    sums_ref[1:2] += jnp.sum(dt_ref[2].astype(f32), axis=0, keepdims=True)


def ga_kernel(gpos, normed_ref, attended_ref, dt_ref, dbr_ref, keep_ref, send_ref, nt_ref):
    j = pl.program_id(0)
    width = normed_ref.shape[1]
    b = width // NB

    @pl.when(j == 0)
    def _():
        nt_ref[...] = normed_ref[...].T

    @pl.when(j == 3)
    def _():
        nt_ref[...] = attended_ref[...].T

    def block(rhs):
        for zf in range(4):
            g = mm(nt_ref[2 * zf * b : 2 * (zf + 1) * b], rhs).astype(bf16)
            put_pair(gpos, j * 4 + zf, keep_ref, send_ref, g[:b], g[b:])

    @pl.when(j < 3)
    def _():
        block(dt_ref[...])

    @pl.when(j == 3)
    def _():
        block(dbr_ref[...])


def b4_kernel(layout, rb, length, slots, tok_ref, emb_ref, dmid_ref, dt_ref, vec_ref, *rest):
    n = max(l[0] for l in layout) + 1
    pieces = rest[:n]
    ig_ref, rs_ref, sums_ref, w_ref, sem = rest[n:]
    step = pl.program_id(0)

    @pl.when(step == 0)
    def _():
        load_blocks(slots, pieces, layout, w_ref, sem)
        sums_ref[...] = jnp.zeros_like(sums_ref)
        rs_ref[...] = jnp.zeros_like(rs_ref)

    d_n = mm_nt(dt_ref[0], square(w_ref, 0))
    for q in range(1, 3):
        d_n = d_n + mm_nt(dt_ref[q], square(w_ref, q))
    xhat, inv = moments(residual_of(tok_ref, emb_ref, step, rb, length))
    sums_ref[0:1] += jnp.sum(d_n * xhat, axis=0, keepdims=True)
    sums_ref[1:2] += jnp.sum(d_n, axis=0, keepdims=True)
    d_start = dmid_ref[...] + ln_back(d_n * vec_ref[3:4, :], xhat, inv)
    ig_ref[...] = d_start.astype(bf16)
    for r in range(rb):
        rs_ref[pl.ds(step * rb + r, 1), :] = jnp.sum(d_start[r * length : (r + 1) * length], axis=0, keepdims=True)


def f3_kernel(layout, slots, act_ref, middle_ref, vec_ref, *rest):
    n = max(l[0] for l in layout) + 1
    pieces = rest[:n]
    out_ref, w_ref, sem = rest[n:]

    @pl.when(pl.program_id(0) == 0)
    def _():
        load_blocks(slots, pieces, layout, w_ref, sem)

    acc = mm(act_ref[0], square(w_ref, 0))
    for j in range(1, 4):
        acc = acc + mm(act_ref[j], square(w_ref, j))
    out_ref[...] = (middle_ref[...] + (acc + vec_ref[7:8, :])).astype(bf16)


def sds(shape, dtype):
    return jax.ShapeDtypeStruct(shape, dtype)


def full(shape):
    zeros = (0,) * len(shape)
    return pl.BlockSpec(shape, lambda i: zeros)


smem = pl.BlockSpec(memory_space=pltpu.SMEM)
hbm = pl.BlockSpec(memory_space=pl.ANY)


def call(kernel, grid, in_specs, out_shape, out_specs, scratch, flops, nbytes, args):
    return pl.pallas_call(
        kernel,
        grid=grid,
        in_specs=in_specs,
        out_shape=out_shape,
        out_specs=out_specs,
        scratch_shapes=scratch,
        compiler_params=pltpu.CompilerParams(
            dimension_semantics=("arbitrary",), vmem_limit_bytes=VMEM_LIMIT
        ),
        cost_estimate=pl.CostEstimate(flops=flops, bytes_accessed=nbytes, transcendentals=0),
    )(*args)


class Group:
    def __init__(self, arrays, layout, slots):
        self.arrays, self.layout, self.slots = arrays, layout, slots


def compute_f1(tok, emb, seg, pad, vecs, group, rows, length):
    n, width = tok.shape
    rb = 2 if rows % 2 == 0 else 1
    block = rb * length
    pairs = width // (2 * HD)
    b = width // NB
    return call(
        functools.partial(f1_kernel, group.layout, rb, length),
        (rows // rb,),
        [smem, pl.BlockSpec((block, width), lambda i: (i, 0)), full(emb.shape), full(seg.shape), full(pad.shape), full(vecs.shape)]
        + [hbm] * len(group.arrays),
        [sds((n, width), bf16), sds((3, n, width), bf16), sds((rows * pairs, 2 * length, length), bf16),
         sds((n, width), bf16), sds((n, width), f32), sds((n, width), bf16)],
        [pl.BlockSpec((block, width), lambda i: (i, 0)), pl.BlockSpec((3, block, width), lambda i: (0, i, 0)),
         pl.BlockSpec((rb * pairs, 2 * length, length), lambda i: (i, 0, 0)),
         pl.BlockSpec((block, width), lambda i: (i, 0)), pl.BlockSpec((block, width), lambda i: (i, 0)),
         pl.BlockSpec((block, width), lambda i: (i, 0))],
        [pltpu.VMEM((32, b, width), bf16), pltpu.SemaphoreType.DMA((32,))],
        2 * n * width * width * 4 * 3, 20 << 20,
        [group.slots, tok, emb, seg, pad, vecs, *group.arrays],
    )


def compute_f2(n2, cot, hb, group, gpos):
    n, width = n2.shape
    b = width // NB
    chunk = 256 if n % 256 == 0 else n
    return call(
        functools.partial(f2_kernel, group.layout, chunk),
        (4,),
        [smem, smem, full(n2.shape), full(cot.shape), full(hb.shape)] + [hbm] * len(group.arrays),
        [sds((4, n, width), bf16), sds((4, n, width), bf16), sds((16, b, width), bf16), sds((16, b, width), bf16)],
        [pl.BlockSpec((None, n, width), lambda i: (i, 0, 0)), pl.BlockSpec((None, n, width), lambda i: (i, 0, 0)),
         full((16, b, width)), full((16, b, width))],
        [pltpu.VMEM((32, b, width), bf16), pltpu.VMEM((chunk, width), f32), pltpu.SemaphoreType.DMA((32,))],
        2 * n * width * width * 8 * 2, 20 << 20,
        [group.slots, gpos, n2, cot, hb, *group.arrays],
    )


def compute_b1(n2, cot, gp, group, gpos):
    n, width = n2.shape
    b = width // NB
    chunk = 256 if n % 256 == 0 else n
    return call(
        functools.partial(b1_kernel, group.layout, chunk),
        (4,),
        [smem, smem, full(n2.shape), full(cot.shape), pl.BlockSpec((None, n, width), lambda i: (i, 0, 0))]
        + [hbm] * len(group.arrays),
        [sds((4, n, width), bf16), sds((8, width), f32), sds((8, width), f32), sds((16, b, width), bf16), sds((16, b, width), bf16)],
        [pl.BlockSpec((None, n, width), lambda i: (i, 0, 0)), full((8, width)), full((8, width)),
         full((16, b, width)), full((16, b, width))],
        [pltpu.VMEM((32, b, width), bf16), pltpu.VMEM((width, n), bf16), pltpu.VMEM((chunk, width), f32),
         pltpu.SemaphoreType.DMA((32,))],
        2 * n * width * width * 8 * 2, 20 << 20,
        [group.slots, gpos, n2, cot, gp, *group.arrays],
    )


def compute_b2(dh, cot, middle, vecs, ga, gb):
    n, width = cot.shape
    b = width // NB
    block = 256 if n % 256 == 0 else n
    tile = pl.BlockSpec((block, width), lambda i: (i, 0))
    return call(
        functools.partial(b2_kernel, ga.layout, gb.layout),
        (n // block,),
        [smem, smem, pl.BlockSpec((4, block, width), lambda i: (0, i, 0)), tile, tile, full(vecs.shape)]
        + [hbm] * (len(ga.arrays) + len(gb.arrays)),
        [sds((n, width), f32), sds((n, width), bf16), sds((n, width), bf16), sds((8, width), f32)],
        [tile, tile, tile, full((8, width))],
        [pltpu.VMEM((32, b, width), bf16), pltpu.VMEM((32, b, width), bf16),
         pltpu.SemaphoreType.DMA((32,)), pltpu.SemaphoreType.DMA((32,))],
        2 * n * width * width * 5 * 2, 20 << 20,
        [ga.slots, gb.slots, dh, cot, middle, vecs, *ga.arrays, *gb.arrays],
    )


def compute_b3(datt, triple, att, rows, length):
    n, width = datt.shape
    rb = 2 if rows % 2 == 0 else 1
    block = rb * length
    pairs = width // (2 * HD)
    wide = pl.BlockSpec((3, block, width), lambda i: (0, i, 0))
    return call(
        functools.partial(b3_kernel, rb, length),
        (rows // rb,),
        [pl.BlockSpec((block, width), lambda i: (i, 0)), wide,
         pl.BlockSpec((rb * pairs, 2 * length, length), lambda i: (i, 0, 0))],
        [sds((3, n, width), bf16), sds((8, width), f32)],
        [wide, full((8, width))],
        [],
        2 * n * width * width * 5 * 2, 20 << 20,
        [datt, triple, att],
    )


def compute_ga(normed, attended, dt, dbr, gpos):
    n, width = normed.shape
    b = width // NB
    return call(
        ga_kernel,
        (4,),
        [smem, full(normed.shape), full(attended.shape),
         pl.BlockSpec((None, n, width), lambda i: (jnp.minimum(i, 2), 0, 0)), full(dbr.shape)],
        [sds((16, b, width), bf16), sds((16, b, width), bf16)],
        [full((16, b, width)), full((16, b, width))],
        [pltpu.VMEM((width, n), bf16)],
        2 * n * width * width * 4 * 2, 12 << 20,
        [gpos, normed, attended, dt, dbr],
    )


def compute_b4(tok, emb, dmid, dt, vecs, group, rows, length):
    n, width = tok.shape
    rb = 2 if rows % 2 == 0 else 1
    block = rb * length
    b = width // NB
    return call(
        functools.partial(b4_kernel, group.layout, rb, length),
        (rows // rb,),
        [smem, pl.BlockSpec((block, width), lambda i: (i, 0)), full(emb.shape), pl.BlockSpec((block, width), lambda i: (i, 0)),
         pl.BlockSpec((3, block, width), lambda i: (0, i, 0)), full(vecs.shape)] + [hbm] * len(group.arrays),
        [sds((n, width), bf16), sds((8 * ((rows + 7) // 8), width), f32), sds((8, width), f32)],
        [pl.BlockSpec((block, width), lambda i: (i, 0)), full((8 * ((rows + 7) // 8), width)), full((8, width))],
        [pltpu.VMEM((32, b, width), bf16), pltpu.SemaphoreType.DMA((32,))],
        2 * n * width * width * 3 * 2, 12 << 20,
        [group.slots, tok, emb, dmid, dt, vecs, *group.arrays],
    )


def compute_f3(active, middle, vecs, group):
    n, width = middle.shape
    b = width // NB
    block = 256 if n % 256 == 0 else n
    return call(
        functools.partial(f3_kernel, group.layout),
        (n // block,),
        [smem, pl.BlockSpec((4, block, width), lambda i: (0, i, 0)), pl.BlockSpec((block, width), lambda i: (i, 0)), full(vecs.shape)]
        + [hbm] * len(group.arrays),
        sds((n, width), bf16),
        pl.BlockSpec((block, width), lambda i: (i, 0)),
        [pltpu.VMEM((32, b, width), bf16), pltpu.SemaphoreType.DMA((32,))],
        2 * n * width * width * 4 * 2, 12 << 20,
        [group.slots, active, middle, vecs, *group.arrays],
    )


def plain_groups(own_a, own_b, own_c, small):
    width = own_a.shape[2]
    slots = jnp.arange(32, dtype=jnp.int32)

    def group(whole):
        return Group([whole.reshape(32, width // NB, width)], [(0, 0, 32)], slots)

    a = lax.all_gather(own_a, "fsdp", axis=1, tiled=True)
    b = lax.all_gather(own_b, "fsdp", axis=1, tiled=True)
    c = lax.all_gather(own_c, "fsdp", axis=0, tiled=True)
    vec = [lax.all_gather(v, "fsdp", axis=0, tiled=True) for v in small]
    return group(a), group(b), group(c), jnp.stack(vec[:8]).astype(f32), vec[8].astype(f32).reshape(4, width)


def plain_scatter(keep, send, rows_first):
    b, width = keep.shape[1:]
    g = jnp.stack([keep.reshape(4, 4, b, width), send.reshape(4, 4, b, width)], axis=2)
    if rows_first:
        g = g.transpose(1, 2, 0, 3, 4).reshape(32 * b, width)
        s = lax.psum_scatter(g.astype(f32), "fsdp", scatter_dimension=0, tiled=True)
        return lax.psum(s, "dp")
    g = g.reshape(4, NB * b, width)
    s = lax.psum_scatter(g.astype(f32), "fsdp", scatter_dimension=1, tiled=True)
    return lax.psum(s, "dp")


def pick(stacked, i):
    return lax.dynamic_index_in_dim(stacked, i, axis=0, keepdims=False)


def xor_perm(n, k):
    return [(i, i ^ k) for i in range(n)]


def core_swap(v):
    return lax.ppermute(v, "fsdp", xor_perm(8, 1))


def x_swap(v):
    return lax.ppermute(v, "dp", xor_perm(4, 1))


def y_swap(v):
    return lax.ppermute(v, "dp", xor_perm(4, 2))


def diagonal_swap(v):
    return lax.ppermute(v, "dp", xor_perm(4, 3))


def z_shift(v, k):
    return lax.ppermute(v, "fsdp", [(i, (i + 2 * k) % 8) for i in range(8)])


def tie(values, after):
    return lax.optimization_barrier((values, after))[0]


def columns(v):
    return lax.all_to_all(jnp.broadcast_to(v[None], (4,) + v.shape), "dp", 0, 0, tiled=True)


def fast_slots(z, c):
    table = []
    for e in (0, 1):
        for q in range(4):
            for k in range(4):
                table.append(q * NB + 2 * lax.rem(z - k + 4, 4) + (c ^ e))
    return jnp.stack(table).astype(jnp.int32)


def along_z(v):
    return [v] + [z_shift(v, k) for k in (1, 2, 3)]


def rows_of(got, first, count):
    return jnp.stack([g[first : first + count] for g in got])


def down_slots(z, c, quarters_in):
    table = []
    for e in (0, 1):
        for part in quarters_in:
            for k in range(4):
                table += [8 * lax.rem(z - k + 4, 4) + 4 * (c ^ e) + q for q in part]
    return jnp.stack(table).astype(jnp.int32)


def fast_small(e0, e1, z, c, width, rows):
    pair = jnp.stack([jnp.where(c == 0, e0, e1), jnp.where(c == 0, e1, e0)], axis=1)
    got = jnp.stack([pick(pair, lax.rem(z - i + 4, 4)) for i in range(4)])
    got = got.reshape(8, 16, width).astype(f32)
    vecs = got[:, :8, : width // 8].transpose(1, 0, 2).reshape(8, width)
    hb = got[:, 8, : width // 2].reshape(4, width)
    ids = (got[:, 9, :rows] * 32.0 + got[:, 10, :rows]).astype(jnp.int32)
    return vecs, hb, ids


def add(u, v):
    return (u.astype(f32) + v.astype(f32)).astype(bf16)


class Scatter:
    def __init__(self, keep, send):
        b, width = keep.shape[1:]
        self.keep = keep.reshape(4, 4, b, width)
        self.got = core_swap(send).reshape(4, 4, b, width)

    def split(self):
        def part(deltas, half):
            ks = slice(2 * half, 2 * half + 2)
            return jnp.stack([add(self.keep[dl, ks], self.got[dl, ks]) for dl in deltas])

        self.out = [part((1, 3), 0), part((2, 3), 1)]
        self.own = [part((0, 2), 0), part((0, 1), 1)]

    def one(self):
        self.r1 = [x_swap(self.out[0]), y_swap(self.out[1])]

    def two(self):
        h = [add(self.own[i], self.r1[i]) for i in range(2)]
        self.h = h
        self.r2 = [y_swap(h[0][1]), x_swap(h[1][1])]

    def three(self):
        h3 = [add(self.h[i][0], self.r2[i]) for i in range(2)]
        h3 = [h3[0][0], h3[0][1], h3[1][0], h3[1][1]]
        self.r3 = [h3[0]] + [z_shift(h3[k], k) for k in (1, 2, 3)]

    def total(self):
        return sum(p.astype(f32) for p in self.r3).astype(bf16)


def per_device(
    fast, tokens, timesteps, segments, padding, cotangent, step_table,
    triple_weight, query_bias, value_bias, output_weight, output_bias,
    first_gain, first_shift, second_gain, second_shift,
    hidden_weight, hidden_bias, down_weight, down_bias,
):
    micro, local_rows, length, width = tokens.shape
    rows = micro * local_rows
    n = rows * length
    nd, nf = lax.axis_size("dp"), lax.axis_size("fsdp")
    d, f = lax.axis_index("dp"), lax.axis_index("fsdp")
    z, c = f // 2, lax.rem(f, 2)
    tok = tokens.reshape(n, width)
    cot = cotangent.reshape(n, width)
    seg = segments.reshape(rows, length).astype(f32)
    pad = padding.reshape(rows, length).astype(f32)

    ids = timesteps.reshape(rows)
    steps = lax.iota(jnp.int32, step_table.shape[0])
    q4 = [triple_weight[:, i * width : (i + 1) * width] for i in range(3)] + [output_weight]
    h4 = [hidden_weight[:, i * width : (i + 1) * width] for i in range(4)]
    vec_args = (query_bias, value_bias, output_bias, first_gain, first_shift, second_gain, second_shift, down_bias)
    if fast:
        b = width // NB
        own_a = pick(jnp.stack(q4), d)
        own_b = pick(jnp.stack(h4), d)
        small = jnp.zeros((16, width), bf16)
        small = small.at[:8, : width // nf].set(jnp.stack(vec_args))
        small = small.at[8, : 4 * width // nf].set(hidden_bias)
        small = small.at[9:11, :rows].set(jnp.stack([ids // 32, lax.rem(ids, 32)]).astype(bf16))
        got = along_z(jnp.concatenate([own_a, small], axis=0))
        s0 = rows_of(got, 0, b)
        e0 = rows_of(got, b, 16)
        e1 = core_swap(e0)
        own_c = [down_weight[i * b : (i + 1) * b] for i in range(4)]
        mine_a = columns(s0)
        got1 = along_z(tie(jnp.concatenate([own_b, own_c[0]], axis=0), got))
        vecs, hb, here = fast_small(e0, e1, z, c, width, rows)
        gpos = [(q ^ d) * 4 + lax.rem(zf - z + 4, 4) for q in range(4) for zf in range(4)] + [c]
        gpos = jnp.stack(gpos).astype(jnp.int32)
    else:
        ga, gb, gc, vecs, hb = plain_groups(
            jnp.stack(q4), jnp.stack(h4), down_weight, vec_args + (hidden_bias,)
        )
        gpos = jnp.concatenate([jnp.arange(16, dtype=jnp.int32), jnp.zeros((1,), jnp.int32)])
        here = lax.all_gather(ids, "fsdp", axis=0, tiled=True)

    onehot = (here.reshape(nf * rows)[:, None] == steps[None, :]).astype(bf16)
    looked = jnp.dot(onehot, step_table, preferred_element_type=f32).astype(bf16)
    looked = looked.reshape(nf, rows, width // nf)
    if fast:
        (mine_a, looked), got1 = lax.optimization_barrier(((mine_a, looked), got1))
    emb = lax.all_to_all(looked, "fsdp", 0, 0, tiled=True)
    emb = emb.transpose(1, 0, 2).reshape(rows, width).astype(f32)

    if fast:
        flat = (16, b, width)
        mine_a = mine_a.reshape(flat)
        core_a = core_swap(mine_a)
        s0 = rows_of(got1, 0, b)
        c0 = rows_of(got1, b, b)
        ga = Group([mine_a, core_a], [(0, 0, 16), (1, 0, 16)], fast_slots(z, c))
        tok_in, s0, own_c12 = tie((tok, s0, jnp.concatenate(own_c[1:3], axis=0)), (core_a, emb, c0))
        mine_b = columns(s0)
        got2 = along_z(own_c12)
    else:
        tok_in = tok
    normed, triple, att, attended, middle, n2 = compute_f1(tok_in, emb, seg, pad, vecs, ga, rows, length)
    if fast:
        mine_b, got2, n2 = lax.optimization_barrier((mine_b, got2, n2))
        mine_b = mine_b.reshape(flat)
        core_b = core_swap(mine_b)
        gb = Group([mine_b, core_b], [(0, 0, 16), (1, 0, 16)], fast_slots(z, c))
        n2, c0, c12, c3 = tie((n2, c0, got2, own_c[3]), core_b)
        c12 = jnp.stack(c12).reshape(8, b, width)
        got3 = along_z(c3)
        c0x, c12x = core_swap(c0), core_swap(c12)
    active, gp, keep_c, send_c = compute_f2(n2, cot, hb, gb, gpos)
    if fast:
        got3, c0x, c12x, gp, keep_c, send_c = lax.optimization_barrier((got3, c0x, c12x, gp, keep_c, send_c))
        c3 = jnp.stack(got3)
        c3x = core_swap(c3)
        gc = Group(
            [c0, c12, c3, c0x, c12x, c3x],
            [(0, 0, 4), (1, 0, 8), (2, 0, 4), (3, 0, 4), (4, 0, 8), (5, 0, 4)],
            down_slots(z, c, ((0,), (1, 2), (3,))),
        )
        sc = Scatter(keep_c, send_c)
        sc.split()
        gp, sc.out = lax.optimization_barrier((gp, sc.out))
        sc.one()
    dh, hb_sum, db_sum, keep_b, send_b = compute_b1(n2, cot, gp, gc, gpos)
    if fast:
        dh, keep_b, send_b, sc.r1 = lax.optimization_barrier((dh, keep_b, send_b, sc.r1))
        sc.two()
        sb = Scatter(keep_b, send_b)
        sb.split()
        dh, sb.out, sc.r2 = lax.optimization_barrier((dh, sb.out, sc.r2))
        sb.one()
        sc.three()
    dmid, dbr, datt, sums2 = compute_b2(dh, cot, middle, vecs, ga, gb)
    if fast:
        datt, sb.r1, sc.r3 = lax.optimization_barrier((datt, sb.r1, sc.r3))
        sb.two()
        out_c = columns(sc.total())
    dt, sums3 = compute_b3(datt, triple, att, rows, length)
    if fast:
        dt, sb.r2, out_c = lax.optimization_barrier((dt, sb.r2, out_c))
        sb.three()
    keep_a, send_a = compute_ga(normed, attended, dt, dbr, gpos)
    if fast:
        keep_a, send_a, sb.r3 = lax.optimization_barrier((keep_a, send_a, sb.r3))
        sa = Scatter(keep_a, send_a)
        sa.split()
        dt, sa.out = lax.optimization_barrier((dt, sa.out))
        sa.one()
    input_grad, row_sums, sums4 = compute_b4(tok, emb, dmid, dt, vecs, ga, rows, length)
    row_sums = row_sums[:rows]

    part = width // nf
    sums = jnp.concatenate(
        [row_sums, sums3[0:2], sums2[2:3], sums4[0:2], sums2[0:2], db_sum[0:1]], axis=0
    )
    lanes = sums.reshape(rows + 8, nf, part).transpose(1, 0, 2).reshape(nf, (rows + 8) * part)
    marks = jnp.broadcast_to(ids.astype(f32)[None, :], (nf, rows))
    payload = jnp.concatenate([lanes, hb_sum[:4].reshape(nf, 4 * part), marks], axis=1)
    moved = lax.all_to_all(payload, "fsdp", 0, 0, tiled=True)
    if fast:
        sa.r1, moved, active = lax.optimization_barrier((sa.r1, moved, active))
        sa.two()
        moved = columns(moved).reshape(nd * nf, payload.shape[1])
    else:
        moved = lax.all_gather(moved, "dp", axis=0, tiled=True)
    result = compute_f3(active, middle, vecs, gc)
    if fast:
        sa.r2, moved, tb = lax.optimization_barrier((sa.r2, moved, sb.r3))
        sa.three()
        sb.r3 = tb
        out_b = columns(sb.total())
        sa.r3, out_b = lax.optimization_barrier((sa.r3, out_b))
        out_a = columns(sa.total()).astype(f32)
        out_b = out_b.astype(f32)
        down_grad = out_c.astype(f32).reshape(4 * b, width)
    else:
        out_b = plain_scatter(keep_b, send_b, False)
        out_a = plain_scatter(keep_a, send_a, False)
        down_grad = plain_scatter(keep_c, send_c, True)
    hidden_grad = jnp.concatenate([out_b[i] for i in range(4)], axis=1)
    triple_grad = jnp.concatenate([out_a[i] for i in range(3)], axis=1)
    output_grad = out_a[3]
    table_rows = moved[:, : rows * part].reshape(nd * nf * rows, part)
    all_ids = moved[:, (rows + 12) * part :].astype(jnp.int32).reshape(1, nd * nf * rows)
    all_hot = (steps[:, None] == all_ids).astype(f32)
    table_grad = jnp.dot(all_hot, table_rows, precision=highest)
    vec_sums = jnp.sum(moved[:, rows * part : (rows + 12) * part], axis=0)
    v = [vec_sums[i * part : (i + 1) * part] for i in range(8)]
    hidden_bias_grad = vec_sums[8 * part :]
    shape = tokens.shape
    return (
        result.reshape(shape), input_grad.reshape(shape), table_grad, triple_grad, v[0], v[1], output_grad, v[2],
        v[3], v[4], v[5], v[6], hidden_grad, hidden_bias_grad, down_grad, v[7],
    )


def solution(mesh):
    fast = mesh.shape["dp"] == 4 and mesh.shape["fsdp"] == 8
    batch = ("dp", "fsdp")
    vec, mat, tab = P("fsdp"), P("fsdp", None), P(None, "fsdp")
    tokens_spec = P(None, batch, None, None)
    return jax.shard_map(
        functools.partial(per_device, fast),
        mesh=mesh,
        in_specs=(
            tokens_spec, P(None, batch), P(None, batch, None), P(None, batch, None), tokens_spec,
            tab, mat, vec, vec, mat, vec, vec, vec, vec, vec, mat, vec, mat, vec,
        ),
        out_specs=(
            tokens_spec, tokens_spec, tab, mat, vec, vec, mat, vec, vec, vec, vec, vec, mat, vec, mat, vec,
        ),
        check_vma=False,
    )
```

```python
import functools
import math

import jax
import jax.numpy as jnp
from jax import lax
from jax.experimental import pallas as pl
from jax.experimental.pallas import tpu as pltpu
from jax.sharding import PartitionSpec as P

HEADS = 12
HD = 64
EPS = 1e-05
MASKED = -1e30
SCALE = 1.0 / math.sqrt(HD)
GELU_C = math.sqrt(2.0 / math.pi)
GELU_A = 0.044715
VMEM_LIMIT = 60 * 1024 * 1024
highest = lax.Precision.HIGHEST
f32 = jnp.float32
bf16 = jnp.bfloat16

NB = 8


def mm(a, b):
    return lax.dot_general(a, b, (((1,), (0,)), ((), ())), preferred_element_type=f32)


def mm_nt(a, b):
    return lax.dot_general(a, b, (((1,), (1,)), ((), ())), preferred_element_type=f32)


def mm_tn(a, b):
    return lax.dot_general(a, b, (((0,), (0,)), ((), ())), preferred_element_type=f32)


def moments(v):
    average = jnp.mean(v, axis=-1, keepdims=True)
    centered = v - average
    variance = jnp.mean(centered * centered, axis=-1, keepdims=True)
    inv = lax.rsqrt(variance + EPS)
    return centered * inv, inv


def ln_back(e, xhat, inv):
    return (e - jnp.mean(e, -1, keepdims=True) - xhat * jnp.mean(e * xhat, -1, keepdims=True)) * inv


def start_blocks(slots_ref, pieces, layout, w_ref, sem):
    i = 0
    for piece, first, count in layout:
        for t in range(count):
            slot = slots_ref[i]
            pltpu.make_async_copy(pieces[piece].at[first + t], w_ref.at[slot], sem.at[slot]).start()
            i += 1


def wait_blocks(w_ref, sem, first, count):
    def one(t, carry):
        pltpu.make_async_copy(w_ref.at[first + t], w_ref.at[first + t], sem.at[first + t]).wait()
        return carry

    lax.fori_loop(0, count, one, 0)


def load_blocks(slots_ref, pieces, layout, w_ref, sem):
    start_blocks(slots_ref, pieces, layout, w_ref, sem)
    wait_blocks(w_ref, sem, 0, 32)


def square(w_ref, j):
    part = w_ref[NB * j : NB * (j + 1)]
    return part.reshape(part.shape[0] * part.shape[1], part.shape[2])


def put_pair(gpos_ref, at, keep_ref, send_ref, even, odd):
    idx = gpos_ref[at]
    side = gpos_ref[16]

    @pl.when(side == 0)
    def _():
        keep_ref[idx] = even
        send_ref[idx] = odd

    @pl.when(side != 0)
    def _():
        keep_ref[idx] = odd
        send_ref[idx] = even


def half_mask(rows, width):
    lane = lax.broadcasted_iota(jnp.int32, (rows, width), 1)
    return lane < HD


def both(x2, first):
    zero = jnp.zeros_like(x2)
    return jnp.concatenate([jnp.where(first, x2, zero), jnp.where(first, zero, x2)], axis=0)


def residual_of(tok_ref, emb_ref, step, rb, length):
    parts = []
    for r in range(rb):
        rows = tok_ref[r * length : (r + 1) * length].astype(f32)
        parts.append(rows + emb_ref[pl.ds(step * rb + r, 1), :])
    return jnp.concatenate(parts, axis=0) if rb > 1 else parts[0]


def f1_kernel(layout, rb, length, slots, tok_ref, emb_ref, seg_ref, pad_ref, vec_ref, *rest):
    n = max(l[0] for l in layout) + 1
    pieces = rest[:n]
    normed_ref, triple_ref, att_ref, attended_ref, middle_ref, n2_ref, w_ref, sem = rest[n:]
    step = pl.program_id(0)

    @pl.when(step == 0)
    def _():
        load_blocks(slots, pieces, layout, w_ref, sem)

    x = residual_of(tok_ref, emb_ref, step, rb, length)
    xhat, _inv = moments(x)
    normed = (xhat * vec_ref[3:4, :] + vec_ref[4:5, :]).astype(bf16)
    normed_ref[...] = normed
    width = normed.shape[1]
    for q, row in ((0, 0), (1, None), (2, 1)):
        t = mm(normed, square(w_ref, q))
        if row is not None:
            t = t + vec_ref[row : row + 1, :]
        triple_ref[q] = t.astype(bf16)
    eye = lax.broadcasted_iota(jnp.int32, (length, length), 0) == lax.broadcasted_iota(
        jnp.int32, (length, length), 1
    )
    first = half_mask(length, 2 * HD)
    for r in range(rb):
        seg = jnp.broadcast_to(seg_ref[pl.ds(step * rb + r, 1), :], (length, length))
        pad = jnp.broadcast_to(pad_ref[pl.ds(step * rb + r, 1), :], (length, length))
        same = seg == seg.T
        allowed = same & ((pad == 0.0) | eye)
        allowed = jnp.where(allowed, 1.0, 0.0)
        allowed = jnp.concatenate([allowed, allowed], axis=0) > 0.5
        rows = slice(r * length, (r + 1) * length)
        for hp in range(width // (2 * HD)):
            lanes = slice(hp * 2 * HD, (hp + 1) * 2 * HD)
            qs = both(triple_ref[0, rows, lanes], first)
            s = mm_nt(qs, triple_ref[1, rows, lanes]) * SCALE
            s = jnp.where(allowed, s, MASKED)
            top = jnp.max(s, axis=-1, keepdims=True)
            e = jnp.exp(s - top)
            p = (e / jnp.sum(e, axis=-1, keepdims=True)).astype(bf16)
            att_ref[r * (width // (2 * HD)) + hp] = p
            wide = jnp.concatenate([p[:length], p[length:]], axis=1)
            o = mm(wide, both(triple_ref[2, rows, lanes], first))
            attended_ref[rows, lanes] = o.astype(bf16)
    branch = mm(attended_ref[...], square(w_ref, 3)) + vec_ref[2:3, :]
    middle = x + branch
    middle_ref[...] = middle
    xhat2, _inv2 = moments(middle)
    n2_ref[...] = (xhat2 * vec_ref[5:6, :] + vec_ref[6:7, :]).astype(bf16)


def f2_kernel(layout, chunk, slots, gpos, n2_ref, cot_ref, hb_ref, *rest):
    n = max(l[0] for l in layout) + 1
    pieces = rest[:n]
    active_ref, gp_ref, keep_ref, send_ref, w_ref, h_ref, sem = rest[n:]
    j = pl.program_id(0)

    @pl.when(j == 0)
    def _():
        start_blocks(slots, pieces, layout, w_ref, sem)

    wait_blocks(w_ref, sem, j * NB, NB)
    tokens, width = n2_ref.shape
    w = w_ref[pl.ds(j * NB, NB)].reshape(width, width)
    bias = hb_ref[pl.ds(j, 1), :]
    sub = 32
    for m in range(tokens // chunk):
        h_ref[...] = mm(n2_ref[m * chunk : (m + 1) * chunk], w)
        for s in range(chunk // sub):
            v = h_ref[s * sub : (s + 1) * sub] + bias
            v2 = v * v
            t = jnp.tanh((GELU_C * v) * (1.0 + GELU_A * v2))
            half = 0.5 * (1.0 + t)
            at = slice(m * chunk + s * sub, m * chunk + (s + 1) * sub)
            active_ref[at] = (v * half).astype(bf16)
            slope = half + (0.5 * GELU_C) * v * (1.0 - t * t) * (1.0 + (3.0 * GELU_A) * v2)
            gp_ref[at] = slope.astype(bf16)
    cot = cot_ref[...]
    hw = width // 2
    ev = mm_tn(active_ref[:, :hw], cot).astype(bf16)
    od = mm_tn(active_ref[:, hw:], cot).astype(bf16)
    b = width // NB
    for q in range(4):
        put_pair(gpos, q * 4 + j, keep_ref, send_ref, ev[q * b : (q + 1) * b], od[q * b : (q + 1) * b])


def b1_kernel(layout, chunk, slots, gpos, n2_ref, cot_ref, gp_ref, *rest):
    n = max(l[0] for l in layout) + 1
    pieces = rest[:n]
    dh_ref, hb_ref, db_ref, keep_ref, send_ref, w_ref, nt_ref, h_ref, sem = rest[n:]
    j = pl.program_id(0)
    tokens, width = n2_ref.shape

    @pl.when(j == 0)
    def _():
        start_blocks(slots, pieces, layout, w_ref, sem)
        nt_ref[...] = n2_ref[...].T
        db_ref[...] = jnp.zeros_like(db_ref)
        db_ref[0:1] = jnp.sum(cot_ref[...].astype(f32), axis=0, keepdims=True)
        hb_ref[...] = jnp.zeros_like(hb_ref)

    wait_blocks(w_ref, sem, j * NB, NB)
    w = w_ref[pl.ds(j * NB, NB)].reshape(width, width)
    sub = 32
    total = jnp.zeros((8, width), f32)
    for m in range(tokens // chunk):
        h_ref[...] = mm_nt(cot_ref[m * chunk : (m + 1) * chunk], w)
        for s in range(chunk // sub):
            at = slice(m * chunk + s * sub, m * chunk + (s + 1) * sub)
            dh = (h_ref[s * sub : (s + 1) * sub] * gp_ref[at].astype(f32)).astype(bf16)
            dh_ref[at] = dh
            total = total + jnp.sum(dh.astype(f32).reshape(sub // 8, 8, width), axis=0)
    hb_ref[pl.ds(j, 1), :] = jnp.sum(total, axis=0, keepdims=True)
    b = width // NB
    dh_all = dh_ref[...]
    for zf in range(4):
        g = mm(nt_ref[zf * 2 * b : (zf + 1) * 2 * b], dh_all).astype(bf16)
        put_pair(gpos, j * 4 + zf, keep_ref, send_ref, g[:b], g[b:])


def b2_kernel(layout_a, layout_b, slots_a, slots_b, dh_ref, cot_ref, middle_ref, vec_ref, *rest):
    na = max(l[0] for l in layout_a) + 1
    nb = max(l[0] for l in layout_b) + 1
    pieces_a, pieces_b, rest = rest[:na], rest[na : na + nb], rest[na + nb :]
    dmid_ref, dbr_ref, datt_ref, sums_ref, wa_ref, wb_ref, sem_a, sem_b = rest

    @pl.when(pl.program_id(0) == 0)
    def _():
        start_blocks(slots_b, pieces_b, layout_b, wb_ref, sem_b)
        start_blocks(slots_a, pieces_a, layout_a, wa_ref, sem_a)
        sums_ref[...] = jnp.zeros_like(sums_ref)
        wait_blocks(wb_ref, sem_b, 0, 32)

    d_n2 = mm_nt(dh_ref[0], square(wb_ref, 0))
    for j in range(1, 4):
        d_n2 = d_n2 + mm_nt(dh_ref[j], square(wb_ref, j))
    xhat, inv = moments(middle_ref[...])
    sums_ref[0:1] += jnp.sum(d_n2 * xhat, axis=0, keepdims=True)
    sums_ref[1:2] += jnp.sum(d_n2, axis=0, keepdims=True)
    d_middle = cot_ref[...].astype(f32) + ln_back(d_n2 * vec_ref[5:6, :], xhat, inv)
    dmid_ref[...] = d_middle
    d_branch = d_middle.astype(bf16)
    dbr_ref[...] = d_branch
    sums_ref[2:3] += jnp.sum(d_branch.astype(f32), axis=0, keepdims=True)

    @pl.when(pl.program_id(0) == 0)
    def _():
        wait_blocks(wa_ref, sem_a, 0, 32)

    datt_ref[...] = mm_nt(d_branch, square(wa_ref, 3)).astype(bf16)


def b3_kernel(rb, length, datt_ref, triple_ref, att_ref, dt_ref, sums_ref):
    width = datt_ref.shape[1]

    @pl.when(pl.program_id(0) == 0)
    def _():
        sums_ref[...] = jnp.zeros_like(sums_ref)

    first = half_mask(length, 2 * HD)
    pairs = width // (2 * HD)
    for r in range(rb):
        rows = slice(r * length, (r + 1) * length)
        for hp in range(pairs):
            lanes = slice(hp * 2 * HD, (hp + 1) * 2 * HD)
            dos = both(datt_ref[rows, lanes], first)
            p_low = att_ref[r * pairs + hp]
            p = p_low.astype(f32)
            d_a = mm_nt(dos, triple_ref[2, rows, lanes])
            inner = jnp.sum(p * d_a, axis=-1, keepdims=True)
            ds = (p * (d_a - inner)).astype(bf16)
            wide = jnp.concatenate([ds[:length], ds[length:]], axis=1)
            dt_ref[0, rows, lanes] = (mm(wide, both(triple_ref[1, rows, lanes], first)) * SCALE).astype(bf16)
            dt_ref[1, rows, lanes] = (mm_tn(ds, both(triple_ref[0, rows, lanes], first)) * SCALE).astype(bf16)
            dt_ref[2, rows, lanes] = mm_tn(p_low, dos).astype(bf16)
    sums_ref[0:1] += jnp.sum(dt_ref[0].astype(f32), axis=0, keepdims=True)
    sums_ref[1:2] += jnp.sum(dt_ref[2].astype(f32), axis=0, keepdims=True)


def ga_kernel(gpos, normed_ref, attended_ref, dt_ref, dbr_ref, keep_ref, send_ref, nt_ref):
    j = pl.program_id(0)
    width = normed_ref.shape[1]
    b = width // NB

    @pl.when(j == 0)
    def _():
        nt_ref[...] = normed_ref[...].T

    @pl.when(j == 3)
    def _():
        nt_ref[...] = attended_ref[...].T

    def block(rhs):
        for zf in range(4):
            g = mm(nt_ref[2 * zf * b : 2 * (zf + 1) * b], rhs).astype(bf16)
            put_pair(gpos, j * 4 + zf, keep_ref, send_ref, g[:b], g[b:])

    @pl.when(j < 3)
    def _():
        block(dt_ref[...])

    @pl.when(j == 3)
    def _():
        block(dbr_ref[...])


def b4_kernel(layout, rb, length, slots, tok_ref, emb_ref, dmid_ref, dt_ref, vec_ref, *rest):
    n = max(l[0] for l in layout) + 1
    pieces = rest[:n]
    ig_ref, rs_ref, sums_ref, w_ref, sem = rest[n:]
    step = pl.program_id(0)

    @pl.when(step == 0)
    def _():
        load_blocks(slots, pieces, layout, w_ref, sem)
        sums_ref[...] = jnp.zeros_like(sums_ref)
        rs_ref[...] = jnp.zeros_like(rs_ref)

    d_n = mm_nt(dt_ref[0], square(w_ref, 0))
    for q in range(1, 3):
        d_n = d_n + mm_nt(dt_ref[q], square(w_ref, q))
    xhat, inv = moments(residual_of(tok_ref, emb_ref, step, rb, length))
    sums_ref[0:1] += jnp.sum(d_n * xhat, axis=0, keepdims=True)
    sums_ref[1:2] += jnp.sum(d_n, axis=0, keepdims=True)
    d_start = dmid_ref[...] + ln_back(d_n * vec_ref[3:4, :], xhat, inv)
    ig_ref[...] = d_start.astype(bf16)
    for r in range(rb):
        rs_ref[pl.ds(step * rb + r, 1), :] = jnp.sum(d_start[r * length : (r + 1) * length], axis=0, keepdims=True)


def f3_kernel(layout, slots, act_ref, middle_ref, vec_ref, *rest):
    n = max(l[0] for l in layout) + 1
    pieces = rest[:n]
    out_ref, w_ref, sem = rest[n:]

    @pl.when(pl.program_id(0) == 0)
    def _():
        load_blocks(slots, pieces, layout, w_ref, sem)

    acc = mm(act_ref[0], square(w_ref, 0))
    for j in range(1, 4):
        acc = acc + mm(act_ref[j], square(w_ref, j))
    out_ref[...] = (middle_ref[...] + (acc + vec_ref[7:8, :])).astype(bf16)


def sds(shape, dtype):
    return jax.ShapeDtypeStruct(shape, dtype)


def full(shape):
    zeros = (0,) * len(shape)
    return pl.BlockSpec(shape, lambda i: zeros)


smem = pl.BlockSpec(memory_space=pltpu.SMEM)
hbm = pl.BlockSpec(memory_space=pl.ANY)


def call(kernel, grid, in_specs, out_shape, out_specs, scratch, flops, nbytes, args):
    return pl.pallas_call(
        kernel,
        grid=grid,
        in_specs=in_specs,
        out_shape=out_shape,
        out_specs=out_specs,
        scratch_shapes=scratch,
        compiler_params=pltpu.CompilerParams(
            dimension_semantics=("arbitrary",), vmem_limit_bytes=VMEM_LIMIT
        ),
        cost_estimate=pl.CostEstimate(flops=flops, bytes_accessed=nbytes, transcendentals=0),
    )(*args)


class Group:
    def __init__(self, arrays, layout, slots):
        self.arrays, self.layout, self.slots = arrays, layout, slots


def compute_f1(tok, emb, seg, pad, vecs, group, rows, length):
    n, width = tok.shape
    rb = 2 if rows % 2 == 0 else 1
    block = rb * length
    pairs = width // (2 * HD)
    b = width // NB
    return call(
        functools.partial(f1_kernel, group.layout, rb, length),
        (rows // rb,),
        [smem, pl.BlockSpec((block, width), lambda i: (i, 0)), full(emb.shape), full(seg.shape), full(pad.shape), full(vecs.shape)]
        + [hbm] * len(group.arrays),
        [sds((n, width), bf16), sds((3, n, width), bf16), sds((rows * pairs, 2 * length, length), bf16),
         sds((n, width), bf16), sds((n, width), f32), sds((n, width), bf16)],
        [pl.BlockSpec((block, width), lambda i: (i, 0)), pl.BlockSpec((3, block, width), lambda i: (0, i, 0)),
         pl.BlockSpec((rb * pairs, 2 * length, length), lambda i: (i, 0, 0)),
         pl.BlockSpec((block, width), lambda i: (i, 0)), pl.BlockSpec((block, width), lambda i: (i, 0)),
         pl.BlockSpec((block, width), lambda i: (i, 0))],
        [pltpu.VMEM((32, b, width), bf16), pltpu.SemaphoreType.DMA((32,))],
        2 * n * width * width * 4 * 3, 20 << 20,
        [group.slots, tok, emb, seg, pad, vecs, *group.arrays],
    )


def compute_f2(n2, cot, hb, group, gpos):
    n, width = n2.shape
    b = width // NB
    chunk = 256 if n % 256 == 0 else n
    return call(
        functools.partial(f2_kernel, group.layout, chunk),
        (4,),
        [smem, smem, full(n2.shape), full(cot.shape), full(hb.shape)] + [hbm] * len(group.arrays),
        [sds((4, n, width), bf16), sds((4, n, width), bf16), sds((16, b, width), bf16), sds((16, b, width), bf16)],
        [pl.BlockSpec((None, n, width), lambda i: (i, 0, 0)), pl.BlockSpec((None, n, width), lambda i: (i, 0, 0)),
         full((16, b, width)), full((16, b, width))],
        [pltpu.VMEM((32, b, width), bf16), pltpu.VMEM((chunk, width), f32), pltpu.SemaphoreType.DMA((32,))],
        2 * n * width * width * 8 * 2, 20 << 20,
        [group.slots, gpos, n2, cot, hb, *group.arrays],
    )


def compute_b1(n2, cot, gp, group, gpos):
    n, width = n2.shape
    b = width // NB
    chunk = 256 if n % 256 == 0 else n
    return call(
        functools.partial(b1_kernel, group.layout, chunk),
        (4,),
        [smem, smem, full(n2.shape), full(cot.shape), pl.BlockSpec((None, n, width), lambda i: (i, 0, 0))]
        + [hbm] * len(group.arrays),
        [sds((4, n, width), bf16), sds((8, width), f32), sds((8, width), f32), sds((16, b, width), bf16), sds((16, b, width), bf16)],
        [pl.BlockSpec((None, n, width), lambda i: (i, 0, 0)), full((8, width)), full((8, width)),
         full((16, b, width)), full((16, b, width))],
        [pltpu.VMEM((32, b, width), bf16), pltpu.VMEM((width, n), bf16), pltpu.VMEM((chunk, width), f32),
         pltpu.SemaphoreType.DMA((32,))],
        2 * n * width * width * 8 * 2, 20 << 20,
        [group.slots, gpos, n2, cot, gp, *group.arrays],
    )


def compute_b2(dh, cot, middle, vecs, ga, gb):
    n, width = cot.shape
    b = width // NB
    block = 256 if n % 256 == 0 else n
    tile = pl.BlockSpec((block, width), lambda i: (i, 0))
    return call(
        functools.partial(b2_kernel, ga.layout, gb.layout),
        (n // block,),
        [smem, smem, pl.BlockSpec((4, block, width), lambda i: (0, i, 0)), tile, tile, full(vecs.shape)]
        + [hbm] * (len(ga.arrays) + len(gb.arrays)),
        [sds((n, width), f32), sds((n, width), bf16), sds((n, width), bf16), sds((8, width), f32)],
        [tile, tile, tile, full((8, width))],
        [pltpu.VMEM((32, b, width), bf16), pltpu.VMEM((32, b, width), bf16),
         pltpu.SemaphoreType.DMA((32,)), pltpu.SemaphoreType.DMA((32,))],
        2 * n * width * width * 5 * 2, 20 << 20,
        [ga.slots, gb.slots, dh, cot, middle, vecs, *ga.arrays, *gb.arrays],
    )


def compute_b3(datt, triple, att, rows, length):
    n, width = datt.shape
    rb = 2 if rows % 2 == 0 else 1
    block = rb * length
    pairs = width // (2 * HD)
    wide = pl.BlockSpec((3, block, width), lambda i: (0, i, 0))
    return call(
        functools.partial(b3_kernel, rb, length),
        (rows // rb,),
        [pl.BlockSpec((block, width), lambda i: (i, 0)), wide,
         pl.BlockSpec((rb * pairs, 2 * length, length), lambda i: (i, 0, 0))],
        [sds((3, n, width), bf16), sds((8, width), f32)],
        [wide, full((8, width))],
        [],
        2 * n * width * width * 5 * 2, 20 << 20,
        [datt, triple, att],
    )


def compute_ga(normed, attended, dt, dbr, gpos):
    n, width = normed.shape
    b = width // NB
    return call(
        ga_kernel,
        (4,),
        [smem, full(normed.shape), full(attended.shape),
         pl.BlockSpec((None, n, width), lambda i: (jnp.minimum(i, 2), 0, 0)), full(dbr.shape)],
        [sds((16, b, width), bf16), sds((16, b, width), bf16)],
        [full((16, b, width)), full((16, b, width))],
        [pltpu.VMEM((width, n), bf16)],
        2 * n * width * width * 4 * 2, 12 << 20,
        [gpos, normed, attended, dt, dbr],
    )


def compute_b4(tok, emb, dmid, dt, vecs, group, rows, length):
    n, width = tok.shape
    rb = 2 if rows % 2 == 0 else 1
    block = rb * length
    b = width // NB
    return call(
        functools.partial(b4_kernel, group.layout, rb, length),
        (rows // rb,),
        [smem, pl.BlockSpec((block, width), lambda i: (i, 0)), full(emb.shape), pl.BlockSpec((block, width), lambda i: (i, 0)),
         pl.BlockSpec((3, block, width), lambda i: (0, i, 0)), full(vecs.shape)] + [hbm] * len(group.arrays),
        [sds((n, width), bf16), sds((8 * ((rows + 7) // 8), width), f32), sds((8, width), f32)],
        [pl.BlockSpec((block, width), lambda i: (i, 0)), full((8 * ((rows + 7) // 8), width)), full((8, width))],
        [pltpu.VMEM((32, b, width), bf16), pltpu.SemaphoreType.DMA((32,))],
        2 * n * width * width * 3 * 2, 12 << 20,
        [group.slots, tok, emb, dmid, dt, vecs, *group.arrays],
    )


def compute_f3(active, middle, vecs, group):
    n, width = middle.shape
    b = width // NB
    block = 256 if n % 256 == 0 else n
    return call(
        functools.partial(f3_kernel, group.layout),
        (n // block,),
        [smem, pl.BlockSpec((4, block, width), lambda i: (0, i, 0)), pl.BlockSpec((block, width), lambda i: (i, 0)), full(vecs.shape)]
        + [hbm] * len(group.arrays),
        sds((n, width), bf16),
        pl.BlockSpec((block, width), lambda i: (i, 0)),
        [pltpu.VMEM((32, b, width), bf16), pltpu.SemaphoreType.DMA((32,))],
        2 * n * width * width * 4 * 2, 12 << 20,
        [group.slots, active, middle, vecs, *group.arrays],
    )


def plain_groups(own_a, own_b, own_c, small):
    width = own_a.shape[2]
    slots = jnp.arange(32, dtype=jnp.int32)

    def group(whole):
        return Group([whole.reshape(32, width // NB, width)], [(0, 0, 32)], slots)

    a = lax.all_gather(own_a, "fsdp", axis=1, tiled=True)
    b = lax.all_gather(own_b, "fsdp", axis=1, tiled=True)
    c = lax.all_gather(own_c, "fsdp", axis=0, tiled=True)
    vec = [lax.all_gather(v, "fsdp", axis=0, tiled=True) for v in small]
    return group(a), group(b), group(c), jnp.stack(vec[:8]).astype(f32), vec[8].astype(f32).reshape(4, width)


def plain_scatter(keep, send, rows_first):
    b, width = keep.shape[1:]
    g = jnp.stack([keep.reshape(4, 4, b, width), send.reshape(4, 4, b, width)], axis=2)
    if rows_first:
        g = g.transpose(1, 2, 0, 3, 4).reshape(32 * b, width)
        s = lax.psum_scatter(g.astype(f32), "fsdp", scatter_dimension=0, tiled=True)
        return lax.psum(s, "dp")
    g = g.reshape(4, NB * b, width)
    s = lax.psum_scatter(g.astype(f32), "fsdp", scatter_dimension=1, tiled=True)
    return lax.psum(s, "dp")


def pick(stacked, i):
    return lax.dynamic_index_in_dim(stacked, i, axis=0, keepdims=False)


def xor_perm(n, k):
    return [(i, i ^ k) for i in range(n)]


def core_swap(v):
    return lax.ppermute(v, "fsdp", xor_perm(8, 1))


def x_swap(v):
    return lax.ppermute(v, "dp", xor_perm(4, 1))


def y_swap(v):
    return lax.ppermute(v, "dp", xor_perm(4, 2))


def diagonal_swap(v):
    return lax.ppermute(v, "dp", xor_perm(4, 3))


def z_shift(v, k):
    return lax.ppermute(v, "fsdp", [(i, (i + 2 * k) % 8) for i in range(8)])


def tie(values, after):
    return lax.optimization_barrier((values, after))[0]


def columns(v):
    return lax.all_to_all(jnp.broadcast_to(v[None], (4,) + v.shape), "dp", 0, 0, tiled=True)


def fast_slots(z, c):
    table = []
    for e in (0, 1):
        for q in range(4):
            for k in range(4):
                table.append(q * NB + 2 * lax.rem(z - k + 4, 4) + (c ^ e))
    return jnp.stack(table).astype(jnp.int32)


def along_z(v):
    return [v] + [z_shift(v, k) for k in (1, 2, 3)]


def rows_of(got, first, count):
    return jnp.stack([g[first : first + count] for g in got])


def down_slots(z, c, quarters_in):
    table = []
    for e in (0, 1):
        for part in quarters_in:
            for k in range(4):
                table += [8 * lax.rem(z - k + 4, 4) + 4 * (c ^ e) + q for q in part]
    return jnp.stack(table).astype(jnp.int32)


def shard_order(e0, e1, z, c):
    pair = jnp.stack([jnp.where(c == 0, e0, e1), jnp.where(c == 0, e1, e0)], axis=1)
    got = jnp.stack([pick(pair, lax.rem(z - i + 4, 4)) for i in range(4)])
    return got.reshape((8,) + got.shape[2:])


def fast_small(got, width, rows):
    got = got.astype(f32)
    vecs = got[:, :8, : width // 8].transpose(1, 0, 2).reshape(8, width)
    hb = got[:, 8, : width // 2].reshape(4, width)
    ids = (got[:, 9, :rows] * 32.0 + got[:, 10, :rows]).astype(jnp.int32)
    return vecs, hb, ids


def add(u, v):
    return (u.astype(f32) + v.astype(f32)).astype(bf16)


class Scatter:
    def __init__(self, keep, send):
        b, width = keep.shape[1:]
        self.keep = keep.reshape(4, 4, b, width)
        self.got = core_swap(send).reshape(4, 4, b, width)

    def split(self):
        def part(deltas, half):
            ks = slice(2 * half, 2 * half + 2)
            return jnp.stack([add(self.keep[dl, ks], self.got[dl, ks]) for dl in deltas])

        self.out = [part((1, 3), 0), part((2, 3), 1)]
        self.own = [part((0, 2), 0), part((0, 1), 1)]

    def one(self):
        self.r1 = [x_swap(self.out[0]), y_swap(self.out[1])]

    def two(self):
        h = [add(self.own[i], self.r1[i]) for i in range(2)]
        self.h = h
        self.r2 = [y_swap(h[0][1]), x_swap(h[1][1])]

    def three(self):
        h3 = [add(self.h[i][0], self.r2[i]) for i in range(2)]
        h3 = [h3[0][0], h3[0][1], h3[1][0], h3[1][1]]
        self.r3 = [h3[0]] + [z_shift(h3[k], k) for k in (1, 2, 3)]

    def total(self):
        return sum(p.astype(f32) for p in self.r3).astype(bf16)


def spread(mine):
    return [mine, x_swap(mine), y_swap(mine), diagonal_swap(mine)]


def quarters(got, d):
    got = jnp.stack(got)
    return [pick(got, d ^ q).astype(f32) for q in range(4)]


def per_device(
    fast, tokens, timesteps, segments, padding, cotangent, step_table,
    triple_weight, query_bias, value_bias, output_weight, output_bias,
    first_gain, first_shift, second_gain, second_shift,
    hidden_weight, hidden_bias, down_weight, down_bias,
):
    micro, local_rows, length, width = tokens.shape
    rows = micro * local_rows
    n = rows * length
    nd, nf = lax.axis_size("dp"), lax.axis_size("fsdp")
    d, f = lax.axis_index("dp"), lax.axis_index("fsdp")
    z, c = f // 2, lax.rem(f, 2)
    tok = tokens.reshape(n, width)
    cot = cotangent.reshape(n, width)
    seg = segments.reshape(rows, length).astype(f32)
    pad = padding.reshape(rows, length).astype(f32)

    ids = timesteps.reshape(rows)
    steps = lax.iota(jnp.int32, step_table.shape[0])
    q4 = [triple_weight[:, i * width : (i + 1) * width] for i in range(3)] + [output_weight]
    h4 = [hidden_weight[:, i * width : (i + 1) * width] for i in range(4)]
    vec_args = (query_bias, value_bias, output_bias, first_gain, first_shift, second_gain, second_shift, down_bias)
    if fast:
        b = width // NB
        own_a = pick(jnp.stack(q4), d)
        own_b = pick(jnp.stack(h4), d)
        small = jnp.zeros((16, width), bf16)
        small = small.at[:8, : width // nf].set(jnp.stack(vec_args))
        small = small.at[8, : 4 * width // nf].set(hidden_bias)
        small = small.at[9:11, :rows].set(jnp.stack([ids // 32, lax.rem(ids, 32)]).astype(bf16))
        got = along_z(jnp.concatenate([own_a, small], axis=0))
        s0 = rows_of(got, 0, b)
        e0 = rows_of(got, b, 16)
        mine_a = columns(s0)
        got1 = along_z(tie(jnp.concatenate([own_b, down_weight[:b]], axis=0), got))
        vecs, hb, here = fast_small(shard_order(e0, core_swap(e0), z, c), width, rows)
        gpos = [(q ^ d) * 4 + lax.rem(zf - z + 4, 4) for q in range(4) for zf in range(4)] + [c]
        gpos = jnp.stack(gpos).astype(jnp.int32)
        slots = fast_slots(z, c)
        slots_c = down_slots(z, c, ((0,), (1, 2), (3,)))
    else:
        ga, gb, gc, vecs, hb = plain_groups(
            jnp.stack(q4), jnp.stack(h4), down_weight, vec_args + (hidden_bias,)
        )
        gpos = jnp.concatenate([jnp.arange(16, dtype=jnp.int32), jnp.zeros((1,), jnp.int32)])
        here = lax.all_gather(ids, "fsdp", axis=0, tiled=True)

    onehot = (here.reshape(nf * rows)[:, None] == steps[None, :]).astype(bf16)
    looked = jnp.dot(onehot, step_table, preferred_element_type=f32).astype(bf16)
    if fast:
        looked, seg, pad, vecs, hb, gpos, slots, slots_c = lax.optimization_barrier(
            (looked.reshape(rows, width), seg, pad, vecs, hb, gpos, slots, slots_c)
        )
        sent = jnp.pad(looked, ((0, 16 - rows), (0, 0)))
        got_e = jnp.stack(along_z(sent))
        mine_a, got1, got_e = lax.optimization_barrier((mine_a, got1, got_e))
        emb = shard_order(got_e, core_swap(got_e), z, c)[:, :rows].reshape(nf, nf, rows, width // nf)
        emb = pick(emb.transpose(1, 0, 2, 3), f)
    else:
        emb = lax.all_to_all(looked.reshape(nf, rows, width // nf), "fsdp", 0, 0, tiled=True)
    emb = emb.transpose(1, 0, 2).reshape(rows, width).astype(f32)

    if fast:
        flat = (16, b, width)
        mine_a = mine_a.reshape(flat)
        core_a = core_swap(mine_a)
        ga = Group([mine_a, core_a], [(0, 0, 16), (1, 0, 16)], slots)
        mine_b = columns(rows_of(got1, 0, b))
        c0 = rows_of(got1, b, b)
        got2 = along_z(tie(down_weight[b : 3 * b], got1))
        tok_in = tie(tok, (core_a, emb))
    else:
        tok_in = tok
    normed, triple, att, attended, middle, n2 = compute_f1(tok_in, emb, seg, pad, vecs, ga, rows, length)
    if fast:
        mine_b, n2, got2 = lax.optimization_barrier((mine_b.reshape(flat), n2, got2))
        core_b = core_swap(mine_b)
        gb = Group([mine_b, core_b], [(0, 0, 16), (1, 0, 16)], slots)
        n2, c0, got2, own_c3 = tie((n2, c0, got2, down_weight[3 * b :]), core_b)
        got3 = along_z(own_c3)
        c12 = jnp.stack(got2).reshape(8, b, width)
        c0x, c12x = core_swap(c0), core_swap(c12)
    active, gp, keep_c, send_c = compute_f2(n2, cot, hb, gb, gpos)
    if fast:
        got3, c0x, c12x, gp, keep_c, send_c = lax.optimization_barrier((got3, c0x, c12x, gp, keep_c, send_c))
        c3 = jnp.stack(got3)
        gc = Group(
            [c0, c12, c3, c0x, c12x, core_swap(c3)],
            [(0, 0, 4), (1, 0, 8), (2, 0, 4), (3, 0, 4), (4, 0, 8), (5, 0, 4)],
            slots_c,
        )
        sc = Scatter(keep_c, send_c)
        sc.split()
        gp, sc.out = lax.optimization_barrier((gp, sc.out))
        sc.one()
    dh, hb_sum, db_sum, keep_b, send_b = compute_b1(n2, cot, gp, gc, gpos)
    if fast:
        dh, keep_b, send_b, sc.r1 = lax.optimization_barrier((dh, keep_b, send_b, sc.r1))
        sc.two()
        sb = Scatter(keep_b, send_b)
        sb.split()
        dh, sb.out = lax.optimization_barrier((dh, sb.out))
        sb.one()
    dmid, dbr, datt, sums2 = compute_b2(dh, cot, middle, vecs, ga, gb)
    if fast:
        datt, sb.r1, sc.r2 = lax.optimization_barrier((datt, sb.r1, sc.r2))
        sb.two()
        sc.three()
    dt, sums3 = compute_b3(datt, triple, att, rows, length)
    if fast:
        dt, sb.r2, sc.r3 = lax.optimization_barrier((dt, sb.r2, sc.r3))
        sb.three()
        mine_c = sc.total()
    keep_a, send_a = compute_ga(normed, attended, dt, dbr, gpos)
    if fast:
        keep_a, send_a, sb.r3, mine_c, dt = lax.optimization_barrier((keep_a, send_a, sb.r3, mine_c, dt))
        sa = Scatter(keep_a, send_a)
        sa.split()
        dt, sa.out, active = lax.optimization_barrier((dt, sa.out, active))
        sa.one()
        out_c = spread(mine_c)
        mine_b = sb.total()
    input_grad, row_sums, sums4 = compute_b4(tok, emb, dmid, dt, vecs, ga, rows, length)
    if fast:
        result = compute_f3(active, middle, vecs, gc)
        sa.r1, row_sums, sums4, result, out_c = lax.optimization_barrier((sa.r1, row_sums, sums4, result, out_c))

    part = width // nf
    every = [row_sums, sums3, sums2, sums4, db_sum, hb_sum]
    lines = row_sums.shape[0] + 32
    marks = jnp.broadcast_to(ids.astype(f32)[None, :], (nf, rows))
    lanes = jnp.concatenate(every[:5], axis=0).reshape(lines, nf, part).transpose(1, 0, 2).reshape(nf, lines * part)
    payload = jnp.concatenate([lanes, hb_sum[:4].reshape(nf, 4 * part), marks], axis=1)
    nt, end = rows * part, payload.shape[1] - rows
    if fast:
        sa.two()
        out_b = spread(mine_b)
    moved = lax.all_to_all(payload, "fsdp", 0, 0, tiled=True)
    if fast:
        sa.r2, moved, out_b = lax.optimization_barrier((sa.r2, moved, out_b))
        sa.three()
        moved = columns(moved).reshape(nd * nf, payload.shape[1])
        moved, sa.r3 = lax.optimization_barrier((moved, sa.r3))
    else:
        moved = lax.all_gather(moved, "dp", axis=0, tiled=True)
    table_rows = moved[:, :nt].reshape(nd * nf * rows, part)
    all_ids = moved[:, end:].astype(jnp.int32).reshape(1, nd * nf * rows)
    vec_sums = jnp.sum(moved[:, nt:end], axis=0)
    if not fast:
        result = compute_f3(active, middle, vecs, gc)
    if fast:
        out_a, out_b, out_c = (quarters(v, d) for v in (spread(sa.total()), out_b, out_c))
        down_grad = jnp.concatenate(out_c, axis=0)
    else:
        out_b = plain_scatter(keep_b, send_b, False)
        out_a = plain_scatter(keep_a, send_a, False)
        down_grad = plain_scatter(keep_c, send_c, True)
    hidden_grad = jnp.concatenate([out_b[i] for i in range(4)], axis=1)
    triple_grad = jnp.concatenate([out_a[i] for i in range(3)], axis=1)
    output_grad = out_a[3]
    all_hot = (steps[:, None] == all_ids).astype(f32)
    table_grad = jnp.dot(all_hot, table_rows, precision=highest)
    kept = vec_sums[(lines - 32 - rows) * part : (lines - rows) * part].reshape(32, part)
    v = [kept[i] for i in (0, 1, 10, 16, 17, 8, 9, 24)]
    hidden_bias_grad = vec_sums[(lines - rows) * part :]
    shape = tokens.shape
    return (
        result.reshape(shape), input_grad.reshape(shape), table_grad, triple_grad, v[0], v[1], output_grad, v[2],
        v[3], v[4], v[5], v[6], hidden_grad, hidden_bias_grad, down_grad, v[7],
    )


def solution(mesh):
    fast = mesh.shape["dp"] == 4 and mesh.shape["fsdp"] == 8
    batch = ("dp", "fsdp")
    vec, mat, tab = P("fsdp"), P("fsdp", None), P(None, "fsdp")
    tokens_spec = P(None, batch, None, None)
    return jax.shard_map(
        functools.partial(per_device, fast),
        mesh=mesh,
        in_specs=(
            tokens_spec, P(None, batch), P(None, batch, None), P(None, batch, None), tokens_spec,
            tab, mat, vec, vec, mat, vec, vec, vec, vec, vec, mat, vec, mat, vec,
        ),
        out_specs=(
            tokens_spec, tokens_spec, tab, mat, vec, vec, mat, vec, vec, vec, vec, vec, mat, vec, mat, vec,
        ),
        check_vma=False,
    )
```

```python
import functools
import math

import jax
import jax.numpy as jnp
from jax import lax
from jax.experimental import pallas as pl
from jax.experimental.pallas import tpu as pltpu
from jax.sharding import PartitionSpec as P

HEADS = 12
HD = 64
EPS = 1e-05
MASKED = -1e30
SCALE = 1.0 / math.sqrt(HD)
GELU_C = math.sqrt(2.0 / math.pi)
GELU_A = 0.044715
VMEM_LIMIT = 60 * 1024 * 1024
highest = lax.Precision.HIGHEST
f32 = jnp.float32
bf16 = jnp.bfloat16

NB = 8


def mm(a, b):
    return lax.dot_general(a, b, (((1,), (0,)), ((), ())), preferred_element_type=f32)


def mm_nt(a, b):
    return lax.dot_general(a, b, (((1,), (1,)), ((), ())), preferred_element_type=f32)


def mm_tn(a, b):
    return lax.dot_general(a, b, (((0,), (0,)), ((), ())), preferred_element_type=f32)


def moments(v):
    average = jnp.mean(v, axis=-1, keepdims=True)
    centered = v - average
    variance = jnp.mean(centered * centered, axis=-1, keepdims=True)
    inv = lax.rsqrt(variance + EPS)
    return centered * inv, inv


def ln_back(e, xhat, inv):
    return (e - jnp.mean(e, -1, keepdims=True) - xhat * jnp.mean(e * xhat, -1, keepdims=True)) * inv


def start_blocks(slots_ref, pieces, layout, w_ref, sem, low=None):
    i = 0
    for piece, first, count in layout:
        for t in range(count):
            slot = slots_ref[i]
            if low is None:
                pltpu.make_async_copy(pieces[piece].at[first + t], w_ref.at[slot], sem.at[slot]).start()
            else:

                @pl.when(slot >= low)
                def _(piece=piece, at=first + t, slot=slot):
                    place = slot - low
                    pltpu.make_async_copy(pieces[piece].at[at], w_ref.at[place], sem.at[place]).start()

            i += 1


def wait_blocks(w_ref, sem, first, count):
    def one(t, carry):
        pltpu.make_async_copy(w_ref.at[first + t], w_ref.at[first + t], sem.at[first + t]).wait()
        return carry

    lax.fori_loop(0, count, one, 0)


def load_blocks(slots_ref, pieces, layout, w_ref, sem):
    start_blocks(slots_ref, pieces, layout, w_ref, sem)
    wait_blocks(w_ref, sem, 0, 32)


def square(w_ref, j):
    part = w_ref[NB * j : NB * (j + 1)]
    return part.reshape(part.shape[0] * part.shape[1], part.shape[2])


def block_copies(gpos_ref, spots, buf_ref, even_rows, odd_rows, b, keep_ref, send_ref, sem):
    for side in range(2):
        first, second = (keep_ref, send_ref) if side == 0 else (send_ref, keep_ref)
        copies = []
        for t, at in enumerate(spots):
            idx = gpos_ref[at]
            copies.append(pltpu.make_async_copy(buf_ref.at[pl.ds(even_rows[t], b)], first.at[idx], sem.at[2 * t]))
            copies.append(pltpu.make_async_copy(buf_ref.at[pl.ds(odd_rows[t], b)], second.at[idx], sem.at[2 * t + 1]))
        yield side, copies


def send_blocks(gpos_ref, spots, buf_ref, even_rows, odd_rows, b, keep_ref, send_ref, sem):
    core = gpos_ref[16]
    for side, copies in block_copies(gpos_ref, spots, buf_ref, even_rows, odd_rows, b, keep_ref, send_ref, sem):

        @pl.when(core == side)
        def _(copies=copies):
            for cp in copies:
                cp.start()


def drain_blocks(buf_ref, b, sem):
    for t in range(8):
        pltpu.make_async_copy(buf_ref.at[pl.ds(0, b)], buf_ref.at[pl.ds(0, b)], sem.at[t]).wait()


def half_mask(rows, width):
    lane = lax.broadcasted_iota(jnp.int32, (rows, width), 1)
    return lane < HD


def both(x2, first):
    zero = jnp.zeros_like(x2)
    return jnp.concatenate([jnp.where(first, x2, zero), jnp.where(first, zero, x2)], axis=0)


def residual_of(tok_ref, emb_ref, step, rb, length):
    parts = []
    for r in range(rb):
        rows = tok_ref[r * length : (r + 1) * length].astype(f32)
        parts.append(rows + emb_ref[pl.ds(step * rb + r, 1), :])
    return jnp.concatenate(parts, axis=0) if rb > 1 else parts[0]


def f1_kernel(layout, rb, length, slots, tok_ref, emb_ref, seg_ref, pad_ref, vec_ref, *rest):
    n = max(l[0] for l in layout) + 1
    pieces = rest[:n]
    normed_ref, triple_ref, att_ref, attended_ref, middle_ref, n2_ref, w_ref, sem = rest[n:]
    step = pl.program_id(0)

    @pl.when(step == 0)
    def _():
        load_blocks(slots, pieces, layout, w_ref, sem)

    x = residual_of(tok_ref, emb_ref, step, rb, length)
    xhat, _inv = moments(x)
    normed = (xhat * vec_ref[3:4, :] + vec_ref[4:5, :]).astype(bf16)
    normed_ref[...] = normed
    width = normed.shape[1]
    for q, row in ((0, 0), (1, None), (2, 1)):
        t = mm(normed, square(w_ref, q))
        if row is not None:
            t = t + vec_ref[row : row + 1, :]
        triple_ref[q] = t.astype(bf16)
    eye = lax.broadcasted_iota(jnp.int32, (length, length), 0) == lax.broadcasted_iota(
        jnp.int32, (length, length), 1
    )
    first = half_mask(length, 2 * HD)
    masks = []
    for r in range(rb):
        seg = jnp.broadcast_to(seg_ref[pl.ds(step * rb + r, 1), :], (length, length))
        pad = jnp.broadcast_to(pad_ref[pl.ds(step * rb + r, 1), :], (length, length))
        allowed = (seg == seg.T) & ((pad == 0.0) | eye)
        allowed = jnp.where(allowed, 1.0, 0.0)
        masks.append(jnp.concatenate([allowed, allowed], axis=0) > 0.5)
    pairs = width // (2 * HD)
    every = [(r, hp) for r in range(rb) for hp in range(pairs)]
    for start in range(0, len(every), 12):
        some = []
        for r, hp in every[start : start + 12]:
            rows = slice(r * length, (r + 1) * length)
            lanes = slice(hp * 2 * HD, (hp + 1) * 2 * HD)
            s = mm_nt(both(triple_ref[0, rows, lanes], first), triple_ref[1, rows, lanes]) * SCALE
            some.append((r, hp, rows, lanes, jnp.where(masks[r], s, MASKED)))
        done = []
        for r, hp, rows, lanes, s in some:
            e = jnp.exp(s - jnp.max(s, axis=-1, keepdims=True))
            p = (e / jnp.sum(e, axis=-1, keepdims=True)).astype(bf16)
            att_ref[r * pairs + hp] = p
            done.append((rows, lanes, p))
        for rows, lanes, p in done:
            wide = jnp.concatenate([p[:length], p[length:]], axis=1)
            attended_ref[rows, lanes] = mm(wide, both(triple_ref[2, rows, lanes], first)).astype(bf16)
    branch = mm(attended_ref[...], square(w_ref, 3)) + vec_ref[2:3, :]
    middle = x + branch
    middle_ref[...] = middle
    xhat2, _inv2 = moments(middle)
    n2_ref[...] = (xhat2 * vec_ref[5:6, :] + vec_ref[6:7, :]).astype(bf16)


def gelu_rows(h_ref, bias, active_ref, gp_ref, first, count):
    sub = 32
    for m in range(count // sub):
        at = slice(first + m * sub, first + (m + 1) * sub)
        v = h_ref[at] + bias
        v2 = v * v
        w = GELU_C * v
        cubic = w * v2
        t = jnp.tanh(w + cubic * GELU_A)
        half = 0.5 * t + 0.5
        active_ref[at] = (v * half).astype(bf16)
        steep = w + cubic * (3.0 * GELU_A)
        gp_ref[at] = (half + (half - half * t) * steep).astype(bf16)


def f2_kernel(layout, slots, gpos, n2_ref, cot_hbm, hb_ref, *rest):
    n = max(l[0] for l in layout) + 1
    pieces = rest[:n]
    active_ref, gp_ref, keep_ref, send_ref, w_ref, h_ref, g_ref, cot_ref, sem, cot_sem, out_sem = rest[n:]
    j = pl.program_id(0)
    load = pltpu.make_async_copy(cot_hbm, cot_ref, cot_sem)

    @pl.when(j == 0)
    def _():
        start_blocks(slots, pieces, layout, w_ref, sem)
        load.start()

    wait_blocks(w_ref, sem, j * NB, NB)
    tokens, width = n2_ref.shape
    b = width // NB
    bias = hb_ref[pl.ds(j, 1), :]
    slot = lax.rem(j, 2)

    @pl.when(j >= 2)
    def _():
        drain_blocks(g_ref.at[slot], b, out_sem.at[slot])

    part = w_ref[pl.ds(j * NB, NB)].reshape(width, width)
    half = tokens // 2
    h_ref[:half] = mm(n2_ref[:half], part)
    h_ref[half:] = mm(n2_ref[half:], part)
    gelu_rows(h_ref, bias, active_ref, gp_ref, 0, half)
    gelu_rows(h_ref, bias, active_ref, gp_ref, half, half)

    @pl.when(j == 0)
    def _():
        load.wait()

    g_ref[slot] = mm_tn(active_ref[...], cot_ref[...]).astype(bf16)
    spots = [q * 4 + j for q in range(4)]
    even_rows, odd_rows = [q * b for q in range(4)], [(4 + q) * b for q in range(4)]
    send_blocks(gpos, spots, g_ref.at[slot], even_rows, odd_rows, b, keep_ref, send_ref, out_sem.at[slot])

    @pl.when(j == 3)
    def _():
        drain_blocks(g_ref.at[0], b, out_sem.at[0])
        drain_blocks(g_ref.at[1], b, out_sem.at[1])


def b1_kernel(layout, chunk, slots, gpos, n2_ref, cot_ref, gp_ref, *rest):
    n = max(l[0] for l in layout) + 1
    pieces = rest[:n]
    dh_ref, hb_ref, db_ref, keep_ref, send_ref, w_ref, h_ref, g_ref, sem, out_sem = rest[n:]
    j = pl.program_id(0)
    tokens, width = n2_ref.shape
    b = width // NB
    slot = lax.rem(j, 2)

    @pl.when(j == 0)
    def _():
        start_blocks(slots, pieces, layout, w_ref, sem)
        db_ref[...] = jnp.zeros_like(db_ref)
        db_ref[0:1] = jnp.sum(cot_ref[...].astype(f32), axis=0, keepdims=True)
        hb_ref[...] = jnp.zeros_like(hb_ref)

    wait_blocks(w_ref, sem, j * NB, NB)
    w = w_ref[pl.ds(j * NB, NB)].reshape(width, width)
    sub = 32
    total = jnp.zeros((8, width), f32)
    for m in range(tokens // chunk):
        h_ref[m] = mm_nt(cot_ref[m * chunk : (m + 1) * chunk], w)
    for m in range(tokens // chunk):
        for s in range(chunk // sub):
            at = slice(m * chunk + s * sub, m * chunk + (s + 1) * sub)
            dh = (h_ref[m, s * sub : (s + 1) * sub] * gp_ref[at].astype(f32)).astype(bf16)
            dh_ref[at] = dh
            total = total + jnp.sum(dh.astype(f32).reshape(sub // 8, 8, width), axis=0)
    hb_ref[pl.ds(j, 1), :] = jnp.sum(total, axis=0, keepdims=True)

    @pl.when(j >= 2)
    def _():
        drain_blocks(g_ref.at[slot], b, out_sem.at[slot])

    g_ref[slot] = mm_tn(n2_ref[...], dh_ref[...]).astype(bf16)
    spots = [j * 4 + zf for zf in range(4)]
    even_rows, odd_rows = [2 * zf * b for zf in range(4)], [(2 * zf + 1) * b for zf in range(4)]
    send_blocks(gpos, spots, g_ref.at[slot], even_rows, odd_rows, b, keep_ref, send_ref, out_sem.at[slot])

    @pl.when(j == 3)
    def _():
        drain_blocks(g_ref.at[0], b, out_sem.at[0])
        drain_blocks(g_ref.at[1], b, out_sem.at[1])


def b2_kernel(
    layout_a, layout_b, rb, length, slots_a, slots_b,
    dh_ref, cot_ref, middle_ref, vec_ref, triple_ref, att_ref, *rest
):
    na = max(l[0] for l in layout_a) + 1
    nb = max(l[0] for l in layout_b) + 1
    pieces_a, pieces_b, rest = rest[:na], rest[na : na + nb], rest[na + nb :]
    dmid_ref, dbr_ref, dt_ref, sums_ref, wo_ref, wb_ref, datt_ref, sem_a, sem_b = rest
    width = cot_ref.shape[1]
    b = width // NB

    @pl.when(pl.program_id(0) == 0)
    def _():
        start_blocks(slots_b, pieces_b, layout_b, wb_ref, sem_b)
        start_blocks(slots_a, pieces_a, layout_a, wo_ref, sem_a, 3 * NB)
        sums_ref[...] = jnp.zeros_like(sums_ref)
        wait_blocks(wb_ref, sem_b, 0, 32)
        wait_blocks(wo_ref, sem_a, 0, NB)

    def slope(j):
        return mm_nt(dh_ref[:, j * width : (j + 1) * width], square(wb_ref, j))

    d_n2 = slope(0)
    for j in range(1, 4):
        d_n2 = d_n2 + slope(j)
    xhat, inv = moments(middle_ref[...])
    sums_ref[0:1] += jnp.sum(d_n2 * xhat, axis=0, keepdims=True)
    sums_ref[1:2] += jnp.sum(d_n2, axis=0, keepdims=True)
    d_middle = cot_ref[...].astype(f32) + ln_back(d_n2 * vec_ref[5:6, :], xhat, inv)
    dmid_ref[...] = d_middle
    d_branch = d_middle.astype(bf16)
    dbr_ref[...] = d_branch
    sums_ref[2:3] += jnp.sum(d_branch.astype(f32), axis=0, keepdims=True)

    datt_ref[...] = mm_nt(d_branch, wo_ref[...].reshape(width, width)).astype(bf16)
    first = half_mask(length, 2 * HD)
    pairs = width // (2 * HD)
    every = [(r, hp) for r in range(rb) for hp in range(pairs)]
    for start in range(0, len(every), 6):
        some = []
        for r, hp in every[start : start + 6]:
            rows = slice(r * length, (r + 1) * length)
            lanes = slice(hp * 2 * HD, (hp + 1) * 2 * HD)
            dos = both(datt_ref[rows, lanes], first)
            some.append((rows, lanes, dos, att_ref[r * pairs + hp], mm_nt(dos, triple_ref[2, rows, lanes])))
        slopes = []
        for rows, lanes, dos, p_low, d_a in some:
            dt_ref[2, rows, lanes] = mm_tn(p_low, dos).astype(bf16)
            p = p_low.astype(f32)
            inner = jnp.sum(p * d_a, axis=-1, keepdims=True)
            slopes.append((p * (d_a - inner)).astype(bf16))
        for (rows, lanes, dos, p_low, d_a), ds in zip(some, slopes):
            wide = jnp.concatenate([ds[:length], ds[length:]], axis=1)
            dt_ref[0, rows, lanes] = (mm(wide, both(triple_ref[1, rows, lanes], first)) * SCALE).astype(bf16)
            dt_ref[1, rows, lanes] = (mm_tn(ds, both(triple_ref[0, rows, lanes], first)) * SCALE).astype(bf16)
    sums_ref[3:4] += jnp.sum(dt_ref[0].astype(f32), axis=0, keepdims=True)
    sums_ref[4:5] += jnp.sum(dt_ref[2].astype(f32), axis=0, keepdims=True)


def ga_kernel(
    gpos, normed_ref, dt_ref, attended_hbm, dbr_hbm, keep_ref, send_ref, attended_ref, dbr_ref, g_ref, in_sem, out_sem
):
    j = pl.program_id(0)
    width = normed_ref.shape[1]
    b = width // NB
    slot = lax.rem(j, 2)
    loads = [
        pltpu.make_async_copy(attended_hbm, attended_ref, in_sem.at[0]),
        pltpu.make_async_copy(dbr_hbm, dbr_ref, in_sem.at[1]),
    ]

    @pl.when(j == 0)
    def _():
        for cp in loads:
            cp.start()

    @pl.when(j >= 2)
    def _():
        drain_blocks(g_ref.at[slot], b, out_sem.at[slot])

    @pl.when(j < 3)
    def _():
        g_ref[slot] = mm_tn(normed_ref[...], dt_ref[...]).astype(bf16)

    @pl.when(j == 3)
    def _():
        for cp in loads:
            cp.wait()
        g_ref[slot] = mm_tn(attended_ref[...], dbr_ref[...]).astype(bf16)

    spots = [j * 4 + zf for zf in range(4)]
    even_rows, odd_rows = [2 * zf * b for zf in range(4)], [(2 * zf + 1) * b for zf in range(4)]
    send_blocks(gpos, spots, g_ref.at[slot], even_rows, odd_rows, b, keep_ref, send_ref, out_sem.at[slot])

    @pl.when(j == 3)
    def _():
        drain_blocks(g_ref.at[0], b, out_sem.at[0])
        drain_blocks(g_ref.at[1], b, out_sem.at[1])


def b4_kernel(layout, rb, length, slots, tok_ref, emb_ref, dmid_ref, dt_ref, vec_ref, *rest):
    n = max(l[0] for l in layout) + 1
    pieces = rest[:n]
    ig_ref, rs_ref, sums_ref, w_ref, sem = rest[n:]
    step = pl.program_id(0)

    @pl.when(step == 0)
    def _():
        load_blocks(slots, pieces, layout, w_ref, sem)
        sums_ref[...] = jnp.zeros_like(sums_ref)
        rs_ref[...] = jnp.zeros_like(rs_ref)

    d_n = mm_nt(dt_ref[0], square(w_ref, 0))
    for q in range(1, 3):
        d_n = d_n + mm_nt(dt_ref[q], square(w_ref, q))
    xhat, inv = moments(residual_of(tok_ref, emb_ref, step, rb, length))
    sums_ref[0:1] += jnp.sum(d_n * xhat, axis=0, keepdims=True)
    sums_ref[1:2] += jnp.sum(d_n, axis=0, keepdims=True)
    d_start = dmid_ref[...] + ln_back(d_n * vec_ref[3:4, :], xhat, inv)
    ig_ref[...] = d_start.astype(bf16)
    for r in range(rb):
        rs_ref[pl.ds(step * rb + r, 1), :] = jnp.sum(d_start[r * length : (r + 1) * length], axis=0, keepdims=True)


def f3_kernel(layout, slots, act_ref, middle_ref, vec_ref, *rest):
    n = max(l[0] for l in layout) + 1
    pieces = rest[:n]
    out_ref, w_ref, sem = rest[n:]

    @pl.when(pl.program_id(0) == 0)
    def _():
        load_blocks(slots, pieces, layout, w_ref, sem)

    width = middle_ref.shape[1]
    acc = mm(act_ref[...], w_ref[...].reshape(4 * width, width))
    out_ref[...] = (middle_ref[...] + (acc + vec_ref[7:8, :])).astype(bf16)


def sds(shape, dtype):
    return jax.ShapeDtypeStruct(shape, dtype)


def full(shape):
    zeros = (0,) * len(shape)
    return pl.BlockSpec(shape, lambda i: zeros)


smem = pl.BlockSpec(memory_space=pltpu.SMEM)
hbm = pl.BlockSpec(memory_space=pl.ANY)


def call(kernel, grid, in_specs, out_shape, out_specs, scratch, flops, nbytes, args):
    return pl.pallas_call(
        kernel,
        grid=grid,
        in_specs=in_specs,
        out_shape=out_shape,
        out_specs=out_specs,
        scratch_shapes=scratch,
        compiler_params=pltpu.CompilerParams(
            dimension_semantics=("arbitrary",), vmem_limit_bytes=VMEM_LIMIT
        ),
        cost_estimate=pl.CostEstimate(flops=flops, bytes_accessed=nbytes, transcendentals=0),
    )(*args)


class Group:
    def __init__(self, arrays, layout, slots):
        self.arrays, self.layout, self.slots = arrays, layout, slots


def compute_f1(tok, emb, seg, pad, vecs, group, rows, length):
    n, width = tok.shape
    rb = 2 if rows % 2 == 0 else 1
    block = rb * length
    pairs = width // (2 * HD)
    b = width // NB
    return call(
        functools.partial(f1_kernel, group.layout, rb, length),
        (rows // rb,),
        [smem, pl.BlockSpec((block, width), lambda i: (i, 0)), full(emb.shape), full(seg.shape), full(pad.shape), full(vecs.shape)]
        + [hbm] * len(group.arrays),
        [sds((n, width), bf16), sds((3, n, width), bf16), sds((rows * pairs, 2 * length, length), bf16),
         sds((n, width), bf16), sds((n, width), f32), sds((n, width), bf16)],
        [pl.BlockSpec((block, width), lambda i: (i, 0)), pl.BlockSpec((3, block, width), lambda i: (0, i, 0)),
         pl.BlockSpec((rb * pairs, 2 * length, length), lambda i: (i, 0, 0)),
         pl.BlockSpec((block, width), lambda i: (i, 0)), pl.BlockSpec((block, width), lambda i: (i, 0)),
         pl.BlockSpec((block, width), lambda i: (i, 0))],
        [pltpu.VMEM((32, b, width), bf16), pltpu.SemaphoreType.DMA((32,))],
        2 * n * width * width * 4 * 3, 20 << 20,
        [group.slots, tok, emb, seg, pad, vecs, *group.arrays],
    )


def compute_f2(n2, cot, hb, group, gpos):
    n, width = n2.shape
    b = width // NB
    column = pl.BlockSpec((n, width), lambda i: (0, i))
    return call(
        functools.partial(f2_kernel, group.layout),
        (4,),
        [smem, smem, full(n2.shape), hbm, full(hb.shape)] + [hbm] * len(group.arrays),
        [sds((n, 4 * width), bf16), sds((n, 4 * width), bf16), sds((16, b, width), bf16), sds((16, b, width), bf16)],
        [column, column, hbm, hbm],
        [pltpu.VMEM((32, b, width), bf16), pltpu.VMEM((n, width), f32), pltpu.VMEM((2, width, width), bf16), pltpu.VMEM((n, width), bf16),
         pltpu.SemaphoreType.DMA((32,)), pltpu.SemaphoreType.DMA(()), pltpu.SemaphoreType.DMA((2, 8))],
        2 * n * width * width * 8 * 2, 20 << 20,
        [group.slots, gpos, n2, cot, hb, *group.arrays],
    )


def compute_b1(n2, cot, gp, group, gpos):
    n, width = n2.shape
    b = width // NB
    chunk = 256 if n % 256 == 0 else n
    column = pl.BlockSpec((n, width), lambda i: (0, i))
    return call(
        functools.partial(b1_kernel, group.layout, chunk),
        (4,),
        [smem, smem, full(n2.shape), full(cot.shape), column] + [hbm] * len(group.arrays),
        [sds((n, 4 * width), bf16), sds((8, width), f32), sds((8, width), f32), sds((16, b, width), bf16), sds((16, b, width), bf16)],
        [column, full((8, width)), full((8, width)), hbm, hbm],
        [pltpu.VMEM((32, b, width), bf16), pltpu.VMEM((n // chunk, chunk, width), f32), pltpu.VMEM((2, width, width), bf16),
         pltpu.SemaphoreType.DMA((32,)), pltpu.SemaphoreType.DMA((2, 8))],
        2 * n * width * width * 8 * 2, 20 << 20,
        [group.slots, gpos, n2, cot, gp, *group.arrays],
    )


def compute_b2(dh, cot, middle, vecs, triple, att, ga, gb, rows, length):
    n, width = cot.shape
    rb = 2 if rows % 2 == 0 else 1
    block = rb * length
    pairs = width // (2 * HD)
    b = width // NB
    tile = pl.BlockSpec((block, width), lambda i: (i, 0))
    wide = pl.BlockSpec((3, block, width), lambda i: (0, i, 0))
    return call(
        functools.partial(b2_kernel, ga.layout, gb.layout, rb, length),
        (rows // rb,),
        [smem, smem, pl.BlockSpec((block, 4 * width), lambda i: (i, 0)), tile, tile, full(vecs.shape), wide,
         pl.BlockSpec((rb * pairs, 2 * length, length), lambda i: (i, 0, 0))]
        + [hbm] * (len(ga.arrays) + len(gb.arrays)),
        [sds((n, width), f32), sds((n, width), bf16), sds((3, n, width), bf16), sds((8, width), f32)],
        [tile, tile, wide, full((8, width))],
        [pltpu.VMEM((NB, b, width), bf16), pltpu.VMEM((32, b, width), bf16), pltpu.VMEM((block, width), bf16),
         pltpu.SemaphoreType.DMA((NB,)), pltpu.SemaphoreType.DMA((32,))],
        2 * n * width * width * 10, 30 << 20,
        [ga.slots, gb.slots, dh, cot, middle, vecs, triple, att, *ga.arrays, *gb.arrays],
    )


def compute_ga(normed, attended, dt, dbr, gpos):
    n, width = normed.shape
    b = width // NB
    return call(
        ga_kernel,
        (4,),
        [smem, full(normed.shape), pl.BlockSpec((None, n, width), lambda i: (jnp.minimum(i, 2), 0, 0)), hbm, hbm],
        [sds((16, b, width), bf16), sds((16, b, width), bf16)],
        [hbm, hbm],
        [pltpu.VMEM((n, width), bf16), pltpu.VMEM((n, width), bf16), pltpu.VMEM((2, width, width), bf16),
         pltpu.SemaphoreType.DMA((2,)), pltpu.SemaphoreType.DMA((2, 8))],
        2 * n * width * width * 4 * 2, 12 << 20,
        [gpos, normed, dt, attended, dbr],
    )


def compute_b4(tok, emb, dmid, dt, vecs, group, rows, length):
    n, width = tok.shape
    rb = 2 if rows % 2 == 0 else 1
    block = rb * length
    b = width // NB
    return call(
        functools.partial(b4_kernel, group.layout, rb, length),
        (rows // rb,),
        [smem, pl.BlockSpec((block, width), lambda i: (i, 0)), full(emb.shape), pl.BlockSpec((block, width), lambda i: (i, 0)),
         pl.BlockSpec((3, block, width), lambda i: (0, i, 0)), full(vecs.shape)] + [hbm] * len(group.arrays),
        [sds((n, width), bf16), sds((8 * ((rows + 7) // 8), width), f32), sds((8, width), f32)],
        [pl.BlockSpec((block, width), lambda i: (i, 0)), full((8 * ((rows + 7) // 8), width)), full((8, width))],
        [pltpu.VMEM((32, b, width), bf16), pltpu.SemaphoreType.DMA((32,))],
        2 * n * width * width * 3 * 2, 12 << 20,
        [group.slots, tok, emb, dmid, dt, vecs, *group.arrays],
    )


def compute_f3(active, middle, vecs, group):
    n, width = middle.shape
    b = width // NB
    block = 256 if n % 256 == 0 else n
    return call(
        functools.partial(f3_kernel, group.layout),
        (n // block,),
        [smem, pl.BlockSpec((block, 4 * width), lambda i: (i, 0)), pl.BlockSpec((block, width), lambda i: (i, 0)), full(vecs.shape)]
        + [hbm] * len(group.arrays),
        sds((n, width), bf16),
        pl.BlockSpec((block, width), lambda i: (i, 0)),
        [pltpu.VMEM((32, b, width), bf16), pltpu.SemaphoreType.DMA((32,))],
        2 * n * width * width * 4 * 2, 12 << 20,
        [group.slots, active, middle, vecs, *group.arrays],
    )


def plain_groups(own_a, own_b, own_c, small):
    width = own_a.shape[2]
    slots = jnp.arange(32, dtype=jnp.int32)

    def group(whole):
        return Group([whole.reshape(32, width // NB, width)], [(0, 0, 32)], slots)

    a = lax.all_gather(own_a, "fsdp", axis=1, tiled=True)
    b = lax.all_gather(own_b, "fsdp", axis=1, tiled=True)
    c = lax.all_gather(own_c, "fsdp", axis=0, tiled=True)
    vec = [lax.all_gather(v, "fsdp", axis=0, tiled=True) for v in small]
    return group(a), group(b), group(c), jnp.stack(vec[:8]).astype(f32), vec[8].astype(f32).reshape(4, width)


def plain_scatter(keep, send, rows_first):
    b, width = keep.shape[1:]
    g = jnp.stack([keep.reshape(4, 4, b, width), send.reshape(4, 4, b, width)], axis=2)
    if rows_first:
        g = g.transpose(1, 2, 0, 3, 4).reshape(32 * b, width)
        s = lax.psum_scatter(g.astype(f32), "fsdp", scatter_dimension=0, tiled=True)
        return lax.psum(s, "dp")
    g = g.reshape(4, NB * b, width)
    s = lax.psum_scatter(g.astype(f32), "fsdp", scatter_dimension=1, tiled=True)
    return lax.psum(s, "dp")


def pick(stacked, i):
    return lax.dynamic_index_in_dim(stacked, i, axis=0, keepdims=False)


def xor_perm(n, k):
    return [(i, i ^ k) for i in range(n)]


def core_swap(v):
    return lax.ppermute(v, "fsdp", xor_perm(8, 1))


def x_swap(v):
    return lax.ppermute(v, "dp", xor_perm(4, 1))


def y_swap(v):
    return lax.ppermute(v, "dp", xor_perm(4, 2))


def diagonal_swap(v):
    return lax.ppermute(v, "dp", xor_perm(4, 3))


def z_shift(v, k):
    return lax.ppermute(v, "fsdp", [(i, (i + 2 * k) % 8) for i in range(8)])


def tie(values, after):
    return lax.optimization_barrier((values, after))[0]


def columns(v):
    return lax.all_to_all(jnp.broadcast_to(v[None], (4,) + v.shape), "dp", 0, 0, tiled=True)


quarter_major = [(e, 4 * q, 4) for q in range(4) for e in (0, 1)]


def fast_slots(z, c):
    table = []
    for q in range(4):
        for e in (0, 1):
            for k in range(4):
                table.append(q * NB + 2 * lax.rem(z - k + 4, 4) + (c ^ e))
    return jnp.stack(table).astype(jnp.int32)


def along_z(v):
    return [v] + [z_shift(v, k) for k in (1, 2, 3)]


def rows_of(got, first, count):
    return jnp.stack([g[first : first + count] for g in got])


def down_slots(z, c, quarters_in):
    table = []
    for e in (0, 1):
        for part in quarters_in:
            for k in range(4):
                table += [8 * lax.rem(z - k + 4, 4) + 4 * (c ^ e) + q for q in part]
    return jnp.stack(table).astype(jnp.int32)


def shard_order(e0, e1, z, c):
    pair = jnp.stack([jnp.where(c == 0, e0, e1), jnp.where(c == 0, e1, e0)], axis=1)
    got = jnp.stack([pick(pair, lax.rem(z - i + 4, 4)) for i in range(4)])
    return got.reshape((8,) + got.shape[2:])


def fast_small(got, width, rows):
    got = got.astype(f32)
    vecs = got[:, :8, : width // 8].transpose(1, 0, 2).reshape(8, width)
    hb = got[:, 8, : width // 2].reshape(4, width)
    ids = (got[:, 9, :rows] * 32.0 + got[:, 10, :rows]).astype(jnp.int32)
    return vecs, hb, ids


def add(u, v):
    return (u.astype(f32) + v.astype(f32)).astype(bf16)


class Scatter:
    def __init__(self, keep, send):
        b, width = keep.shape[1:]
        self.keep = keep.reshape(4, 4, b, width)
        self.got = core_swap(send).reshape(4, 4, b, width)

    def split(self):
        def part(deltas, half):
            ks = slice(2 * half, 2 * half + 2)
            return jnp.stack([add(self.keep[dl, ks], self.got[dl, ks]) for dl in deltas])

        self.out = [part((1, 3), 0), part((2, 3), 1)]
        self.own = [part((0, 2), 0), part((0, 1), 1)]

    def one(self):
        self.r1 = [x_swap(self.out[0]), y_swap(self.out[1])]

    def add_two(self):
        self.on = [add(self.own[i][1], self.r1[i][1]) for i in range(2)]

    def send_two(self):
        self.r2 = [y_swap(self.on[0]), x_swap(self.on[1])]

    def two(self):
        self.add_two()
        self.send_two()

    def three(self):
        first = [self.own[i][0].astype(f32) + self.r1[i][0].astype(f32) for i in range(2)]
        both_halves = [(first[i] + self.r2[i].astype(f32)).astype(bf16) for i in range(2)]
        self.h3 = [both_halves[k // 2][k % 2] for k in range(4)]
        self.r3 = [self.h3[0]] + [z_shift(self.h3[k], k) for k in (1, 2, 3)]

    def total(self):
        return sum(p.astype(f32) for p in self.r3).astype(bf16)


def spread(mine):
    return [mine, x_swap(mine), y_swap(mine), diagonal_swap(mine)]


def quarters(got, d):
    got = jnp.stack(got)
    return [pick(got, d ^ q).astype(f32) for q in range(4)]


def per_device(
    fast, tokens, timesteps, segments, padding, cotangent, step_table,
    triple_weight, query_bias, value_bias, output_weight, output_bias,
    first_gain, first_shift, second_gain, second_shift,
    hidden_weight, hidden_bias, down_weight, down_bias,
):
    micro, local_rows, length, width = tokens.shape
    rows = micro * local_rows
    n = rows * length
    nd, nf = lax.axis_size("dp"), lax.axis_size("fsdp")
    d, f = lax.axis_index("dp"), lax.axis_index("fsdp")
    z, c = f // 2, lax.rem(f, 2)
    tok = tokens.reshape(n, width)
    cot = cotangent.reshape(n, width)
    seg = segments.reshape(rows, length).astype(f32)
    pad = padding.reshape(rows, length).astype(f32)

    ids = timesteps.reshape(rows)
    steps = lax.iota(jnp.int32, step_table.shape[0])
    q4 = [triple_weight[:, i * width : (i + 1) * width] for i in range(3)] + [output_weight]
    h4 = [hidden_weight[:, i * width : (i + 1) * width] for i in range(4)]
    vec_args = (query_bias, value_bias, output_bias, first_gain, first_shift, second_gain, second_shift, down_bias)
    if fast:
        b = width // NB
        own_a = pick(jnp.stack(q4), d)
        own_b = pick(jnp.stack(h4), d)
        small = jnp.zeros((16, width), bf16)
        small = small.at[:8, : width // nf].set(jnp.stack(vec_args))
        small = small.at[8, : 4 * width // nf].set(hidden_bias)
        small = small.at[9:11, :rows].set(jnp.stack([ids // 32, lax.rem(ids, 32)]).astype(bf16))
        got = along_z(jnp.concatenate([own_a, small], axis=0))
        s0 = rows_of(got, 0, b)
        e0 = rows_of(got, b, 16)
        mine_a = columns(s0)
        got1 = along_z(tie(jnp.concatenate([own_b, down_weight[:b]], axis=0), got))
        vecs, hb, here = fast_small(shard_order(e0, core_swap(e0), z, c), width, rows)
        gpos = [(q ^ d) * 4 + lax.rem(zf - z + 4, 4) for q in range(4) for zf in range(4)] + [c]
        gpos = jnp.stack(gpos).astype(jnp.int32)
        slots = fast_slots(z, c)
        slots_c = down_slots(z, c, ((0,), (1, 2), (3,)))
    else:
        ga, gb, gc, vecs, hb = plain_groups(
            jnp.stack(q4), jnp.stack(h4), down_weight, vec_args + (hidden_bias,)
        )
        gpos = jnp.concatenate([jnp.arange(16, dtype=jnp.int32), jnp.zeros((1,), jnp.int32)])
        here = lax.all_gather(ids, "fsdp", axis=0, tiled=True)

    onehot = (here.reshape(nf * rows)[:, None] == steps[None, :]).astype(bf16)
    looked = jnp.dot(onehot, step_table, preferred_element_type=f32).astype(bf16)
    if fast:
        looked, seg, pad, vecs, hb, gpos, slots, slots_c = lax.optimization_barrier(
            (looked.reshape(rows, width), seg, pad, vecs, hb, gpos, slots, slots_c)
        )
        sent = jnp.pad(looked, ((0, 16 - rows), (0, 0)))
        got_e = jnp.stack(along_z(sent))
        mine_a, got1, got_e = lax.optimization_barrier((mine_a, got1, got_e))
        emb = shard_order(got_e, core_swap(got_e), z, c)[:, :rows].reshape(nf, nf, rows, width // nf)
        emb = pick(emb.transpose(1, 0, 2, 3), f)
    else:
        emb = lax.all_to_all(looked.reshape(nf, rows, width // nf), "fsdp", 0, 0, tiled=True)
    emb = emb.transpose(1, 0, 2).reshape(rows, width).astype(f32)

    if fast:
        flat = (16, b, width)
        mine_a = mine_a.reshape(flat)
        core_a = core_swap(mine_a)
        ga = Group([mine_a, core_a], quarter_major, slots)
        mine_b = columns(rows_of(got1, 0, b))
        c0 = rows_of(got1, b, b)
        got2 = along_z(tie(down_weight[b : 3 * b], got1))
        tok_in = tie(tok, (core_a, emb))
    else:
        tok_in = tok
    normed, triple, att, attended, middle, n2 = compute_f1(tok_in, emb, seg, pad, vecs, ga, rows, length)
    if fast:
        mine_b, n2, got2 = lax.optimization_barrier((mine_b.reshape(flat), n2, got2))
        core_b = core_swap(mine_b)
        gb = Group([mine_b, core_b], quarter_major, slots)
        got3 = along_z(tie(down_weight[3 * b :], got2))
        c12 = jnp.stack(got2).reshape(8, b, width)
        n2, c12 = tie((n2, c12), core_b)
        c0x, c12x = core_swap(c0), core_swap(c12)
    active, gp, keep_c, send_c = compute_f2(n2, cot, hb, gb, gpos)
    if fast:
        got3, c0x, c12x, gp, keep_c, send_c = lax.optimization_barrier((got3, c0x, c12x, gp, keep_c, send_c))
        c3 = jnp.stack(got3)
        gc = Group(
            [c0, c12, c3, c0x, c12x, core_swap(c3)],
            [(0, 0, 4), (1, 0, 8), (2, 0, 4), (3, 0, 4), (4, 0, 8), (5, 0, 4)],
            slots_c,
        )
        sc = Scatter(keep_c, send_c)
        sc.split()
        gp, sc.out = lax.optimization_barrier((gp, sc.out))
        sc.one()
    dh, hb_sum, db_sum, keep_b, send_b = compute_b1(n2, cot, gp, gc, gpos)
    if fast:
        dh, keep_b, send_b, sc.r1 = lax.optimization_barrier((dh, keep_b, send_b, sc.r1))
        sc.two()
        sb = Scatter(keep_b, send_b)
        sb.split()
        dh, sb.out = lax.optimization_barrier((dh, sb.out))
        sb.one()
    part = width // nf
    hb_lanes = hb_sum[:4].reshape(nf, 4 * part)
    marks = jnp.broadcast_to(ids.astype(f32)[None, :], (nf, rows))
    dmid, dbr, dt, sums2 = compute_b2(dh, cot, middle, vecs, triple, att, ga, gb, rows, length)
    if fast:
        dt, sb.r1, sc.r2, hb_lanes, marks = lax.optimization_barrier((dt, sb.r1, sc.r2, hb_lanes, marks))
        sb.two()
        sc.three()
    keep_a, send_a = compute_ga(normed, attended, dt, dbr, gpos)
    if fast:
        keep_a, send_a, sc.r3, sb.r2, dt = lax.optimization_barrier((keep_a, send_a, sc.r3, sb.r2, dt))
        sb.three()
        sa = Scatter(keep_a, send_a)
        sa.split()
        dt, sa.out, active = lax.optimization_barrier((dt, sa.out, active))
        sa.one()
        mine_c = sc.total()
    input_grad, row_sums, sums4 = compute_b4(tok, emb, dmid, dt, vecs, ga, rows, length)
    if fast:
        sa.r1, row_sums, sums4, active, sb.r3, mine_c = lax.optimization_barrier(
            (sa.r1, row_sums, sums4, active, sb.r3, mine_c)
        )
        sa.add_two()
        row_sums, sums4, active = tie((row_sums, sums4, active), sa.on)
        result = compute_f3(active, middle, vecs, gc)

    lines = row_sums.shape[0] + 24
    lanes = jnp.concatenate([row_sums, sums2, sums4, db_sum], axis=0).reshape(lines, nf, part).transpose(1, 0, 2).reshape(nf, lines * part)
    payload = jnp.concatenate([lanes, hb_lanes, marks], axis=1)
    nt, end = rows * part, payload.shape[1] - rows
    if fast:
        sa.send_two()
        everyone = jnp.broadcast_to(payload[None], (nd,) + payload.shape).reshape(nd * nf, payload.shape[1])
        moved = lax.all_to_all(everyone, ("dp", "fsdp"), 0, 0, tiled=True)
        mine_b = sb.total()
        sa.r2, moved, mine_b, mine_c, result = lax.optimization_barrier((sa.r2, moved, mine_b, mine_c, result))
        sa.three()
        mine_b, mine_c = tie((mine_b, mine_c), sa.h3)
        out_bc = columns(jnp.concatenate([mine_b, mine_c], axis=0))
    else:
        moved = lax.all_to_all(payload, "fsdp", 0, 0, tiled=True)
        moved = lax.all_gather(moved, "dp", axis=0, tiled=True)
    table_rows = moved[:, :nt].reshape(nd * nf * rows, part)
    all_ids = moved[:, end:].astype(jnp.int32).reshape(1, nd * nf * rows)
    vec_sums = jnp.sum(moved[:, nt:end], axis=0)
    if not fast:
        result = compute_f3(active, middle, vecs, gc)
    if fast:
        sa.r3, out_bc, moved = lax.optimization_barrier((sa.r3, out_bc, moved))
        out_a = quarters(spread(sa.total()), d)
        out_b = out_bc[:, :b].astype(f32)
        down_grad = out_bc[:, b:].astype(f32).reshape(4 * b, width)
    else:
        out_b = plain_scatter(keep_b, send_b, False)
        out_a = plain_scatter(keep_a, send_a, False)
        down_grad = plain_scatter(keep_c, send_c, True)
    hidden_grad = jnp.concatenate([out_b[i] for i in range(4)], axis=1)
    triple_grad = jnp.concatenate([out_a[i] for i in range(3)], axis=1)
    output_grad = out_a[3]
    all_hot = (steps[:, None] == all_ids).astype(f32)
    table_grad = jnp.dot(all_hot, table_rows, precision=highest)
    kept = vec_sums[(lines - 24 - rows) * part : (lines - rows) * part].reshape(24, part)
    v = [kept[i] for i in (3, 4, 2, 8, 9, 0, 1, 16)]
    hidden_bias_grad = vec_sums[(lines - rows) * part :]
    shape = tokens.shape
    return (
        result.reshape(shape), input_grad.reshape(shape), table_grad, triple_grad, v[0], v[1], output_grad, v[2],
        v[3], v[4], v[5], v[6], hidden_grad, hidden_bias_grad, down_grad, v[7],
    )


def solution(mesh):
    fast = mesh.shape["dp"] == 4 and mesh.shape["fsdp"] == 8
    batch = ("dp", "fsdp")
    vec, mat, tab = P("fsdp"), P("fsdp", None), P(None, "fsdp")
    tokens_spec = P(None, batch, None, None)
    return jax.shard_map(
        functools.partial(per_device, fast),
        mesh=mesh,
        in_specs=(
            tokens_spec, P(None, batch), P(None, batch, None), P(None, batch, None), tokens_spec,
            tab, mat, vec, vec, mat, vec, vec, vec, vec, vec, mat, vec, mat, vec,
        ),
        out_specs=(
            tokens_spec, tokens_spec, tab, mat, vec, vec, mat, vec, vec, vec, vec, vec, mat, vec, mat, vec,
        ),
        check_vma=False,
    )
```

```python
import functools
import math

import jax
import jax.numpy as jnp
from jax import lax
from jax.experimental import pallas as pl
from jax.experimental.pallas import tpu as pltpu
from jax.sharding import PartitionSpec as P

HEADS = 12
HD = 64
EPS = 1e-05
MASKED = -1e30
SCALE = 1.0 / math.sqrt(HD)
GELU_C = math.sqrt(2.0 / math.pi)
GELU_A = 0.044715
VMEM_LIMIT = 55 * 1024 * 1024
highest = lax.Precision.HIGHEST
f32 = jnp.float32
bf16 = jnp.bfloat16

NB = 8


def mm(a, b):
    return lax.dot_general(a, b, (((1,), (0,)), ((), ())), preferred_element_type=f32)


def mm_nt(a, b):
    return lax.dot_general(a, b, (((1,), (1,)), ((), ())), preferred_element_type=f32)


def mm_tn(a, b):
    return lax.dot_general(a, b, (((0,), (0,)), ((), ())), preferred_element_type=f32)


def moments(v):
    average = jnp.mean(v, axis=-1, keepdims=True)
    centered = v - average
    variance = jnp.mean(centered * centered, axis=-1, keepdims=True)
    inv = lax.rsqrt(variance + EPS)
    return centered * inv, inv


def ln_back(e, xhat, inv):
    return (e - jnp.mean(e, -1, keepdims=True) - xhat * jnp.mean(e * xhat, -1, keepdims=True)) * inv


def start_blocks(slots_ref, pieces, layout, w_ref, sem, low=None):
    i = 0
    for piece, first, count in layout:
        for t in range(count):
            slot = slots_ref[i]
            if low is None:
                pltpu.make_async_copy(pieces[piece].at[first + t], w_ref.at[slot], sem.at[slot]).start()
            else:

                @pl.when(slot >= low)
                def _(piece=piece, at=first + t, slot=slot):
                    place = slot - low
                    pltpu.make_async_copy(pieces[piece].at[at], w_ref.at[place], sem.at[place]).start()

            i += 1


def wait_blocks(w_ref, sem, first, count):
    def one(t, carry):
        pltpu.make_async_copy(w_ref.at[first + t], w_ref.at[first + t], sem.at[first + t]).wait()
        return carry

    lax.fori_loop(0, count, one, 0)


def load_blocks(slots_ref, pieces, layout, w_ref, sem):
    start_blocks(slots_ref, pieces, layout, w_ref, sem)
    wait_blocks(w_ref, sem, 0, 32)


def square(w_ref, j):
    part = w_ref[NB * j : NB * (j + 1)]
    return part.reshape(part.shape[0] * part.shape[1], part.shape[2])


def send_blocks(gpos_ref, spots, buf_ref, even_rows, odd_rows, b, outs, sem):
    core = gpos_ref[16]
    keep_out, keep_own, send_out, send_own = outs
    for t, at in enumerate(spots):
        place = gpos_ref[at]
        idx = lax.rem(place, 8)
        for parity, row in ((0, even_rows[t]), (1, odd_rows[t])):
            for kept in (True, False):
                for low in (True, False):
                    ref = (keep_out if low else keep_own) if kept else (send_out if low else send_own)
                    mine = (core == parity) if kept else (core != parity)
                    region = (place < 8) if low else (place >= 8)

                    @pl.when(mine & region)
                    def _(ref=ref, row=row, idx=idx, which=2 * t + parity):
                        pltpu.make_async_copy(buf_ref.at[pl.ds(row, b)], ref.at[idx], sem.at[which]).start()


def drain_blocks(buf_ref, b, sem):
    for t in range(8):
        pltpu.make_async_copy(buf_ref.at[pl.ds(0, b)], buf_ref.at[pl.ds(0, b)], sem.at[t]).wait()


def half_mask(rows, width):
    lane = lax.broadcasted_iota(jnp.int32, (rows, width), 1)
    return lane < HD


def both(x2, first):
    zero = jnp.zeros_like(x2)
    return jnp.concatenate([jnp.where(first, x2, zero), jnp.where(first, zero, x2)], axis=0)


def residual_of(tok_ref, emb_ref, step, rb, length):
    parts = []
    for r in range(rb):
        rows = tok_ref[r * length : (r + 1) * length].astype(f32)
        parts.append(rows + emb_ref[pl.ds(step * rb + r, 1), :])
    return jnp.concatenate(parts, axis=0) if rb > 1 else parts[0]


def f1_kernel(layout, rb, length, slots, tok_ref, emb_ref, seg_ref, pad_ref, vec_ref, *rest):
    n = max(l[0] for l in layout) + 1
    pieces = rest[:n]
    normed_ref, triple_ref, att_ref, attended_ref, middle_ref, n2_ref, w_ref, sem = rest[n:]
    step = pl.program_id(0)

    @pl.when(step == 0)
    def _():
        load_blocks(slots, pieces, layout, w_ref, sem)

    x = residual_of(tok_ref, emb_ref, step, rb, length)
    xhat, _inv = moments(x)
    normed = (xhat * vec_ref[3:4, :] + vec_ref[4:5, :]).astype(bf16)
    normed_ref[...] = normed
    width = normed.shape[1]
    for q, row in ((0, 0), (1, None), (2, 1)):
        t = mm(normed, square(w_ref, q))
        if row is not None:
            t = t + vec_ref[row : row + 1, :]
        triple_ref[q] = t.astype(bf16)
    eye = lax.broadcasted_iota(jnp.int32, (length, length), 0) == lax.broadcasted_iota(
        jnp.int32, (length, length), 1
    )
    first = half_mask(length, 2 * HD)
    masks = []
    for r in range(rb):
        seg = jnp.broadcast_to(seg_ref[pl.ds(step * rb + r, 1), :], (length, length))
        pad = jnp.broadcast_to(pad_ref[pl.ds(step * rb + r, 1), :], (length, length))
        allowed = (seg == seg.T) & ((pad == 0.0) | eye)
        allowed = jnp.where(allowed, 1.0, 0.0)
        masks.append(jnp.concatenate([allowed, allowed], axis=0) > 0.5)
    pairs = width // (2 * HD)
    every = [(r, hp) for r in range(rb) for hp in range(pairs)]
    for start in range(0, len(every), 12):
        some = []
        for r, hp in every[start : start + 12]:
            rows = slice(r * length, (r + 1) * length)
            lanes = slice(hp * 2 * HD, (hp + 1) * 2 * HD)
            s = mm_nt(both(triple_ref[0, rows, lanes], first), triple_ref[1, rows, lanes]) * SCALE
            some.append((r, hp, rows, lanes, jnp.where(masks[r], s, MASKED)))
        done = []
        for r, hp, rows, lanes, s in some:
            e = jnp.exp(s - jnp.max(s, axis=-1, keepdims=True))
            p = (e / jnp.sum(e, axis=-1, keepdims=True)).astype(bf16)
            att_ref[r * pairs + hp] = p
            done.append((rows, lanes, p))
        for rows, lanes, p in done:
            wide = jnp.concatenate([p[:length], p[length:]], axis=1)
            attended_ref[rows, lanes] = mm(wide, both(triple_ref[2, rows, lanes], first)).astype(bf16)
    branch = mm(attended_ref[...], square(w_ref, 3)) + vec_ref[2:3, :]
    middle = x + branch
    middle_ref[...] = middle
    xhat2, _inv2 = moments(middle)
    n2_ref[...] = (xhat2 * vec_ref[5:6, :] + vec_ref[6:7, :]).astype(bf16)


def gelu_rows(h_ref, bias, active_ref, gp_ref, first, count):
    sub = 32
    for m in range(count // sub):
        at = slice(first + m * sub, first + (m + 1) * sub)
        v = h_ref[at] + bias
        v2 = v * v
        w = GELU_C * v
        cubic = w * v2
        t = jnp.tanh(w + cubic * GELU_A)
        half = 0.5 * t + 0.5
        active_ref[at] = (v * half).astype(bf16)
        steep = w + cubic * (3.0 * GELU_A)
        gp_ref[at] = (half + (half - half * t) * steep).astype(bf16)


def f2_kernel(layout, slots, gpos, n2_ref, cot_hbm, hb_ref, *rest):
    n = max(l[0] for l in layout) + 1
    pieces = rest[:n]
    active_ref, gp_ref = rest[n : n + 2]
    outs = rest[n + 2 : n + 6]
    w_ref, h_ref, g_ref, cot_ref, sem, cot_sem, out_sem = rest[n + 6 :]
    j = pl.program_id(0)
    load = pltpu.make_async_copy(cot_hbm, cot_ref, cot_sem)

    @pl.when(j == 0)
    def _():
        start_blocks(slots, pieces, layout, w_ref, sem)
        load.start()

    wait_blocks(w_ref, sem, j * NB, NB)
    tokens, width = n2_ref.shape
    b = width // NB
    bias = hb_ref[pl.ds(j, 1), :]
    slot = lax.rem(j, 2)

    @pl.when(j >= 2)
    def _():
        drain_blocks(g_ref.at[slot], b, out_sem.at[slot])

    part = w_ref[pl.ds(j * NB, NB)].reshape(width, width)
    half = tokens // 2
    h_ref[:half] = mm(n2_ref[:half], part)
    h_ref[half:] = mm(n2_ref[half:], part)
    gelu_rows(h_ref, bias, active_ref, gp_ref, 0, half)
    gelu_rows(h_ref, bias, active_ref, gp_ref, half, half)

    @pl.when(j == 0)
    def _():
        load.wait()

    g_ref[slot] = mm_tn(active_ref[...], cot_ref[...]).astype(bf16)
    spots = [q * 4 + j for q in range(4)]
    even_rows, odd_rows = [q * b for q in range(4)], [(4 + q) * b for q in range(4)]
    send_blocks(gpos, spots, g_ref.at[slot], even_rows, odd_rows, b, outs, out_sem.at[slot])

    @pl.when(j == 3)
    def _():
        drain_blocks(g_ref.at[0], b, out_sem.at[0])
        drain_blocks(g_ref.at[1], b, out_sem.at[1])


def b1_kernel(layout, chunk, slots, gpos, n2_ref, cot_ref, gp_ref, *rest):
    n = max(l[0] for l in layout) + 1
    pieces = rest[:n]
    dh_ref, hb_ref, db_ref = rest[n : n + 3]
    outs = rest[n + 3 : n + 7]
    w_ref, h_ref, g_ref, sem, out_sem = rest[n + 7 :]
    j = pl.program_id(0)
    tokens, width = n2_ref.shape
    b = width // NB
    slot = lax.rem(j, 2)

    @pl.when(j == 0)
    def _():
        start_blocks(slots, pieces, layout, w_ref, sem)
        db_ref[...] = jnp.zeros_like(db_ref)
        db_ref[0:1] = jnp.sum(cot_ref[...].astype(f32), axis=0, keepdims=True)
        hb_ref[...] = jnp.zeros_like(hb_ref)

    wait_blocks(w_ref, sem, j * NB, NB)
    w = w_ref[pl.ds(j * NB, NB)].reshape(width, width)
    sub = 32
    total = jnp.zeros((8, width), f32)
    for m in range(tokens // chunk):
        h_ref[m] = mm_nt(cot_ref[m * chunk : (m + 1) * chunk], w)
    for m in range(tokens // chunk):
        for s in range(chunk // sub):
            at = slice(m * chunk + s * sub, m * chunk + (s + 1) * sub)
            dh = (h_ref[m, s * sub : (s + 1) * sub] * gp_ref[at].astype(f32)).astype(bf16)
            dh_ref[at] = dh
            total = total + jnp.sum(dh.astype(f32).reshape(sub // 8, 8, width), axis=0)
    hb_ref[pl.ds(j, 1), :] = jnp.sum(total, axis=0, keepdims=True)

    @pl.when(j >= 2)
    def _():
        drain_blocks(g_ref.at[slot], b, out_sem.at[slot])

    g_ref[slot] = mm_tn(n2_ref[...], dh_ref[...]).astype(bf16)
    spots = [j * 4 + zf for zf in range(4)]
    even_rows, odd_rows = [2 * zf * b for zf in range(4)], [(2 * zf + 1) * b for zf in range(4)]
    send_blocks(gpos, spots, g_ref.at[slot], even_rows, odd_rows, b, outs, out_sem.at[slot])

    @pl.when(j == 3)
    def _():
        drain_blocks(g_ref.at[0], b, out_sem.at[0])
        drain_blocks(g_ref.at[1], b, out_sem.at[1])


def b2_kernel(
    layout_a, layout_b, rb, length, slots_a, slots_b,
    dh_ref, cot_ref, middle_ref, vec_ref, triple_ref, att_ref, *rest
):
    na = max(l[0] for l in layout_a) + 1
    nb = max(l[0] for l in layout_b) + 1
    pieces_a, pieces_b, rest = rest[:na], rest[na : na + nb], rest[na + nb :]
    dmid_ref, dbr_ref, dt_ref, sums_ref, wo_ref, wb_ref, datt_ref, sem_a, sem_b = rest
    width = cot_ref.shape[1]
    b = width // NB

    @pl.when(pl.program_id(0) == 0)
    def _():
        start_blocks(slots_b, pieces_b, layout_b, wb_ref, sem_b)
        start_blocks(slots_a, pieces_a, layout_a, wo_ref, sem_a, 3 * NB)
        sums_ref[...] = jnp.zeros_like(sums_ref)
        wait_blocks(wb_ref, sem_b, 0, 32)
        wait_blocks(wo_ref, sem_a, 0, NB)

    def slope(j):
        return mm_nt(dh_ref[:, j * width : (j + 1) * width], square(wb_ref, j))

    d_n2 = slope(0)
    for j in range(1, 4):
        d_n2 = d_n2 + slope(j)
    xhat, inv = moments(middle_ref[...])
    sums_ref[0:1] += jnp.sum(d_n2 * xhat, axis=0, keepdims=True)
    sums_ref[1:2] += jnp.sum(d_n2, axis=0, keepdims=True)
    d_middle = cot_ref[...].astype(f32) + ln_back(d_n2 * vec_ref[5:6, :], xhat, inv)
    dmid_ref[...] = d_middle
    d_branch = d_middle.astype(bf16)
    dbr_ref[...] = d_branch
    sums_ref[2:3] += jnp.sum(d_branch.astype(f32), axis=0, keepdims=True)

    datt_ref[...] = mm_nt(d_branch, wo_ref[...].reshape(width, width)).astype(bf16)
    first = half_mask(length, 2 * HD)
    pairs = width // (2 * HD)
    every = [(r, hp) for r in range(rb) for hp in range(pairs)]
    for start in range(0, len(every), 6):
        some = []
        for r, hp in every[start : start + 6]:
            rows = slice(r * length, (r + 1) * length)
            lanes = slice(hp * 2 * HD, (hp + 1) * 2 * HD)
            dos = both(datt_ref[rows, lanes], first)
            some.append((rows, lanes, dos, att_ref[r * pairs + hp], mm_nt(dos, triple_ref[2, rows, lanes])))
        slopes = []
        for rows, lanes, dos, p_low, d_a in some:
            dt_ref[2, rows, lanes] = mm_tn(p_low, dos).astype(bf16)
            p = p_low.astype(f32)
            inner = jnp.sum(p * d_a, axis=-1, keepdims=True)
            slopes.append((p * (d_a - inner)).astype(bf16))
        for (rows, lanes, dos, p_low, d_a), ds in zip(some, slopes):
            wide = jnp.concatenate([ds[:length], ds[length:]], axis=1)
            dt_ref[0, rows, lanes] = (mm(wide, both(triple_ref[1, rows, lanes], first)) * SCALE).astype(bf16)
            dt_ref[1, rows, lanes] = (mm_tn(ds, both(triple_ref[0, rows, lanes], first)) * SCALE).astype(bf16)
    sums_ref[3:4] += jnp.sum(dt_ref[0].astype(f32), axis=0, keepdims=True)
    sums_ref[4:5] += jnp.sum(dt_ref[2].astype(f32), axis=0, keepdims=True)


def ga_kernel(gpos, normed_ref, dt_ref, attended_hbm, dbr_hbm, *rest):
    outs = rest[:4]
    attended_ref, dbr_ref, g_ref, in_sem, out_sem = rest[4:]
    j = pl.program_id(0)
    width = normed_ref.shape[1]
    b = width // NB
    slot = lax.rem(j, 2)
    loads = [
        pltpu.make_async_copy(attended_hbm, attended_ref, in_sem.at[0]),
        pltpu.make_async_copy(dbr_hbm, dbr_ref, in_sem.at[1]),
    ]

    @pl.when(j == 0)
    def _():
        for cp in loads:
            cp.start()

    @pl.when(j >= 2)
    def _():
        drain_blocks(g_ref.at[slot], b, out_sem.at[slot])

    @pl.when(j < 3)
    def _():
        g_ref[slot] = mm_tn(normed_ref[...], dt_ref[...]).astype(bf16)

    @pl.when(j == 3)
    def _():
        for cp in loads:
            cp.wait()
        g_ref[slot] = mm_tn(attended_ref[...], dbr_ref[...]).astype(bf16)

    spots = [j * 4 + zf for zf in range(4)]
    even_rows, odd_rows = [2 * zf * b for zf in range(4)], [(2 * zf + 1) * b for zf in range(4)]
    send_blocks(gpos, spots, g_ref.at[slot], even_rows, odd_rows, b, outs, out_sem.at[slot])

    @pl.when(j == 3)
    def _():
        drain_blocks(g_ref.at[0], b, out_sem.at[0])
        drain_blocks(g_ref.at[1], b, out_sem.at[1])


def b4_kernel(layout, rb, length, slots, tok_ref, emb_ref, dmid_ref, dt_ref, vec_ref, sums2_ref, db_ref, *rest):
    n = max(l[0] for l in layout) + 1
    pieces = rest[:n]
    ig_ref, sums_ref, w_ref, sem = rest[n:]
    base = pl.num_programs(0) * rb
    step = pl.program_id(0)

    @pl.when(step == 0)
    def _():
        load_blocks(slots, pieces, layout, w_ref, sem)
        sums_ref[...] = jnp.zeros_like(sums_ref)
        sums_ref[pl.ds(base + 2, 5)] = sums2_ref[0:5]
        sums_ref[pl.ds(base + 7, 1)] = db_ref[0:1]

    d_n = mm_nt(dt_ref[0], square(w_ref, 0))
    for q in range(1, 3):
        d_n = d_n + mm_nt(dt_ref[q], square(w_ref, q))
    xhat, inv = moments(residual_of(tok_ref, emb_ref, step, rb, length))
    sums_ref[pl.ds(base, 1)] += jnp.sum(d_n * xhat, axis=0, keepdims=True)
    sums_ref[pl.ds(base + 1, 1)] += jnp.sum(d_n, axis=0, keepdims=True)
    d_start = dmid_ref[...] + ln_back(d_n * vec_ref[3:4, :], xhat, inv)
    ig_ref[...] = d_start.astype(bf16)
    for r in range(rb):
        sums_ref[pl.ds(step * rb + r, 1), :] = jnp.sum(d_start[r * length : (r + 1) * length], axis=0, keepdims=True)


def f3_kernel(layout, slots, act_ref, middle_ref, vec_ref, *rest):
    n = max(l[0] for l in layout) + 1
    pieces = rest[:n]
    out_ref, w_ref, sem = rest[n:]

    @pl.when(pl.program_id(0) == 0)
    def _():
        load_blocks(slots, pieces, layout, w_ref, sem)

    width = middle_ref.shape[1]
    acc = mm(act_ref[...], w_ref[...].reshape(4 * width, width))
    out_ref[...] = (middle_ref[...] + (acc + vec_ref[7:8, :])).astype(bf16)


def sds(shape, dtype):
    return jax.ShapeDtypeStruct(shape, dtype)


def full(shape):
    zeros = (0,) * len(shape)
    return pl.BlockSpec(shape, lambda i: zeros)


smem = pl.BlockSpec(memory_space=pltpu.SMEM)
hbm = pl.BlockSpec(memory_space=pl.ANY)


def call(kernel, grid, in_specs, out_shape, out_specs, scratch, flops, nbytes, args):
    return pl.pallas_call(
        kernel,
        grid=grid,
        in_specs=in_specs,
        out_shape=out_shape,
        out_specs=out_specs,
        scratch_shapes=scratch,
        compiler_params=pltpu.CompilerParams(
            dimension_semantics=("arbitrary",), vmem_limit_bytes=VMEM_LIMIT
        ),
        cost_estimate=pl.CostEstimate(flops=flops, bytes_accessed=nbytes, transcendentals=0),
    )(*args)


class Group:
    def __init__(self, arrays, layout, slots):
        self.arrays, self.layout, self.slots = arrays, layout, slots


def compute_f1(tok, emb, seg, pad, vecs, group, rows, length):
    n, width = tok.shape
    rb = 2 if rows % 2 == 0 else 1
    block = rb * length
    pairs = width // (2 * HD)
    b = width // NB
    return call(
        functools.partial(f1_kernel, group.layout, rb, length),
        (rows // rb,),
        [smem, pl.BlockSpec((block, width), lambda i: (i, 0)), full(emb.shape), full(seg.shape), full(pad.shape), full(vecs.shape)]
        + [hbm] * len(group.arrays),
        [sds((n, width), bf16), sds((3, n, width), bf16), sds((rows * pairs, 2 * length, length), bf16),
         sds((n, width), bf16), sds((n, width), f32), sds((n, width), bf16)],
        [pl.BlockSpec((block, width), lambda i: (i, 0)), pl.BlockSpec((3, block, width), lambda i: (0, i, 0)),
         pl.BlockSpec((rb * pairs, 2 * length, length), lambda i: (i, 0, 0)),
         pl.BlockSpec((block, width), lambda i: (i, 0)), pl.BlockSpec((block, width), lambda i: (i, 0)),
         pl.BlockSpec((block, width), lambda i: (i, 0))],
        [pltpu.VMEM((32, b, width), bf16), pltpu.SemaphoreType.DMA((32,))],
        2 * n * width * width * 4 * 3, 20 << 20,
        [group.slots, tok, emb, seg, pad, vecs, *group.arrays],
    )


def compute_f2(n2, cot, hb, group, gpos):
    n, width = n2.shape
    b = width // NB
    column = pl.BlockSpec((n, width), lambda i: (0, i))
    return call(
        functools.partial(f2_kernel, group.layout),
        (4,),
        [smem, smem, full(n2.shape), hbm, full(hb.shape)] + [hbm] * len(group.arrays),
        [sds((n, 4 * width), bf16), sds((n, 4 * width), bf16), *[sds((8, b, width), bf16)] * 4],
        [column, column, hbm, hbm, hbm, hbm],
        [pltpu.VMEM((32, b, width), bf16), pltpu.VMEM((n, width), f32), pltpu.VMEM((2, width, width), bf16), pltpu.VMEM((n, width), bf16),
         pltpu.SemaphoreType.DMA((32,)), pltpu.SemaphoreType.DMA(()), pltpu.SemaphoreType.DMA((2, 8))],
        2 * n * width * width * 8 * 2, 20 << 20,
        [group.slots, gpos, n2, cot, hb, *group.arrays],
    )


def compute_b1(n2, cot, gp, group, gpos):
    n, width = n2.shape
    b = width // NB
    chunk = 256 if n % 256 == 0 else n
    column = pl.BlockSpec((n, width), lambda i: (0, i))
    return call(
        functools.partial(b1_kernel, group.layout, chunk),
        (4,),
        [smem, smem, full(n2.shape), full(cot.shape), column] + [hbm] * len(group.arrays),
        [sds((n, 4 * width), bf16), sds((4, width), f32), sds((8, width), f32), *[sds((8, b, width), bf16)] * 4],
        [column, full((4, width)), full((8, width)), hbm, hbm, hbm, hbm],
        [pltpu.VMEM((32, b, width), bf16), pltpu.VMEM((n // chunk, chunk, width), f32), pltpu.VMEM((2, width, width), bf16),
         pltpu.SemaphoreType.DMA((32,)), pltpu.SemaphoreType.DMA((2, 8))],
        2 * n * width * width * 8 * 2, 20 << 20,
        [group.slots, gpos, n2, cot, gp, *group.arrays],
    )


def compute_b2(dh, cot, middle, vecs, triple, att, ga, gb, rows, length):
    n, width = cot.shape
    rb = 2 if rows % 2 == 0 else 1
    block = rb * length
    pairs = width // (2 * HD)
    b = width // NB
    tile = pl.BlockSpec((block, width), lambda i: (i, 0))
    wide = pl.BlockSpec((3, block, width), lambda i: (0, i, 0))
    return call(
        functools.partial(b2_kernel, ga.layout, gb.layout, rb, length),
        (rows // rb,),
        [smem, smem, pl.BlockSpec((block, 4 * width), lambda i: (i, 0)), tile, tile, full(vecs.shape), wide,
         pl.BlockSpec((rb * pairs, 2 * length, length), lambda i: (i, 0, 0))]
        + [hbm] * (len(ga.arrays) + len(gb.arrays)),
        [sds((n, width), f32), sds((n, width), bf16), sds((3, n, width), bf16), sds((8, width), f32)],
        [tile, tile, wide, full((8, width))],
        [pltpu.VMEM((NB, b, width), bf16), pltpu.VMEM((32, b, width), bf16), pltpu.VMEM((block, width), bf16),
         pltpu.SemaphoreType.DMA((NB,)), pltpu.SemaphoreType.DMA((32,))],
        2 * n * width * width * 10, 30 << 20,
        [ga.slots, gb.slots, dh, cot, middle, vecs, triple, att, *ga.arrays, *gb.arrays],
    )


def compute_ga(normed, attended, dt, dbr, gpos):
    n, width = normed.shape
    b = width // NB
    return call(
        ga_kernel,
        (4,),
        [smem, full(normed.shape), pl.BlockSpec((None, n, width), lambda i: (jnp.minimum(i, 2), 0, 0)), hbm, hbm],
        [*[sds((8, b, width), bf16)] * 4],
        [hbm, hbm, hbm, hbm],
        [pltpu.VMEM((n, width), bf16), pltpu.VMEM((n, width), bf16), pltpu.VMEM((2, width, width), bf16),
         pltpu.SemaphoreType.DMA((2,)), pltpu.SemaphoreType.DMA((2, 8))],
        2 * n * width * width * 4 * 2, 12 << 20,
        [gpos, normed, dt, attended, dbr],
    )


def compute_b4(tok, emb, dmid, dt, vecs, sums2, db_sum, group, rows, length):
    n, width = tok.shape
    rb = 2 if rows % 2 == 0 else 1
    block = rb * length
    b = width // NB
    lines = 8 * ((rows + 8 + 7) // 8)
    return call(
        functools.partial(b4_kernel, group.layout, rb, length),
        (rows // rb,),
        [smem, pl.BlockSpec((block, width), lambda i: (i, 0)), full(emb.shape), pl.BlockSpec((block, width), lambda i: (i, 0)),
         pl.BlockSpec((3, block, width), lambda i: (0, i, 0)), full(vecs.shape), full(sums2.shape), full(db_sum.shape)]
        + [hbm] * len(group.arrays),
        [sds((n, width), bf16), sds((lines, width), f32)],
        [pl.BlockSpec((block, width), lambda i: (i, 0)), full((lines, width))],
        [pltpu.VMEM((32, b, width), bf16), pltpu.SemaphoreType.DMA((32,))],
        2 * n * width * width * 3 * 2, 12 << 20,
        [group.slots, tok, emb, dmid, dt, vecs, sums2, db_sum, *group.arrays],
    )


def compute_f3(active, middle, vecs, group):
    n, width = middle.shape
    b = width // NB
    block = 256 if n % 256 == 0 else n
    return call(
        functools.partial(f3_kernel, group.layout),
        (n // block,),
        [smem, pl.BlockSpec((block, 4 * width), lambda i: (i, 0)), pl.BlockSpec((block, width), lambda i: (i, 0)), full(vecs.shape)]
        + [hbm] * len(group.arrays),
        sds((n, width), bf16),
        pl.BlockSpec((block, width), lambda i: (i, 0)),
        [pltpu.VMEM((32, b, width), bf16), pltpu.SemaphoreType.DMA((32,))],
        2 * n * width * width * 4 * 2, 12 << 20,
        [group.slots, active, middle, vecs, *group.arrays],
    )


def plain_groups(own_a, own_b, own_c, small):
    width = own_a.shape[2]
    slots = jnp.arange(32, dtype=jnp.int32)

    def group(whole):
        return Group([whole.reshape(32, width // NB, width)], [(0, 0, 32)], slots)

    a = lax.all_gather(own_a, "fsdp", axis=1, tiled=True)
    b = lax.all_gather(own_b, "fsdp", axis=1, tiled=True)
    c = lax.all_gather(own_c, "fsdp", axis=0, tiled=True)
    vec = [lax.all_gather(v, "fsdp", axis=0, tiled=True) for v in small]
    return group(a), group(b), group(c), jnp.stack(vec[:8]).astype(f32), vec[8].astype(f32).reshape(4, width)


def plain_scatter(keep_out, keep_own, send_out, send_own, rows_first=False):
    b, width = keep_out.shape[1:]
    g = [jnp.concatenate(v, axis=0).reshape(4, 4, b, width) for v in ((keep_out, keep_own), (send_out, send_own))]
    g = jnp.stack(g, axis=2).astype(f32)
    if rows_first:
        g = g.transpose(1, 2, 0, 3, 4).reshape(32 * b, width)
        return lax.psum(lax.psum_scatter(g, "fsdp", scatter_dimension=0, tiled=True), "dp")
    g = g.reshape(4, NB * b, width)
    return lax.psum(lax.psum_scatter(g, "fsdp", scatter_dimension=1, tiled=True), "dp")


def pick(stacked, i):
    return lax.dynamic_index_in_dim(stacked, i, axis=0, keepdims=False)


def xor_perm(n, k):
    return [(i, i ^ k) for i in range(n)]


def core_swap(v):
    return lax.ppermute(v, "fsdp", xor_perm(8, 1))


def x_swap(v):
    return lax.ppermute(v, "dp", xor_perm(4, 1))


def y_swap(v):
    return lax.ppermute(v, "dp", xor_perm(4, 2))


def diagonal_swap(v):
    return lax.ppermute(v, "dp", xor_perm(4, 3))


def z_shift(v, k):
    return lax.ppermute(v, "fsdp", [(i, (i + 2 * k) % 8) for i in range(8)])


def tie(values, after):
    return lax.optimization_barrier((values, after))[0]


def columns(v):
    return lax.all_to_all(jnp.broadcast_to(v[None], (4,) + v.shape), "dp", 0, 0, tiled=True)


quarter_major = [(e, 4 * q, 4) for q in range(4) for e in (0, 1)]


def grad_place(delta, k):
    half, high, low = k // 2, delta // 2, lax.rem(delta, 2)
    leaves, other = jnp.where(half == 0, low, high), jnp.where(half == 0, high, low)
    return (1 - leaves) * 8 + half * 4 + other * 2 + lax.rem(k, 2)


def fast_slots(z, c):
    table = []
    for q in range(4):
        for e in (0, 1):
            for k in range(4):
                table.append(q * NB + 2 * lax.rem(z - k + 4, 4) + (c ^ e))
    return jnp.stack(table).astype(jnp.int32)


def along_z(v):
    return [v] + [z_shift(v, k) for k in (1, 2, 3)]


def rows_of(got, first, count):
    return jnp.stack([g[first : first + count] for g in got])


def down_slots(z, c, quarters_in):
    table = []
    for e in (0, 1):
        for part in quarters_in:
            for k in range(4):
                table += [8 * lax.rem(z - k + 4, 4) + 4 * (c ^ e) + q for q in part]
    return jnp.stack(table).astype(jnp.int32)


def shard_order(e0, e1, z, c):
    pair = jnp.stack([jnp.where(c == 0, e0, e1), jnp.where(c == 0, e1, e0)], axis=1)
    got = jnp.stack([pick(pair, lax.rem(z - i + 4, 4)) for i in range(4)])
    return got.reshape((8,) + got.shape[2:])


def fast_small(got, width, rows):
    got = got.astype(f32)
    vecs = got[:, :8, : width // 8].transpose(1, 0, 2).reshape(8, width)
    hb = got[:, 8, : width // 2].reshape(4, width)
    ids = (got[:, 9, :rows] * 32.0 + got[:, 10, :rows]).astype(jnp.int32)
    return vecs, hb, ids


def plus(*values):
    return sum(v.astype(f32) for v in values).astype(bf16)


class Scatter:
    def __init__(self, keep_out, keep_own, send_out, send_own):
        self.keep = (keep_out, keep_own)
        self.got = (core_swap(send_out), core_swap(send_own))

    def split(self):
        self.out = [plus(self.keep[0][4 * i : 4 * i + 4], self.got[0][4 * i : 4 * i + 4]) for i in range(2)]

    def one(self):
        self.r1 = [x_swap(self.out[0]), y_swap(self.out[1])]

    def add_two(self):
        at = [slice(4 * i + 2, 4 * i + 4) for i in range(2)]
        self.on = [plus(self.keep[1][at[i]], self.got[1][at[i]], self.r1[i][2:]) for i in range(2)]

    def send_two(self):
        self.r2 = [y_swap(self.on[0]), x_swap(self.on[1])]

    def two(self):
        self.add_two()
        self.send_two()

    def three(self):
        at = [slice(4 * i, 4 * i + 2) for i in range(2)]
        halves = [plus(self.keep[1][at[i]], self.got[1][at[i]], self.r1[i][:2], self.r2[i]) for i in range(2)]
        self.h3 = [halves[k // 2][k % 2] for k in range(4)]
        self.r3 = [self.h3[0]] + [z_shift(self.h3[k], k) for k in (1, 2, 3)]

    def total(self):
        return sum(p.astype(f32) for p in self.r3).astype(bf16)


def spread(mine):
    return [mine, x_swap(mine), y_swap(mine), diagonal_swap(mine)]


def quarters(got, d):
    got = jnp.stack(got)
    return [pick(got, d ^ q).astype(f32) for q in range(4)]


def per_device(
    fast, tokens, timesteps, segments, padding, cotangent, step_table,
    triple_weight, query_bias, value_bias, output_weight, output_bias,
    first_gain, first_shift, second_gain, second_shift,
    hidden_weight, hidden_bias, down_weight, down_bias,
):
    micro, local_rows, length, width = tokens.shape
    rows = micro * local_rows
    n = rows * length
    nd, nf = lax.axis_size("dp"), lax.axis_size("fsdp")
    d, f = lax.axis_index("dp"), lax.axis_index("fsdp")
    z, c = f // 2, lax.rem(f, 2)
    tok = tokens.reshape(n, width)
    cot = cotangent.reshape(n, width)
    seg = segments.reshape(rows, length).astype(f32)
    pad = padding.reshape(rows, length).astype(f32)

    ids = timesteps.reshape(rows)
    marks = jnp.broadcast_to(ids.astype(f32)[None, :], (nf, rows))
    steps = lax.iota(jnp.int32, step_table.shape[0])
    q4 = [triple_weight[:, i * width : (i + 1) * width] for i in range(3)] + [output_weight]
    h4 = [hidden_weight[:, i * width : (i + 1) * width] for i in range(4)]
    vec_args = (query_bias, value_bias, output_bias, first_gain, first_shift, second_gain, second_shift, down_bias)
    if fast:
        b = width // NB
        own_a = pick(jnp.stack(q4), d)
        own_b = pick(jnp.stack(h4), d)
        small = jnp.zeros((16, width), bf16)
        small = small.at[:8, : width // nf].set(jnp.stack(vec_args))
        small = small.at[8, : 4 * width // nf].set(hidden_bias)
        small = small.at[9:11, :rows].set(jnp.stack([ids // 32, lax.rem(ids, 32)]).astype(bf16))
        got = along_z(jnp.concatenate([own_a, small], axis=0))
        s0 = rows_of(got, 0, b)
        e0 = rows_of(got, b, 16)
        mine_a = columns(s0)
        got1 = along_z(tie(jnp.concatenate([own_b, down_weight[:b]], axis=0), got))
        vecs, hb, here = fast_small(shard_order(e0, core_swap(e0), z, c), width, rows)
        gpos = [grad_place(q ^ d, lax.rem(zf - z + 4, 4)) for q in range(4) for zf in range(4)] + [c]
        gpos = jnp.stack(gpos).astype(jnp.int32)
        slots = fast_slots(z, c)
        slots_c = down_slots(z, c, ((0,), (1, 2), (3,)))
    else:
        ga, gb, gc, vecs, hb = plain_groups(
            jnp.stack(q4), jnp.stack(h4), down_weight, vec_args + (hidden_bias,)
        )
        gpos = jnp.concatenate([jnp.arange(16, dtype=jnp.int32), jnp.zeros((1,), jnp.int32)])
        here = lax.all_gather(ids, "fsdp", axis=0, tiled=True)

    onehot = (here.reshape(nf * rows)[:, None] == steps[None, :]).astype(bf16)
    looked = jnp.dot(onehot, step_table, preferred_element_type=f32).astype(bf16)
    if fast:
        looked, seg, pad, vecs, hb, gpos, slots, slots_c, marks = lax.optimization_barrier(
            (looked.reshape(rows, width), seg, pad, vecs, hb, gpos, slots, slots_c, marks)
        )
        sent = jnp.pad(looked, ((0, 16 - rows), (0, 0)))
        got_e = jnp.stack(along_z(sent))
        mine_a, got1, got_e = lax.optimization_barrier((mine_a, got1, got_e))
        emb = shard_order(got_e, core_swap(got_e), z, c)[:, :rows].reshape(nf, nf, rows, width // nf)
        emb = pick(emb.transpose(1, 0, 2, 3), f)
    else:
        emb = lax.all_to_all(looked.reshape(nf, rows, width // nf), "fsdp", 0, 0, tiled=True)
    emb = emb.transpose(1, 0, 2).reshape(rows, width).astype(f32)

    if fast:
        flat = (16, b, width)
        mine_a = mine_a.reshape(flat)
        core_a = core_swap(mine_a)
        ga = Group([mine_a, core_a], quarter_major, slots)
        mine_b = columns(rows_of(got1, 0, b))
        got2 = along_z(tie(down_weight[b : 3 * b], got1))
        tok_in = tie(tok, (core_a, emb))
    else:
        tok_in = tok
    normed, triple, att, attended, middle, n2 = compute_f1(tok_in, emb, seg, pad, vecs, ga, rows, length)
    if fast:
        mine_b, n2, got2 = lax.optimization_barrier((mine_b.reshape(flat), n2, got2))
        core_b = core_swap(mine_b)
        gb = Group([mine_b, core_b], quarter_major, slots)
        got3 = along_z(tie(down_weight[3 * b :], got2))
        c0 = rows_of(tie(got1, n2), b, b)
        c12 = jnp.stack(got2).reshape(8, b, width)
        n2, c12 = tie((n2, c12), core_b)
        c0x, c12x = core_swap(c0), core_swap(c12)
    active, gp, *grads_c = compute_f2(n2, cot, hb, gb, gpos)
    if fast:
        got3, c0x, c12x, gp, grads_c = lax.optimization_barrier((got3, c0x, c12x, gp, grads_c))
        c3 = jnp.stack(got3)
        gc = Group(
            [c0, c12, c3, c0x, c12x, core_swap(c3)],
            [(0, 0, 4), (1, 0, 8), (2, 0, 4), (3, 0, 4), (4, 0, 8), (5, 0, 4)],
            slots_c,
        )
        sc = Scatter(*grads_c)
        sc.split()
        gp, sc.out = lax.optimization_barrier((gp, sc.out))
        sc.one()
    dh, hb_sum, db_sum, *grads_b = compute_b1(n2, cot, gp, gc, gpos)
    if fast:
        dh, grads_b, sc.r1, sc.got = lax.optimization_barrier((dh, grads_b, sc.r1, sc.got))
        sc.two()
        sb = Scatter(*grads_b)
        sb.split()
        dh, sb.out = lax.optimization_barrier((dh, sb.out))
        sb.one()
    part = width // nf
    dmid, dbr, dt, sums2 = compute_b2(dh, cot, middle, vecs, triple, att, ga, gb, rows, length)
    if fast:
        dt, sb.r1, sc.r2, hb_sum = lax.optimization_barrier((dt, sb.r1, sc.r2, hb_sum))
        sb.two()
        sc.three()
    grads_a = compute_ga(normed, attended, dt, dbr, gpos)
    if fast:
        grads_a, sc.r3, sb.r2, dt = lax.optimization_barrier((grads_a, sc.r3, sb.r2, dt))
        sb.three()
        sa = Scatter(*grads_a)
        sa.split()
        dt, sa.out, active = lax.optimization_barrier((dt, sa.out, active))
        sa.one()
        mine_c = sc.total()
    input_grad, sums = compute_b4(tok, emb, dmid, dt, vecs, sums2, db_sum, ga, rows, length)
    if fast:
        hb_lanes = tie(hb_sum, sa.out).reshape(nf, 4 * part)
        sa.r1, sums, active, mine_c, hb_lanes, sb.r3 = lax.optimization_barrier(
            (sa.r1, sums, active, mine_c, hb_lanes, sb.r3)
        )
        sa.add_two()
        sums, active = tie((sums, active), sa.on)
        result = compute_f3(active, middle, vecs, gc)

    lines = sums.shape[0]
    if not fast:
        hb_lanes = hb_sum.reshape(nf, 4 * part)
    lanes = sums.reshape(lines, nf, part).transpose(1, 0, 2).reshape(nf, lines * part)
    payload = jnp.concatenate([lanes, hb_lanes, marks], axis=1)
    nt, end = rows * part, payload.shape[1] - rows
    if fast:
        sa.send_two()
        everyone = jnp.broadcast_to(payload[None], (nd,) + payload.shape).reshape(nd * nf, payload.shape[1])
        moved = lax.all_to_all(everyone, ("dp", "fsdp"), 0, 0, tiled=True)
        mine_b = sb.total()
        sa.r2, moved, mine_b, mine_c, result = lax.optimization_barrier((sa.r2, moved, mine_b, mine_c, result))
        sa.three()
        mine_b, mine_c = tie((mine_b, mine_c), sa.h3)
        out_bc = columns(jnp.concatenate([mine_b, mine_c], axis=0))
    else:
        moved = lax.all_to_all(payload, "fsdp", 0, 0, tiled=True)
        moved = lax.all_gather(moved, "dp", axis=0, tiled=True)
    table_rows = moved[:, :nt].reshape(nd * nf * rows, part)
    all_ids = moved[:, end:].astype(jnp.int32).reshape(1, nd * nf * rows)
    vec_sums = jnp.sum(moved[:, nt:end], axis=0)
    if not fast:
        result = compute_f3(active, middle, vecs, gc)
    if fast:
        sa.r3, out_bc, moved = lax.optimization_barrier((sa.r3, out_bc, moved))
        out_a = quarters(spread(sa.total()), d)
        out_b = out_bc[:, :b].astype(f32)
        down_grad = out_bc[:, b:].astype(f32).reshape(4 * b, width)
    else:
        out_b = plain_scatter(*grads_b)
        out_a = plain_scatter(*grads_a)
        down_grad = plain_scatter(*grads_c, rows_first=True)
    hidden_grad = jnp.concatenate([out_b[i] for i in range(4)], axis=1)
    triple_grad = jnp.concatenate([out_a[i] for i in range(3)], axis=1)
    output_grad = out_a[3]
    all_hot = (steps[:, None] == all_ids).astype(f32)
    table_grad = jnp.dot(all_hot, table_rows, precision=highest)
    v = [vec_sums[i * part : (i + 1) * part] for i in (5, 6, 4, 0, 1, 2, 3, 7)]
    hidden_bias_grad = vec_sums[(lines - rows) * part :]
    shape = tokens.shape
    return (
        result.reshape(shape), input_grad.reshape(shape), table_grad, triple_grad, v[0], v[1], output_grad, v[2],
        v[3], v[4], v[5], v[6], hidden_grad, hidden_bias_grad, down_grad, v[7],
    )


def solution(mesh):
    fast = mesh.shape["dp"] == 4 and mesh.shape["fsdp"] == 8
    batch = ("dp", "fsdp")
    vec, mat, tab = P("fsdp"), P("fsdp", None), P(None, "fsdp")
    tokens_spec = P(None, batch, None, None)
    return jax.shard_map(
        functools.partial(per_device, fast),
        mesh=mesh,
        in_specs=(
            tokens_spec, P(None, batch), P(None, batch, None), P(None, batch, None), tokens_spec,
            tab, mat, vec, vec, mat, vec, vec, vec, vec, vec, mat, vec, mat, vec,
        ),
        out_specs=(
            tokens_spec, tokens_spec, tab, mat, vec, vec, mat, vec, vec, vec, vec, vec, mat, vec, mat, vec,
        ),
        check_vma=False,
    )
```

```python
import functools
import math

import jax
import jax.numpy as jnp
from jax import lax
from jax.experimental import pallas as pl
from jax.experimental.pallas import tpu as pltpu
from jax.sharding import PartitionSpec as P

HEADS = 12
HD = 64
EPS = 1e-05
MASKED = -1e30
SCALE = 1.0 / math.sqrt(HD)
GELU_C = math.sqrt(2.0 / math.pi)
GELU_A = 0.044715
VMEM_LIMIT = 55 * 1024 * 1024
highest = lax.Precision.HIGHEST
f32 = jnp.float32
bf16 = jnp.bfloat16

NB = 8


def mm(a, b):
    return lax.dot_general(a, b, (((1,), (0,)), ((), ())), preferred_element_type=f32)


def mm_nt(a, b):
    return lax.dot_general(a, b, (((1,), (1,)), ((), ())), preferred_element_type=f32)


def mm_tn(a, b):
    return lax.dot_general(a, b, (((0,), (0,)), ((), ())), preferred_element_type=f32)


def moments(v):
    average = jnp.mean(v, axis=-1, keepdims=True)
    centered = v - average
    variance = jnp.mean(centered * centered, axis=-1, keepdims=True)
    inv = lax.rsqrt(variance + EPS)
    return centered * inv, inv


def ln_back(e, xhat, inv):
    return (e - jnp.mean(e, -1, keepdims=True) - xhat * jnp.mean(e * xhat, -1, keepdims=True)) * inv


def start_blocks(slots_ref, pieces, layout, w_ref, sem, low=None):
    i = 0
    for piece, first, count in layout:
        for t in range(count):
            slot = slots_ref[i]
            if low is None:
                pltpu.make_async_copy(pieces[piece].at[first + t], w_ref.at[slot], sem.at[slot]).start()
            else:

                @pl.when(slot >= low)
                def _(piece=piece, at=first + t, slot=slot):
                    place = slot - low
                    pltpu.make_async_copy(pieces[piece].at[at], w_ref.at[place], sem.at[place]).start()

            i += 1


def start_wide(slots_ref, pieces, layout, w_ref, sem):
    width = w_ref.shape[0]
    b = width // NB
    i = 0
    for piece, first, count in layout:
        for t in range(count):
            slot = slots_ref[i]
            row = pl.multiple_of(lax.rem(slot, NB) * b, b)
            column = pl.multiple_of(slot // NB * width, width)
            place = w_ref.at[pl.ds(row, b), pl.ds(column, width)]
            pltpu.make_async_copy(pieces[piece].at[first + t], place, sem.at[slot]).start()
            i += 1


def wait_wide(w_ref, sem):
    width = w_ref.shape[0]
    b = width // NB
    place = w_ref.at[pl.ds(0, b), pl.ds(0, width)]
    for slot in range(32):
        pltpu.make_async_copy(place, place, sem.at[slot]).wait()


def wait_blocks(w_ref, sem, first, count):
    def one(t, carry):
        pltpu.make_async_copy(w_ref.at[first + t], w_ref.at[first + t], sem.at[first + t]).wait()
        return carry

    lax.fori_loop(0, count, one, 0)


def load_blocks(slots_ref, pieces, layout, w_ref, sem):
    start_blocks(slots_ref, pieces, layout, w_ref, sem)
    wait_blocks(w_ref, sem, 0, 32)


def square(w_ref, j):
    part = w_ref[NB * j : NB * (j + 1)]
    return part.reshape(part.shape[0] * part.shape[1], part.shape[2])


def send_blocks(gpos_ref, spots, buf_ref, even_rows, odd_rows, b, outs, sem):
    core = gpos_ref[16]
    keep_out, keep_own, send_out, send_own = outs
    for t, at in enumerate(spots):
        place = gpos_ref[at]
        idx = lax.rem(place, 8)
        for parity, row in ((0, even_rows[t]), (1, odd_rows[t])):
            for kept in (True, False):
                for low in (True, False):
                    ref = (keep_out if low else keep_own) if kept else (send_out if low else send_own)
                    mine = (core == parity) if kept else (core != parity)
                    region = (place < 8) if low else (place >= 8)

                    @pl.when(mine & region)
                    def _(ref=ref, row=row, idx=idx, which=2 * t + parity):
                        pltpu.make_async_copy(buf_ref.at[pl.ds(row, b)], ref.at[idx], sem.at[which]).start()


def drain_blocks(buf_ref, b, sem):
    for t in range(8):
        pltpu.make_async_copy(buf_ref.at[pl.ds(0, b)], buf_ref.at[pl.ds(0, b)], sem.at[t]).wait()


def half_mask(rows, width):
    lane = lax.broadcasted_iota(jnp.int32, (rows, width), 1)
    return lane < HD


def both(x2, first):
    zero = jnp.zeros_like(x2)
    return jnp.concatenate([jnp.where(first, x2, zero), jnp.where(first, zero, x2)], axis=0)


def residual_of(tok_ref, emb_ref, step, rb, length):
    parts = []
    for r in range(rb):
        rows = tok_ref[r * length : (r + 1) * length].astype(f32)
        parts.append(rows + emb_ref[pl.ds(step * rb + r, 1), :])
    return jnp.concatenate(parts, axis=0) if rb > 1 else parts[0]


def f1_kernel(layout, rb, length, slots, tok_ref, emb_ref, seg_ref, pad_ref, vec_ref, *rest):
    n = max(l[0] for l in layout) + 1
    pieces = rest[:n]
    normed_ref, triple_ref, att_ref, attended_ref, middle_ref, n2_ref, w_ref, sem = rest[n:]
    step = pl.program_id(0)

    @pl.when(step == 0)
    def _():
        load_blocks(slots, pieces, layout, w_ref, sem)

    x = residual_of(tok_ref, emb_ref, step, rb, length)
    xhat, _inv = moments(x)
    normed = (xhat * vec_ref[3:4, :] + vec_ref[4:5, :]).astype(bf16)
    normed_ref[...] = normed
    width = normed.shape[1]
    for q, row in ((0, 0), (1, None), (2, 1)):
        t = mm(normed, square(w_ref, q))
        if row is not None:
            t = t + vec_ref[row : row + 1, :]
        triple_ref[q] = t.astype(bf16)
    eye = lax.broadcasted_iota(jnp.int32, (length, length), 0) == lax.broadcasted_iota(
        jnp.int32, (length, length), 1
    )
    first = half_mask(length, 2 * HD)
    masks = []
    for r in range(rb):
        seg = jnp.broadcast_to(seg_ref[pl.ds(step * rb + r, 1), :], (length, length))
        pad = jnp.broadcast_to(pad_ref[pl.ds(step * rb + r, 1), :], (length, length))
        allowed = (seg == seg.T) & ((pad == 0.0) | eye)
        allowed = jnp.where(allowed, 1.0, 0.0)
        masks.append(jnp.concatenate([allowed, allowed], axis=0) > 0.5)
    pairs = width // (2 * HD)
    every = [(r, hp) for r in range(rb) for hp in range(pairs)]
    for start in range(0, len(every), 12):
        some = []
        for r, hp in every[start : start + 12]:
            rows = slice(r * length, (r + 1) * length)
            lanes = slice(hp * 2 * HD, (hp + 1) * 2 * HD)
            s = mm_nt(both(triple_ref[0, rows, lanes], first), triple_ref[1, rows, lanes]) * SCALE
            some.append((r, hp, rows, lanes, jnp.where(masks[r], s, MASKED)))
        done = []
        for r, hp, rows, lanes, s in some:
            e = jnp.exp(s - jnp.max(s, axis=-1, keepdims=True))
            p = (e / jnp.sum(e, axis=-1, keepdims=True)).astype(bf16)
            att_ref[r * pairs + hp] = p
            done.append((rows, lanes, p))
        for rows, lanes, p in done:
            wide = jnp.concatenate([p[:length], p[length:]], axis=1)
            attended_ref[rows, lanes] = mm(wide, both(triple_ref[2, rows, lanes], first)).astype(bf16)
    branch = mm(attended_ref[...], square(w_ref, 3)) + vec_ref[2:3, :]
    middle = x + branch
    middle_ref[...] = middle
    xhat2, _inv2 = moments(middle)
    n2_ref[...] = (xhat2 * vec_ref[5:6, :] + vec_ref[6:7, :]).astype(bf16)


def gelu_rows(h_ref, bias, active_ref, gp_ref, first, count):
    sub = 32
    for m in range(count // sub):
        at = slice(first + m * sub, first + (m + 1) * sub)
        v = h_ref[at] + bias
        v2 = v * v
        w = GELU_C * v
        cubic = w * v2
        t = jnp.tanh(w + cubic * GELU_A)
        half = 0.5 * t + 0.5
        active_ref[at] = (v * half).astype(bf16)
        steep = w + cubic * (3.0 * GELU_A)
        gp_ref[at] = (half + (half - half * t) * steep).astype(bf16)


def f2_kernel(layout, slots, gpos, n2_ref, cot_hbm, hb_ref, *rest):
    n = max(l[0] for l in layout) + 1
    pieces = rest[:n]
    active_ref, gp_ref = rest[n : n + 2]
    outs = rest[n + 2 : n + 6]
    w_ref, h_ref, g_ref, cot_ref, sem, cot_sem, out_sem = rest[n + 6 :]
    j = pl.program_id(0)
    load = pltpu.make_async_copy(cot_hbm, cot_ref, cot_sem)

    @pl.when(j == 0)
    def _():
        start_blocks(slots, pieces, layout, w_ref, sem)
        load.start()

    wait_blocks(w_ref, sem, j * NB, NB)
    tokens, width = n2_ref.shape
    b = width // NB
    bias = hb_ref[pl.ds(j, 1), :]
    slot = lax.rem(j, 2)

    @pl.when(j >= 2)
    def _():
        drain_blocks(g_ref.at[slot], b, out_sem.at[slot])

    part = w_ref[pl.ds(j * NB, NB)].reshape(width, width)
    half = tokens // 2
    h_ref[:half] = mm(n2_ref[:half], part)
    h_ref[half:] = mm(n2_ref[half:], part)
    gelu_rows(h_ref, bias, active_ref, gp_ref, 0, half)
    gelu_rows(h_ref, bias, active_ref, gp_ref, half, half)

    @pl.when(j == 0)
    def _():
        load.wait()

    g_ref[slot] = mm_tn(active_ref[...], cot_ref[...]).astype(bf16)
    spots = [q * 4 + j for q in range(4)]
    even_rows, odd_rows = [q * b for q in range(4)], [(4 + q) * b for q in range(4)]
    send_blocks(gpos, spots, g_ref.at[slot], even_rows, odd_rows, b, outs, out_sem.at[slot])

    @pl.when(j == 3)
    def _():
        drain_blocks(g_ref.at[0], b, out_sem.at[0])
        drain_blocks(g_ref.at[1], b, out_sem.at[1])


def b1_kernel(layout, chunk, slots, gpos, n2_ref, cot_ref, gp_ref, *rest):
    n = max(l[0] for l in layout) + 1
    pieces = rest[:n]
    dh_ref, hb_ref, db_ref = rest[n : n + 3]
    outs = rest[n + 3 : n + 7]
    w_ref, h_ref, g_ref, sem, out_sem = rest[n + 7 :]
    j = pl.program_id(0)
    tokens, width = n2_ref.shape
    b = width // NB
    slot = lax.rem(j, 2)

    @pl.when(j == 0)
    def _():
        start_blocks(slots, pieces, layout, w_ref, sem)
        db_ref[...] = jnp.zeros_like(db_ref)
        db_ref[0:1] = jnp.sum(cot_ref[...].astype(f32), axis=0, keepdims=True)
        hb_ref[...] = jnp.zeros_like(hb_ref)

    wait_blocks(w_ref, sem, j * NB, NB)
    w = w_ref[pl.ds(j * NB, NB)].reshape(width, width)
    sub = 32
    total = jnp.zeros((8, width), f32)
    for m in range(tokens // chunk):
        h_ref[m] = mm_nt(cot_ref[m * chunk : (m + 1) * chunk], w)
    for m in range(tokens // chunk):
        for s in range(chunk // sub):
            at = slice(m * chunk + s * sub, m * chunk + (s + 1) * sub)
            dh = (h_ref[m, s * sub : (s + 1) * sub] * gp_ref[at].astype(f32)).astype(bf16)
            dh_ref[at] = dh
            total = total + jnp.sum(dh.astype(f32).reshape(sub // 8, 8, width), axis=0)
    hb_ref[pl.ds(j, 1), :] = jnp.sum(total, axis=0, keepdims=True)

    @pl.when(j >= 2)
    def _():
        drain_blocks(g_ref.at[slot], b, out_sem.at[slot])

    g_ref[slot] = mm_tn(n2_ref[...], dh_ref[...]).astype(bf16)
    spots = [j * 4 + zf for zf in range(4)]
    even_rows, odd_rows = [2 * zf * b for zf in range(4)], [(2 * zf + 1) * b for zf in range(4)]
    send_blocks(gpos, spots, g_ref.at[slot], even_rows, odd_rows, b, outs, out_sem.at[slot])

    @pl.when(j == 3)
    def _():
        drain_blocks(g_ref.at[0], b, out_sem.at[0])
        drain_blocks(g_ref.at[1], b, out_sem.at[1])


def b2_kernel(
    layout_a, layout_b, rb, length, slots_a, slots_b,
    dh_ref, cot_ref, middle_ref, vec_ref, triple_ref, att_ref, *rest
):
    na = max(l[0] for l in layout_a) + 1
    nb = max(l[0] for l in layout_b) + 1
    pieces_a, pieces_b, rest = rest[:na], rest[na : na + nb], rest[na + nb :]
    dmid_ref, dbr_ref, dt_ref, sums_ref, wo_ref, wb_ref, datt_ref, sem_a, sem_b = rest
    width = cot_ref.shape[1]
    b = width // NB

    @pl.when(pl.program_id(0) == 0)
    def _():
        start_wide(slots_b, pieces_b, layout_b, wb_ref, sem_b)
        start_blocks(slots_a, pieces_a, layout_a, wo_ref, sem_a, 3 * NB)
        sums_ref[...] = jnp.zeros_like(sums_ref)
        wait_wide(wb_ref, sem_b)
        wait_blocks(wo_ref, sem_a, 0, NB)

    d_n2 = mm_nt(dh_ref[...], wb_ref[...])
    xhat, inv = moments(middle_ref[...])
    sums_ref[0:1] += jnp.sum(d_n2 * xhat, axis=0, keepdims=True)
    sums_ref[1:2] += jnp.sum(d_n2, axis=0, keepdims=True)
    d_middle = cot_ref[...].astype(f32) + ln_back(d_n2 * vec_ref[5:6, :], xhat, inv)
    dmid_ref[...] = d_middle
    d_branch = d_middle.astype(bf16)
    dbr_ref[...] = d_branch
    sums_ref[2:3] += jnp.sum(d_branch.astype(f32), axis=0, keepdims=True)

    datt_ref[...] = mm_nt(d_branch, wo_ref[...].reshape(width, width)).astype(bf16)
    first = half_mask(length, 2 * HD)
    pairs = width // (2 * HD)
    every = [(r, hp) for r in range(rb) for hp in range(pairs)]
    for start in range(0, len(every), 12):
        some = []
        for r, hp in every[start : start + 12]:
            rows = slice(r * length, (r + 1) * length)
            lanes = slice(hp * 2 * HD, (hp + 1) * 2 * HD)
            dos = both(datt_ref[rows, lanes], first)
            some.append((rows, lanes, dos, att_ref[r * pairs + hp], mm_nt(dos, triple_ref[2, rows, lanes])))
        slopes = []
        for rows, lanes, dos, p_low, d_a in some:
            dt_ref[2, rows, lanes] = mm_tn(p_low, dos).astype(bf16)
            p = p_low.astype(f32)
            inner = jnp.sum(p * d_a, axis=-1, keepdims=True)
            slopes.append((p * (d_a - inner)).astype(bf16))
        for (rows, lanes, dos, p_low, d_a), ds in zip(some, slopes):
            wide = jnp.concatenate([ds[:length], ds[length:]], axis=1)
            dt_ref[0, rows, lanes] = (mm(wide, both(triple_ref[1, rows, lanes], first)) * SCALE).astype(bf16)
            dt_ref[1, rows, lanes] = (mm_tn(ds, both(triple_ref[0, rows, lanes], first)) * SCALE).astype(bf16)
    sums_ref[3:4] += jnp.sum(dt_ref[0].astype(f32), axis=0, keepdims=True)
    sums_ref[4:5] += jnp.sum(dt_ref[2].astype(f32), axis=0, keepdims=True)


def ga_kernel(gpos, normed_ref, dt_ref, attended_hbm, dbr_hbm, *rest):
    outs = rest[:4]
    attended_ref, dbr_ref, g_ref, in_sem, out_sem = rest[4:]
    j = pl.program_id(0)
    width = normed_ref.shape[1]
    b = width // NB
    slot = lax.rem(j, 2)
    loads = [
        pltpu.make_async_copy(attended_hbm, attended_ref, in_sem.at[0]),
        pltpu.make_async_copy(dbr_hbm, dbr_ref, in_sem.at[1]),
    ]

    @pl.when(j == 0)
    def _():
        for cp in loads:
            cp.start()

    @pl.when(j >= 2)
    def _():
        drain_blocks(g_ref.at[slot], b, out_sem.at[slot])

    @pl.when(j < 3)
    def _():
        g_ref[slot] = mm_tn(normed_ref[...], dt_ref[...]).astype(bf16)

    @pl.when(j == 3)
    def _():
        for cp in loads:
            cp.wait()
        g_ref[slot] = mm_tn(attended_ref[...], dbr_ref[...]).astype(bf16)

    spots = [j * 4 + zf for zf in range(4)]
    even_rows, odd_rows = [2 * zf * b for zf in range(4)], [(2 * zf + 1) * b for zf in range(4)]
    send_blocks(gpos, spots, g_ref.at[slot], even_rows, odd_rows, b, outs, out_sem.at[slot])

    @pl.when(j == 3)
    def _():
        drain_blocks(g_ref.at[0], b, out_sem.at[0])
        drain_blocks(g_ref.at[1], b, out_sem.at[1])


def b4_kernel(layout, rb, length, slots, tok_ref, emb_ref, dmid_ref, dt_ref, vec_ref, sums2_ref, db_ref, *rest):
    n = max(l[0] for l in layout) + 1
    pieces = rest[:n]
    ig_ref, sums_ref, w_ref, sem = rest[n:]
    base = pl.num_programs(0) * rb
    step = pl.program_id(0)

    @pl.when(step == 0)
    def _():
        load_blocks(slots, pieces, layout, w_ref, sem)
        sums_ref[...] = jnp.zeros_like(sums_ref)
        sums_ref[pl.ds(base + 2, 5)] = sums2_ref[0:5]
        sums_ref[pl.ds(base + 7, 1)] = db_ref[0:1]

    d_n = mm_nt(dt_ref[0], square(w_ref, 0))
    for q in range(1, 3):
        d_n = d_n + mm_nt(dt_ref[q], square(w_ref, q))
    xhat, inv = moments(residual_of(tok_ref, emb_ref, step, rb, length))
    sums_ref[pl.ds(base, 1)] += jnp.sum(d_n * xhat, axis=0, keepdims=True)
    sums_ref[pl.ds(base + 1, 1)] += jnp.sum(d_n, axis=0, keepdims=True)
    d_start = dmid_ref[...] + ln_back(d_n * vec_ref[3:4, :], xhat, inv)
    ig_ref[...] = d_start.astype(bf16)
    for r in range(rb):
        sums_ref[pl.ds(step * rb + r, 1), :] = jnp.sum(d_start[r * length : (r + 1) * length], axis=0, keepdims=True)


def f3_kernel(layout, slots, act_ref, middle_ref, vec_ref, *rest):
    n = max(l[0] for l in layout) + 1
    pieces = rest[:n]
    out_ref, w_ref, sem = rest[n:]

    @pl.when(pl.program_id(0) == 0)
    def _():
        load_blocks(slots, pieces, layout, w_ref, sem)

    width = middle_ref.shape[1]
    acc = mm(act_ref[...], w_ref[...].reshape(4 * width, width))
    out_ref[...] = (middle_ref[...] + (acc + vec_ref[7:8, :])).astype(bf16)


def sds(shape, dtype):
    return jax.ShapeDtypeStruct(shape, dtype)


def full(shape):
    zeros = (0,) * len(shape)
    return pl.BlockSpec(shape, lambda i: zeros)


smem = pl.BlockSpec(memory_space=pltpu.SMEM)
hbm = pl.BlockSpec(memory_space=pl.ANY)


def call(kernel, grid, in_specs, out_shape, out_specs, scratch, flops, nbytes, args):
    return pl.pallas_call(
        kernel,
        grid=grid,
        in_specs=in_specs,
        out_shape=out_shape,
        out_specs=out_specs,
        scratch_shapes=scratch,
        compiler_params=pltpu.CompilerParams(
            dimension_semantics=("arbitrary",), vmem_limit_bytes=VMEM_LIMIT
        ),
        cost_estimate=pl.CostEstimate(flops=flops, bytes_accessed=nbytes, transcendentals=0),
    )(*args)


class Group:
    def __init__(self, arrays, layout, slots):
        self.arrays, self.layout, self.slots = arrays, layout, slots


def compute_f1(tok, emb, seg, pad, vecs, group, rows, length):
    n, width = tok.shape
    rb = 2 if rows % 2 == 0 else 1
    block = rb * length
    pairs = width // (2 * HD)
    b = width // NB
    return call(
        functools.partial(f1_kernel, group.layout, rb, length),
        (rows // rb,),
        [smem, pl.BlockSpec((block, width), lambda i: (i, 0)), full(emb.shape), full(seg.shape), full(pad.shape), full(vecs.shape)]
        + [hbm] * len(group.arrays),
        [sds((n, width), bf16), sds((3, n, width), bf16), sds((rows * pairs, 2 * length, length), bf16),
         sds((n, width), bf16), sds((n, width), f32), sds((n, width), bf16)],
        [pl.BlockSpec((block, width), lambda i: (i, 0)), pl.BlockSpec((3, block, width), lambda i: (0, i, 0)),
         pl.BlockSpec((rb * pairs, 2 * length, length), lambda i: (i, 0, 0)),
         pl.BlockSpec((block, width), lambda i: (i, 0)), pl.BlockSpec((block, width), lambda i: (i, 0)),
         pl.BlockSpec((block, width), lambda i: (i, 0))],
        [pltpu.VMEM((32, b, width), bf16), pltpu.SemaphoreType.DMA((32,))],
        2 * n * width * width * 4 * 3, 20 << 20,
        [group.slots, tok, emb, seg, pad, vecs, *group.arrays],
    )


def compute_f2(n2, cot, hb, group, gpos):
    n, width = n2.shape
    b = width // NB
    column = pl.BlockSpec((n, width), lambda i: (0, i))
    return call(
        functools.partial(f2_kernel, group.layout),
        (4,),
        [smem, smem, full(n2.shape), hbm, full(hb.shape)] + [hbm] * len(group.arrays),
        [sds((n, 4 * width), bf16), sds((n, 4 * width), bf16), *[sds((8, b, width), bf16)] * 4],
        [column, column, hbm, hbm, hbm, hbm],
        [pltpu.VMEM((32, b, width), bf16), pltpu.VMEM((n, width), f32), pltpu.VMEM((2, width, width), bf16), pltpu.VMEM((n, width), bf16),
         pltpu.SemaphoreType.DMA((32,)), pltpu.SemaphoreType.DMA(()), pltpu.SemaphoreType.DMA((2, 8))],
        2 * n * width * width * 8 * 2, 20 << 20,
        [group.slots, gpos, n2, cot, hb, *group.arrays],
    )


def compute_b1(n2, cot, gp, group, gpos):
    n, width = n2.shape
    b = width // NB
    chunk = n // 2 if n % 64 == 0 else n
    column = pl.BlockSpec((n, width), lambda i: (0, i))
    return call(
        functools.partial(b1_kernel, group.layout, chunk),
        (4,),
        [smem, smem, full(n2.shape), full(cot.shape), column] + [hbm] * len(group.arrays),
        [sds((n, 4 * width), bf16), sds((4, width), f32), sds((8, width), f32), *[sds((8, b, width), bf16)] * 4],
        [column, full((4, width)), full((8, width)), hbm, hbm, hbm, hbm],
        [pltpu.VMEM((32, b, width), bf16), pltpu.VMEM((n // chunk, chunk, width), f32), pltpu.VMEM((2, width, width), bf16),
         pltpu.SemaphoreType.DMA((32,)), pltpu.SemaphoreType.DMA((2, 8))],
        2 * n * width * width * 8 * 2, 20 << 20,
        [group.slots, gpos, n2, cot, gp, *group.arrays],
    )


def compute_b2(dh, cot, middle, vecs, triple, att, ga, gb, rows, length):
    n, width = cot.shape
    rb = 2 if rows % 2 == 0 else 1
    block = rb * length
    pairs = width // (2 * HD)
    b = width // NB
    tile = pl.BlockSpec((block, width), lambda i: (i, 0))
    wide = pl.BlockSpec((3, block, width), lambda i: (0, i, 0))
    return call(
        functools.partial(b2_kernel, ga.layout, gb.layout, rb, length),
        (rows // rb,),
        [smem, smem, pl.BlockSpec((block, 4 * width), lambda i: (i, 0)), tile, tile, full(vecs.shape), wide,
         pl.BlockSpec((rb * pairs, 2 * length, length), lambda i: (i, 0, 0))]
        + [hbm] * (len(ga.arrays) + len(gb.arrays)),
        [sds((n, width), f32), sds((n, width), bf16), sds((3, n, width), bf16), sds((8, width), f32)],
        [tile, tile, wide, full((8, width))],
        [pltpu.VMEM((NB, b, width), bf16), pltpu.VMEM((width, 4 * width), bf16), pltpu.VMEM((block, width), bf16),
         pltpu.SemaphoreType.DMA((NB,)), pltpu.SemaphoreType.DMA((32,))],
        2 * n * width * width * 10, 30 << 20,
        [ga.slots, gb.slots, dh, cot, middle, vecs, triple, att, *ga.arrays, *gb.arrays],
    )


def compute_ga(normed, attended, dt, dbr, gpos):
    n, width = normed.shape
    b = width // NB
    return call(
        ga_kernel,
        (4,),
        [smem, full(normed.shape), pl.BlockSpec((None, n, width), lambda i: (jnp.minimum(i, 2), 0, 0)), hbm, hbm],
        [*[sds((8, b, width), bf16)] * 4],
        [hbm, hbm, hbm, hbm],
        [pltpu.VMEM((n, width), bf16), pltpu.VMEM((n, width), bf16), pltpu.VMEM((2, width, width), bf16),
         pltpu.SemaphoreType.DMA((2,)), pltpu.SemaphoreType.DMA((2, 8))],
        2 * n * width * width * 4 * 2, 12 << 20,
        [gpos, normed, dt, attended, dbr],
    )


def compute_b4(tok, emb, dmid, dt, vecs, sums2, db_sum, group, rows, length):
    n, width = tok.shape
    rb = 2 if rows % 2 == 0 else 1
    block = rb * length
    b = width // NB
    lines = 8 * ((rows + 8 + 7) // 8)
    return call(
        functools.partial(b4_kernel, group.layout, rb, length),
        (rows // rb,),
        [smem, pl.BlockSpec((block, width), lambda i: (i, 0)), full(emb.shape), pl.BlockSpec((block, width), lambda i: (i, 0)),
         pl.BlockSpec((3, block, width), lambda i: (0, i, 0)), full(vecs.shape), full(sums2.shape), full(db_sum.shape)]
        + [hbm] * len(group.arrays),
        [sds((n, width), bf16), sds((lines, width), f32)],
        [pl.BlockSpec((block, width), lambda i: (i, 0)), full((lines, width))],
        [pltpu.VMEM((32, b, width), bf16), pltpu.SemaphoreType.DMA((32,))],
        2 * n * width * width * 3 * 2, 12 << 20,
        [group.slots, tok, emb, dmid, dt, vecs, sums2, db_sum, *group.arrays],
    )


def compute_f3(active, middle, vecs, group):
    n, width = middle.shape
    b = width // NB
    block = 256 if n % 256 == 0 else n
    return call(
        functools.partial(f3_kernel, group.layout),
        (n // block,),
        [smem, pl.BlockSpec((block, 4 * width), lambda i: (i, 0)), pl.BlockSpec((block, width), lambda i: (i, 0)), full(vecs.shape)]
        + [hbm] * len(group.arrays),
        sds((n, width), bf16),
        pl.BlockSpec((block, width), lambda i: (i, 0)),
        [pltpu.VMEM((32, b, width), bf16), pltpu.SemaphoreType.DMA((32,))],
        2 * n * width * width * 4 * 2, 12 << 20,
        [group.slots, active, middle, vecs, *group.arrays],
    )


def plain_groups(own_a, own_b, own_c, small):
    width = own_a.shape[2]
    slots = jnp.arange(32, dtype=jnp.int32)

    def group(whole):
        return Group([whole.reshape(32, width // NB, width)], [(0, 0, 32)], slots)

    a = lax.all_gather(own_a, "fsdp", axis=1, tiled=True)
    b = lax.all_gather(own_b, "fsdp", axis=1, tiled=True)
    c = lax.all_gather(own_c, "fsdp", axis=0, tiled=True)
    vec = [lax.all_gather(v, "fsdp", axis=0, tiled=True) for v in small]
    return group(a), group(b), group(c), jnp.stack(vec[:8]).astype(f32), vec[8].astype(f32).reshape(4, width)


def plain_scatter(keep_out, keep_own, send_out, send_own, rows_first=False):
    b, width = keep_out.shape[1:]
    g = [jnp.concatenate(v, axis=0).reshape(4, 4, b, width) for v in ((keep_out, keep_own), (send_out, send_own))]
    g = jnp.stack(g, axis=2).astype(f32)
    if rows_first:
        g = g.transpose(1, 2, 0, 3, 4).reshape(32 * b, width)
        return lax.psum(lax.psum_scatter(g, "fsdp", scatter_dimension=0, tiled=True), "dp")
    g = g.reshape(4, NB * b, width)
    return lax.psum(lax.psum_scatter(g, "fsdp", scatter_dimension=1, tiled=True), "dp")


def pick(stacked, i):
    return lax.dynamic_index_in_dim(stacked, i, axis=0, keepdims=False)


def xor_perm(n, k):
    return [(i, i ^ k) for i in range(n)]


def core_swap(v):
    return lax.ppermute(v, "fsdp", xor_perm(8, 1))


def x_swap(v):
    return lax.ppermute(v, "dp", xor_perm(4, 1))


def y_swap(v):
    return lax.ppermute(v, "dp", xor_perm(4, 2))


def diagonal_swap(v):
    return lax.ppermute(v, "dp", xor_perm(4, 3))


def z_shift(v, k):
    return lax.ppermute(v, "fsdp", [(i, (i + 2 * k) % 8) for i in range(8)])


def tie(values, after):
    return lax.optimization_barrier((values, after))[0]


def columns(v):
    return lax.all_to_all(jnp.broadcast_to(v[None], (4,) + v.shape), "dp", 0, 0, tiled=True)


quarter_major = [(e, 4 * q, 4) for q in range(4) for e in (0, 1)]


def grad_place(delta, k):
    half, high, low = k // 2, delta // 2, lax.rem(delta, 2)
    leaves, other = jnp.where(half == 0, low, high), jnp.where(half == 0, high, low)
    return (1 - leaves) * 8 + half * 4 + other * 2 + lax.rem(k, 2)


def fast_slots(z, c):
    table = []
    for q in range(4):
        for e in (0, 1):
            for k in range(4):
                table.append(q * NB + 2 * lax.rem(z - k + 4, 4) + (c ^ e))
    return jnp.stack(table).astype(jnp.int32)


def along_z(v):
    return [v] + [z_shift(v, k) for k in (1, 2, 3)]


def rows_of(got, first, count):
    return jnp.stack([g[first : first + count] for g in got])


def down_slots(z, c, quarters_in):
    table = []
    for e in (0, 1):
        for part in quarters_in:
            for k in range(4):
                table += [8 * lax.rem(z - k + 4, 4) + 4 * (c ^ e) + q for q in part]
    return jnp.stack(table).astype(jnp.int32)


def shard_order(e0, e1, z, c):
    pair = jnp.stack([jnp.where(c == 0, e0, e1), jnp.where(c == 0, e1, e0)], axis=1)
    got = jnp.stack([pick(pair, lax.rem(z - i + 4, 4)) for i in range(4)])
    return got.reshape((8,) + got.shape[2:])


def fast_small(got, width, rows):
    got = got.astype(f32)
    vecs = got[:, :8, : width // 8].transpose(1, 0, 2).reshape(8, width)
    hb = got[:, 8, : width // 2].reshape(4, width)
    ids = (got[:, 9, :rows] * 32.0 + got[:, 10, :rows]).astype(jnp.int32)
    return vecs, hb, ids


def plus(*values):
    return sum(v.astype(f32) for v in values).astype(bf16)


class Scatter:
    def __init__(self, keep_out, keep_own, send_out, send_own):
        self.keep = (keep_out, keep_own)
        self.got = (core_swap(send_out), core_swap(send_own))

    def split(self):
        self.out = [plus(self.keep[0][4 * i : 4 * i + 4], self.got[0][4 * i : 4 * i + 4]) for i in range(2)]

    def one(self):
        self.r1 = [x_swap(self.out[0]), y_swap(self.out[1])]

    def add_two(self):
        at = [slice(4 * i + 2, 4 * i + 4) for i in range(2)]
        self.on = [plus(self.keep[1][at[i]], self.got[1][at[i]], self.r1[i][2:]) for i in range(2)]

    def send_two(self):
        self.r2 = [y_swap(self.on[0]), x_swap(self.on[1])]

    def two(self):
        self.add_two()
        self.send_two()

    def three(self, after=()):
        at = [slice(4 * i, 4 * i + 2) for i in range(2)]
        halves = [plus(self.keep[1][at[i]], self.got[1][at[i]], self.r1[i][:2], self.r2[i]) for i in range(2)]
        self.h3 = [halves[k // 2][k % 2] for k in range(4)]
        last = tie(self.h3[1], after) if after else self.h3[1]
        self.r3 = [self.h3[0], z_shift(last, 1), z_shift(self.h3[2], 2), z_shift(self.h3[3], 3)]

    def total(self):
        return sum(p.astype(f32) for p in self.r3).astype(bf16)


def spread(mine):
    return [mine, x_swap(mine), y_swap(mine), diagonal_swap(mine)]


def quarters(got, d):
    got = jnp.stack(got)
    return [pick(got, d ^ q).astype(f32) for q in range(4)]


def per_device(
    fast, tokens, timesteps, segments, padding, cotangent, step_table,
    triple_weight, query_bias, value_bias, output_weight, output_bias,
    first_gain, first_shift, second_gain, second_shift,
    hidden_weight, hidden_bias, down_weight, down_bias,
):
    micro, local_rows, length, width = tokens.shape
    rows = micro * local_rows
    n = rows * length
    nd, nf = lax.axis_size("dp"), lax.axis_size("fsdp")
    d, f = lax.axis_index("dp"), lax.axis_index("fsdp")
    z, c = f // 2, lax.rem(f, 2)
    tok = tokens.reshape(n, width)
    cot = cotangent.reshape(n, width)
    seg = segments.reshape(rows, length).astype(f32)
    pad = padding.reshape(rows, length).astype(f32)

    ids = timesteps.reshape(rows)
    marks = jnp.broadcast_to(ids.astype(f32)[None, :], (nf, rows))
    steps = lax.iota(jnp.int32, step_table.shape[0])
    q4 = [triple_weight[:, i * width : (i + 1) * width] for i in range(3)] + [output_weight]
    h4 = [hidden_weight[:, i * width : (i + 1) * width] for i in range(4)]
    vec_args = (query_bias, value_bias, output_bias, first_gain, first_shift, second_gain, second_shift, down_bias)
    if fast:
        b = width // NB
        own_a = pick(jnp.stack(q4), d)
        own_b = pick(jnp.stack(h4), d)
        small = jnp.zeros((16, width), bf16)
        small = small.at[:8, : width // nf].set(jnp.stack(vec_args))
        small = small.at[8, : 4 * width // nf].set(hidden_bias)
        small = small.at[9:11, :rows].set(jnp.stack([ids // 32, lax.rem(ids, 32)]).astype(bf16))
        got = along_z(jnp.concatenate([own_a, small], axis=0))
        s0 = rows_of(got, 0, b)
        e0 = rows_of(got, b, 16)
        mine_a = columns(s0)
        got1 = along_z(tie(jnp.concatenate([own_b, down_weight[:b]], axis=0), got))
        vecs, hb, here = fast_small(shard_order(e0, core_swap(e0), z, c), width, rows)
        gpos = [grad_place(q ^ d, lax.rem(zf - z + 4, 4)) for q in range(4) for zf in range(4)] + [c]
        gpos = jnp.stack(gpos).astype(jnp.int32)
        slots = fast_slots(z, c)
        slots_c = down_slots(z, c, ((0,), (1, 2), (3,)))
    else:
        ga, gb, gc, vecs, hb = plain_groups(
            jnp.stack(q4), jnp.stack(h4), down_weight, vec_args + (hidden_bias,)
        )
        gpos = jnp.concatenate([jnp.arange(16, dtype=jnp.int32), jnp.zeros((1,), jnp.int32)])
        here = lax.all_gather(ids, "fsdp", axis=0, tiled=True)

    onehot = (here.reshape(nf * rows)[:, None] == steps[None, :]).astype(bf16)
    looked = jnp.dot(onehot, step_table, preferred_element_type=f32).astype(bf16)
    if fast:
        looked, seg, pad, vecs, hb, gpos, slots, slots_c, marks = lax.optimization_barrier(
            (looked.reshape(rows, width), seg, pad, vecs, hb, gpos, slots, slots_c, marks)
        )
        sent = jnp.pad(looked, ((0, 16 - rows), (0, 0)))
        got_e = [sent, z_shift(sent, 1), z_shift(sent, 2), z_shift(tie(sent, got1[3]), 3)]
        got_e = jnp.stack(got_e)
        mine_a, got1, got_e = lax.optimization_barrier((mine_a, got1, got_e))
        emb = shard_order(got_e, core_swap(got_e), z, c)[:, :rows].reshape(nf, nf, rows, width // nf)
        emb = pick(emb.transpose(1, 0, 2, 3), f)
    else:
        emb = lax.all_to_all(looked.reshape(nf, rows, width // nf), "fsdp", 0, 0, tiled=True)
    emb = emb.transpose(1, 0, 2).reshape(rows, width).astype(f32)

    if fast:
        flat = (16, b, width)
        mine_a = mine_a.reshape(flat)
        core_a = core_swap(mine_a)
        ga = Group([mine_a, core_a], quarter_major, slots)
        mine_b = columns(rows_of(got1, 0, b))
        c0 = rows_of(got1, b, b)
        got2 = along_z(tie(down_weight[b : 3 * b], got1))
        tok_in = tie(tok, (core_a, emb))
    else:
        tok_in = tok
    normed, triple, att, attended, middle, n2 = compute_f1(tok_in, emb, seg, pad, vecs, ga, rows, length)
    if fast:
        c0x = core_swap(c0)
        mine_b, n2, got2, c0x = lax.optimization_barrier((mine_b.reshape(flat), n2, got2, c0x))
        core_b = core_swap(mine_b)
        gb = Group([mine_b, core_b], quarter_major, slots)
        got3 = along_z(tie(down_weight[3 * b :], got2))
        c12 = jnp.stack(got2).reshape(8, b, width)
        n2, c12 = tie((n2, c12), core_b)
        c12x = core_swap(c12)
    active, gp, *grads_c = compute_f2(n2, cot, hb, gb, gpos)
    if fast:
        got3, c0x, c12x, gp, grads_c = lax.optimization_barrier((got3, c0x, c12x, gp, grads_c))
        c3 = jnp.stack(got3)
        gc = Group(
            [c0, c12, c3, c0x, c12x, core_swap(c3)],
            [(0, 0, 4), (1, 0, 8), (2, 0, 4), (3, 0, 4), (4, 0, 8), (5, 0, 4)],
            slots_c,
        )
        sc = Scatter(*grads_c)
        sc.split()
        gp, sc.out = lax.optimization_barrier((gp, sc.out))
        sc.one()
    dh, hb_sum, db_sum, *grads_b = compute_b1(n2, cot, gp, gc, gpos)
    if fast:
        dh, grads_b, sc.r1, sc.got = lax.optimization_barrier((dh, grads_b, sc.r1, sc.got))
        sc.two()
        sb = Scatter(*grads_b)
        sb.split()
        dh, sb.out = lax.optimization_barrier((dh, sb.out))
        sb.one()
    part = width // nf
    dmid, dbr, dt, sums2 = compute_b2(dh, cot, middle, vecs, triple, att, ga, gb, rows, length)
    if fast:
        dt, sb.r1, sc.r2, hb_sum = lax.optimization_barrier((dt, sb.r1, sc.r2, hb_sum))
        sb.two()
        sc.three()
    grads_a = compute_ga(normed, attended, dt, dbr, gpos)
    if fast:
        grads_a, sc.r3, sb.r2, dt = lax.optimization_barrier((grads_a, sc.r3, sb.r2, dt))
        sa = Scatter(*grads_a)
        sa.split()
        sb.three((sa.got[1],))
        dt, sa.out, active = lax.optimization_barrier((dt, sa.out, active))
        sa.one()
        mine_c = sc.total()
    input_grad, sums = compute_b4(tok, emb, dmid, dt, vecs, sums2, db_sum, ga, rows, length)
    if fast:
        hb_lanes = tie(hb_sum, sa.out).reshape(nf, 4 * part)
        sa.r1, sums, active, mine_c, hb_lanes, sb.r3 = lax.optimization_barrier(
            (sa.r1, sums, active, mine_c, hb_lanes, sb.r3)
        )
        sa.add_two()
        sums, active = tie((sums, active), sa.on)
        result = compute_f3(active, middle, vecs, gc)

    lines = sums.shape[0]
    if not fast:
        hb_lanes = hb_sum.reshape(nf, 4 * part)
    lanes = sums.reshape(lines, nf, part).transpose(1, 0, 2).reshape(nf, lines * part)
    payload = jnp.concatenate([lanes, hb_lanes, marks], axis=1)
    nt, end = rows * part, payload.shape[1] - rows
    if fast:
        sa.send_two()
        everyone = jnp.broadcast_to(payload[None], (nd,) + payload.shape).reshape(nd * nf, payload.shape[1])
        moved = lax.all_to_all(everyone, ("dp", "fsdp"), 0, 0, tiled=True)
        mine_b = sb.total()
        sa.r2, moved, mine_b, mine_c, result = lax.optimization_barrier((sa.r2, moved, mine_b, mine_c, result))
        sa.three()
        mine_b, mine_c = tie((mine_b, mine_c), sa.h3)
        out_bc = columns(jnp.concatenate([mine_b, mine_c], axis=0))
    else:
        moved = lax.all_to_all(payload, "fsdp", 0, 0, tiled=True)
        moved = lax.all_gather(moved, "dp", axis=0, tiled=True)
    table_rows = moved[:, :nt].reshape(nd * nf * rows, part)
    all_ids = moved[:, end:].astype(jnp.int32).reshape(1, nd * nf * rows)
    vec_sums = jnp.sum(moved[:, nt:end], axis=0)
    if not fast:
        result = compute_f3(active, middle, vecs, gc)
    if fast:
        sa.r3, out_bc, moved = lax.optimization_barrier((sa.r3, out_bc, moved))
        out_a = quarters(spread(sa.total()), d)
        out_b = out_bc[:, :b].astype(f32)
        down_grad = out_bc[:, b:].astype(f32).reshape(4 * b, width)
    else:
        out_b = plain_scatter(*grads_b)
        out_a = plain_scatter(*grads_a)
        down_grad = plain_scatter(*grads_c, rows_first=True)
    hidden_grad = jnp.concatenate([out_b[i] for i in range(4)], axis=1)
    triple_grad = jnp.concatenate([out_a[i] for i in range(3)], axis=1)
    output_grad = out_a[3]
    all_hot = (steps[:, None] == all_ids).astype(f32)
    table_grad = jnp.dot(all_hot, table_rows, precision=highest)
    v = [vec_sums[i * part : (i + 1) * part] for i in (5, 6, 4, 0, 1, 2, 3, 7)]
    hidden_bias_grad = vec_sums[(lines - rows) * part :]
    shape = tokens.shape
    return (
        result.reshape(shape), input_grad.reshape(shape), table_grad, triple_grad, v[0], v[1], output_grad, v[2],
        v[3], v[4], v[5], v[6], hidden_grad, hidden_bias_grad, down_grad, v[7],
    )


def solution(mesh):
    fast = mesh.shape["dp"] == 4 and mesh.shape["fsdp"] == 8
    batch = ("dp", "fsdp")
    vec, mat, tab = P("fsdp"), P("fsdp", None), P(None, "fsdp")
    tokens_spec = P(None, batch, None, None)
    return jax.shard_map(
        functools.partial(per_device, fast),
        mesh=mesh,
        in_specs=(
            tokens_spec, P(None, batch), P(None, batch, None), P(None, batch, None), tokens_spec,
            tab, mat, vec, vec, mat, vec, vec, vec, vec, vec, mat, vec, mat, vec,
        ),
        out_specs=(
            tokens_spec, tokens_spec, tab, mat, vec, vec, mat, vec, vec, vec, vec, vec, mat, vec, mat, vec,
        ),
        check_vma=False,
    )
```

```python
import functools
import math

import jax
import jax.numpy as jnp
from jax import lax
from jax.experimental import pallas as pl
from jax.experimental.pallas import tpu as pltpu
from jax.sharding import PartitionSpec as P

HEADS = 12
HD = 64
EPS = 1e-05
MASKED = -1e30
SCALE = 1.0 / math.sqrt(HD)
GELU_C = math.sqrt(2.0 / math.pi)
GELU_A = 0.044715
VMEM_LIMIT = 55 * 1024 * 1024
highest = lax.Precision.HIGHEST
f32 = jnp.float32
bf16 = jnp.bfloat16

NB = 8


def mm(a, b):
    return lax.dot_general(a, b, (((1,), (0,)), ((), ())), preferred_element_type=f32)


def mm_nt(a, b):
    return lax.dot_general(a, b, (((1,), (1,)), ((), ())), preferred_element_type=f32)


def mm_tn(a, b):
    return lax.dot_general(a, b, (((0,), (0,)), ((), ())), preferred_element_type=f32)


def moments(v):
    average = jnp.mean(v, axis=-1, keepdims=True)
    centered = v - average
    variance = jnp.mean(centered * centered, axis=-1, keepdims=True)
    inv = lax.rsqrt(variance + EPS)
    return centered * inv, inv


def ln_back(e, xhat, inv):
    return (e - jnp.mean(e, -1, keepdims=True) - xhat * jnp.mean(e * xhat, -1, keepdims=True)) * inv


def start_blocks(slots_ref, pieces, layout, w_ref, sem, low=None):
    i = 0
    for piece, first, count in layout:
        for t in range(count):
            slot = slots_ref[i]
            if low is None:
                pltpu.make_async_copy(pieces[piece].at[first + t], w_ref.at[slot], sem.at[slot]).start()
            else:

                @pl.when(slot >= low)
                def _(piece=piece, at=first + t, slot=slot):
                    place = slot - low
                    pltpu.make_async_copy(pieces[piece].at[at], w_ref.at[place], sem.at[place]).start()

            i += 1


def start_wide(slots_ref, pieces, layout, w_ref, sem):
    width = w_ref.shape[0]
    b = width // NB
    i = 0
    for piece, first, count in layout:
        for t in range(count):
            slot = slots_ref[i]
            row = pl.multiple_of(lax.rem(slot, NB) * b, b)
            column = pl.multiple_of(slot // NB * width, width)
            place = w_ref.at[pl.ds(row, b), pl.ds(column, width)]
            pltpu.make_async_copy(pieces[piece].at[first + t], place, sem.at[slot]).start()
            i += 1


def wait_wide(w_ref, sem):
    width = w_ref.shape[0]
    b = width // NB
    place = w_ref.at[pl.ds(0, b), pl.ds(0, width)]
    for slot in range(32):
        pltpu.make_async_copy(place, place, sem.at[slot]).wait()


def wait_blocks(w_ref, sem, first, count):
    def one(t, carry):
        pltpu.make_async_copy(w_ref.at[first + t], w_ref.at[first + t], sem.at[first + t]).wait()
        return carry

    lax.fori_loop(0, count, one, 0)


def load_blocks(slots_ref, pieces, layout, w_ref, sem):
    start_blocks(slots_ref, pieces, layout, w_ref, sem)
    wait_blocks(w_ref, sem, 0, 32)


def square(w_ref, j):
    part = w_ref[NB * j : NB * (j + 1)]
    return part.reshape(part.shape[0] * part.shape[1], part.shape[2])


def send_blocks(gpos_ref, spots, buf_ref, even_rows, odd_rows, b, outs, sem):
    core = gpos_ref[16]
    keep_out, keep_own, send_out, send_own = outs
    for t, at in enumerate(spots):
        place = gpos_ref[at]
        idx = lax.rem(place, 8)
        for parity, row in ((0, even_rows[t]), (1, odd_rows[t])):
            for kept in (True, False):
                for low in (True, False):
                    ref = (keep_out if low else keep_own) if kept else (send_out if low else send_own)
                    mine = (core == parity) if kept else (core != parity)
                    region = (place < 8) if low else (place >= 8)

                    @pl.when(mine & region)
                    def _(ref=ref, row=row, idx=idx, which=2 * t + parity):
                        pltpu.make_async_copy(buf_ref.at[pl.ds(row, b)], ref.at[idx], sem.at[which]).start()


def drain_blocks(buf_ref, b, sem):
    for t in range(8):
        pltpu.make_async_copy(buf_ref.at[pl.ds(0, b)], buf_ref.at[pl.ds(0, b)], sem.at[t]).wait()


def half_mask(rows, width):
    lane = lax.broadcasted_iota(jnp.int32, (rows, width), 1)
    return lane < HD


def both(x2, first):
    zero = jnp.zeros_like(x2)
    return jnp.concatenate([jnp.where(first, x2, zero), jnp.where(first, zero, x2)], axis=0)


def residual_of(tok_ref, emb_ref, step, rb, length):
    parts = []
    for r in range(rb):
        rows = tok_ref[r * length : (r + 1) * length].astype(f32)
        parts.append(rows + emb_ref[pl.ds(step * rb + r, 1), :])
    return jnp.concatenate(parts, axis=0) if rb > 1 else parts[0]


def f1_kernel(layout, rb, length, slots, tok_ref, emb_ref, seg_ref, pad_ref, vec_ref, *rest):
    n = max(l[0] for l in layout) + 1
    pieces = rest[:n]
    normed_ref, triple_ref, att_ref, attended_ref, middle_ref, n2_ref, w_ref, sem = rest[n:]
    step = pl.program_id(0)

    @pl.when(step == 0)
    def _():
        load_blocks(slots, pieces, layout, w_ref, sem)

    x = residual_of(tok_ref, emb_ref, step, rb, length)
    xhat, _inv = moments(x)
    normed = (xhat * vec_ref[3:4, :] + vec_ref[4:5, :]).astype(bf16)
    normed_ref[...] = normed
    width = normed.shape[1]
    for q, row in ((0, 0), (1, None), (2, 1)):
        t = mm(normed, square(w_ref, q))
        if row is not None:
            t = t + vec_ref[row : row + 1, :]
        triple_ref[q] = t.astype(bf16)
    eye = lax.broadcasted_iota(jnp.int32, (length, length), 0) == lax.broadcasted_iota(
        jnp.int32, (length, length), 1
    )
    first = half_mask(length, 2 * HD)
    masks = []
    for r in range(rb):
        seg = jnp.broadcast_to(seg_ref[pl.ds(step * rb + r, 1), :], (length, length))
        pad = jnp.broadcast_to(pad_ref[pl.ds(step * rb + r, 1), :], (length, length))
        allowed = (seg == seg.T) & ((pad == 0.0) | eye)
        allowed = jnp.where(allowed, 1.0, 0.0)
        masks.append(jnp.concatenate([allowed, allowed], axis=0) > 0.5)
    pairs = width // (2 * HD)
    every = [(r, hp) for r in range(rb) for hp in range(pairs)]
    for start in range(0, len(every), 12):
        some = []
        for r, hp in every[start : start + 12]:
            rows = slice(r * length, (r + 1) * length)
            lanes = slice(hp * 2 * HD, (hp + 1) * 2 * HD)
            s = mm_nt(both(triple_ref[0, rows, lanes], first), triple_ref[1, rows, lanes]) * SCALE
            some.append((r, hp, rows, lanes, jnp.where(masks[r], s, MASKED)))
        done = []
        for r, hp, rows, lanes, s in some:
            e = jnp.exp(s - jnp.max(s, axis=-1, keepdims=True))
            p = (e / jnp.sum(e, axis=-1, keepdims=True)).astype(bf16)
            att_ref[r * pairs + hp] = p
            done.append((rows, lanes, p))
        for rows, lanes, p in done:
            wide = jnp.concatenate([p[:length], p[length:]], axis=1)
            attended_ref[rows, lanes] = mm(wide, both(triple_ref[2, rows, lanes], first)).astype(bf16)
    branch = mm(attended_ref[...], square(w_ref, 3)) + vec_ref[2:3, :]
    middle = x + branch
    middle_ref[...] = middle
    xhat2, _inv2 = moments(middle)
    n2_ref[...] = (xhat2 * vec_ref[5:6, :] + vec_ref[6:7, :]).astype(bf16)


def gelu_rows(h_ref, bias, active_ref, gp_ref, first, count):
    sub = 32
    for m in range(count // sub):
        at = slice(first + m * sub, first + (m + 1) * sub)
        v = h_ref[at] + bias
        v2 = v * v
        w = GELU_C * v
        cubic = w * v2
        t = jnp.tanh(w + cubic * GELU_A)
        half = 0.5 * t + 0.5
        active_ref[at] = (v * half).astype(bf16)
        steep = w + cubic * (3.0 * GELU_A)
        gp_ref[at] = (half + (half - half * t) * steep).astype(bf16)


def f2_kernel(layout, slots, gpos, n2_ref, cot_hbm, hb_ref, *rest):
    n = max(l[0] for l in layout) + 1
    pieces = rest[:n]
    active_ref, gp_ref = rest[n : n + 2]
    outs = rest[n + 2 : n + 6]
    w_ref, h_ref, g_ref, cot_ref, sem, cot_sem, out_sem = rest[n + 6 :]
    j = pl.program_id(0)
    load = pltpu.make_async_copy(cot_hbm, cot_ref, cot_sem)

    @pl.when(j == 0)
    def _():
        start_blocks(slots, pieces, layout, w_ref, sem)
        load.start()

    wait_blocks(w_ref, sem, j * NB, NB)
    tokens, width = n2_ref.shape
    b = width // NB
    bias = hb_ref[pl.ds(j, 1), :]
    slot = lax.rem(j, 2)

    @pl.when(j >= 2)
    def _():
        drain_blocks(g_ref.at[slot], b, out_sem.at[slot])

    part = w_ref[pl.ds(j * NB, NB)].reshape(width, width)
    half = tokens // 2
    h_ref[:half] = mm(n2_ref[:half], part)
    h_ref[half:] = mm(n2_ref[half:], part)
    gelu_rows(h_ref, bias, active_ref, gp_ref, 0, half)
    gelu_rows(h_ref, bias, active_ref, gp_ref, half, half)

    @pl.when(j == 0)
    def _():
        load.wait()

    g_ref[slot] = mm_tn(active_ref[...], cot_ref[...]).astype(bf16)
    spots = [q * 4 + j for q in range(4)]
    even_rows, odd_rows = [q * b for q in range(4)], [(4 + q) * b for q in range(4)]
    send_blocks(gpos, spots, g_ref.at[slot], even_rows, odd_rows, b, outs, out_sem.at[slot])

    @pl.when(j == 3)
    def _():
        drain_blocks(g_ref.at[0], b, out_sem.at[0])
        drain_blocks(g_ref.at[1], b, out_sem.at[1])


def b1_kernel(layout, chunk, slots, gpos, n2_ref, cot_ref, gp_ref, *rest):
    n = max(l[0] for l in layout) + 1
    pieces = rest[:n]
    dh_ref, hb_ref, db_ref = rest[n : n + 3]
    outs = rest[n + 3 : n + 7]
    w_ref, h_ref, g_ref, sem, out_sem = rest[n + 7 :]
    j = pl.program_id(0)
    tokens, width = n2_ref.shape
    b = width // NB
    slot = lax.rem(j, 2)

    @pl.when(j == 0)
    def _():
        start_blocks(slots, pieces, layout, w_ref, sem)
        db_ref[...] = jnp.zeros_like(db_ref)
        db_ref[0:1] = jnp.sum(cot_ref[...].astype(f32), axis=0, keepdims=True)
        hb_ref[...] = jnp.zeros_like(hb_ref)

    wait_blocks(w_ref, sem, j * NB, NB)
    w = w_ref[pl.ds(j * NB, NB)].reshape(width, width)
    sub = 32
    total = jnp.zeros((8, width), f32)
    for m in range(tokens // chunk):
        h_ref[m] = mm_nt(cot_ref[m * chunk : (m + 1) * chunk], w)
    for m in range(tokens // chunk):
        for s in range(chunk // sub):
            at = slice(m * chunk + s * sub, m * chunk + (s + 1) * sub)
            dh = (h_ref[m, s * sub : (s + 1) * sub] * gp_ref[at].astype(f32)).astype(bf16)
            dh_ref[at] = dh
            total = total + jnp.sum(dh.astype(f32).reshape(sub // 8, 8, width), axis=0)
    hb_ref[pl.ds(j, 1), :] = jnp.sum(total, axis=0, keepdims=True)

    @pl.when(j >= 2)
    def _():
        drain_blocks(g_ref.at[slot], b, out_sem.at[slot])

    g_ref[slot] = mm_tn(n2_ref[...], dh_ref[...]).astype(bf16)
    spots = [j * 4 + zf for zf in range(4)]
    even_rows, odd_rows = [2 * zf * b for zf in range(4)], [(2 * zf + 1) * b for zf in range(4)]
    send_blocks(gpos, spots, g_ref.at[slot], even_rows, odd_rows, b, outs, out_sem.at[slot])

    @pl.when(j == 3)
    def _():
        drain_blocks(g_ref.at[0], b, out_sem.at[0])
        drain_blocks(g_ref.at[1], b, out_sem.at[1])


def b2_kernel(
    layout_a, layout_b, rb, length, slots_a, slots_b,
    dh_ref, cot_ref, middle_ref, vec_ref, triple_ref, att_ref, *rest
):
    na = max(l[0] for l in layout_a) + 1
    nb = max(l[0] for l in layout_b) + 1
    pieces_a, pieces_b, rest = rest[:na], rest[na : na + nb], rest[na + nb :]
    dmid_ref, dbr_ref, dt_ref, sums_ref, wo_ref, wb_ref, datt_ref, sem_a, sem_b = rest
    width = cot_ref.shape[1]
    b = width // NB

    @pl.when(pl.program_id(0) == 0)
    def _():
        start_wide(slots_b, pieces_b, layout_b, wb_ref, sem_b)
        start_blocks(slots_a, pieces_a, layout_a, wo_ref, sem_a, 3 * NB)
        sums_ref[...] = jnp.zeros_like(sums_ref)
        wait_wide(wb_ref, sem_b)
        wait_blocks(wo_ref, sem_a, 0, NB)

    d_n2 = mm_nt(dh_ref[...], wb_ref[...])
    xhat, inv = moments(middle_ref[...])
    sums_ref[0:1] += jnp.sum(d_n2 * xhat, axis=0, keepdims=True)
    sums_ref[1:2] += jnp.sum(d_n2, axis=0, keepdims=True)
    d_middle = cot_ref[...].astype(f32) + ln_back(d_n2 * vec_ref[5:6, :], xhat, inv)
    dmid_ref[...] = d_middle
    d_branch = d_middle.astype(bf16)
    dbr_ref[...] = d_branch
    sums_ref[2:3] += jnp.sum(d_branch.astype(f32), axis=0, keepdims=True)

    datt_ref[...] = mm_nt(d_branch, wo_ref[...].reshape(width, width)).astype(bf16)
    first = half_mask(length, 2 * HD)
    pairs = width // (2 * HD)
    every = [(r, hp) for r in range(rb) for hp in range(pairs)]
    for start in range(0, len(every), 12):
        some = []
        for r, hp in every[start : start + 12]:
            rows = slice(r * length, (r + 1) * length)
            lanes = slice(hp * 2 * HD, (hp + 1) * 2 * HD)
            dos = both(datt_ref[rows, lanes], first)
            some.append((rows, lanes, dos, att_ref[r * pairs + hp], mm_nt(dos, triple_ref[2, rows, lanes])))
        slopes = []
        for rows, lanes, dos, p_low, d_a in some:
            dt_ref[2, rows, lanes] = mm_tn(p_low, dos).astype(bf16)
            p = p_low.astype(f32)
            inner = jnp.sum(p * d_a, axis=-1, keepdims=True)
            slopes.append((p * (d_a - inner)).astype(bf16))
        for (rows, lanes, dos, p_low, d_a), ds in zip(some, slopes):
            wide = jnp.concatenate([ds[:length], ds[length:]], axis=1)
            dt_ref[0, rows, lanes] = (mm(wide, both(triple_ref[1, rows, lanes], first)) * SCALE).astype(bf16)
            dt_ref[1, rows, lanes] = (mm_tn(ds, both(triple_ref[0, rows, lanes], first)) * SCALE).astype(bf16)
    sums_ref[3:4] += jnp.sum(dt_ref[0].astype(f32), axis=0, keepdims=True)
    sums_ref[4:5] += jnp.sum(dt_ref[2].astype(f32), axis=0, keepdims=True)


def ga_kernel(gpos, normed_ref, dt_ref, attended_hbm, dbr_hbm, *rest):
    outs = rest[:4]
    attended_ref, dbr_ref, g_ref, in_sem, out_sem = rest[4:]
    j = pl.program_id(0)
    width = normed_ref.shape[1]
    b = width // NB
    slot = lax.rem(j, 2)
    loads = [
        pltpu.make_async_copy(attended_hbm, attended_ref, in_sem.at[0]),
        pltpu.make_async_copy(dbr_hbm, dbr_ref, in_sem.at[1]),
    ]

    @pl.when(j == 0)
    def _():
        for cp in loads:
            cp.start()

    @pl.when(j >= 2)
    def _():
        drain_blocks(g_ref.at[slot], b, out_sem.at[slot])

    @pl.when(j < 3)
    def _():
        g_ref[slot] = mm_tn(normed_ref[...], dt_ref[...]).astype(bf16)

    @pl.when(j == 3)
    def _():
        for cp in loads:
            cp.wait()
        g_ref[slot] = mm_tn(attended_ref[...], dbr_ref[...]).astype(bf16)

    spots = [j * 4 + zf for zf in range(4)]
    even_rows, odd_rows = [2 * zf * b for zf in range(4)], [(2 * zf + 1) * b for zf in range(4)]
    send_blocks(gpos, spots, g_ref.at[slot], even_rows, odd_rows, b, outs, out_sem.at[slot])

    @pl.when(j == 3)
    def _():
        drain_blocks(g_ref.at[0], b, out_sem.at[0])
        drain_blocks(g_ref.at[1], b, out_sem.at[1])


def b4_kernel(layout, rb, length, slots, tok_ref, emb_ref, dmid_ref, dt_ref, vec_ref, sums2_ref, db_ref, *rest):
    n = max(l[0] for l in layout) + 1
    pieces = rest[:n]
    ig_ref, sums_ref, w_ref, sem = rest[n:]
    base = pl.num_programs(0) * rb
    step = pl.program_id(0)

    @pl.when(step == 0)
    def _():
        load_blocks(slots, pieces, layout, w_ref, sem)
        sums_ref[...] = jnp.zeros_like(sums_ref)
        sums_ref[pl.ds(base + 2, 5)] = sums2_ref[0:5]
        sums_ref[pl.ds(base + 7, 1)] = db_ref[0:1]

    d_n = mm_nt(dt_ref[0], square(w_ref, 0))
    for q in range(1, 3):
        d_n = d_n + mm_nt(dt_ref[q], square(w_ref, q))
    xhat, inv = moments(residual_of(tok_ref, emb_ref, step, rb, length))
    sums_ref[pl.ds(base, 1)] += jnp.sum(d_n * xhat, axis=0, keepdims=True)
    sums_ref[pl.ds(base + 1, 1)] += jnp.sum(d_n, axis=0, keepdims=True)
    d_start = dmid_ref[...] + ln_back(d_n * vec_ref[3:4, :], xhat, inv)
    ig_ref[...] = d_start.astype(bf16)
    for r in range(rb):
        sums_ref[pl.ds(step * rb + r, 1), :] = jnp.sum(d_start[r * length : (r + 1) * length], axis=0, keepdims=True)


def f3_kernel(layout, slots, act_ref, middle_ref, vec_ref, *rest):
    n = max(l[0] for l in layout) + 1
    pieces = rest[:n]
    out_ref, w_ref, sem = rest[n:]

    @pl.when(pl.program_id(0) == 0)
    def _():
        load_blocks(slots, pieces, layout, w_ref, sem)

    width = middle_ref.shape[1]
    acc = mm(act_ref[...], w_ref[...].reshape(4 * width, width))
    out_ref[...] = (middle_ref[...] + (acc + vec_ref[7:8, :])).astype(bf16)


def sds(shape, dtype):
    return jax.ShapeDtypeStruct(shape, dtype)


def full(shape):
    zeros = (0,) * len(shape)
    return pl.BlockSpec(shape, lambda i: zeros)


smem = pl.BlockSpec(memory_space=pltpu.SMEM)
hbm = pl.BlockSpec(memory_space=pl.ANY)


def call(kernel, grid, in_specs, out_shape, out_specs, scratch, flops, nbytes, args):
    return pl.pallas_call(
        kernel,
        grid=grid,
        in_specs=in_specs,
        out_shape=out_shape,
        out_specs=out_specs,
        scratch_shapes=scratch,
        compiler_params=pltpu.CompilerParams(
            dimension_semantics=("arbitrary",), vmem_limit_bytes=VMEM_LIMIT
        ),
        cost_estimate=pl.CostEstimate(flops=flops, bytes_accessed=nbytes, transcendentals=0),
    )(*args)


class Group:
    def __init__(self, arrays, layout, slots):
        self.arrays, self.layout, self.slots = arrays, layout, slots


def compute_f1(tok, emb, seg, pad, vecs, group, rows, length):
    n, width = tok.shape
    rb = 2 if rows % 2 == 0 else 1
    block = rb * length
    pairs = width // (2 * HD)
    b = width // NB
    return call(
        functools.partial(f1_kernel, group.layout, rb, length),
        (rows // rb,),
        [smem, pl.BlockSpec((block, width), lambda i: (i, 0)), full(emb.shape), full(seg.shape), full(pad.shape), full(vecs.shape)]
        + [hbm] * len(group.arrays),
        [sds((n, width), bf16), sds((3, n, width), bf16), sds((rows * pairs, 2 * length, length), bf16),
         sds((n, width), bf16), sds((n, width), f32), sds((n, width), bf16)],
        [pl.BlockSpec((block, width), lambda i: (i, 0)), pl.BlockSpec((3, block, width), lambda i: (0, i, 0)),
         pl.BlockSpec((rb * pairs, 2 * length, length), lambda i: (i, 0, 0)),
         pl.BlockSpec((block, width), lambda i: (i, 0)), pl.BlockSpec((block, width), lambda i: (i, 0)),
         pl.BlockSpec((block, width), lambda i: (i, 0))],
        [pltpu.VMEM((32, b, width), bf16), pltpu.SemaphoreType.DMA((32,))],
        2 * n * width * width * 4 * 3, 20 << 20,
        [group.slots, tok, emb, seg, pad, vecs, *group.arrays],
    )


def compute_f2(n2, cot, hb, group, gpos):
    n, width = n2.shape
    b = width // NB
    column = pl.BlockSpec((n, width), lambda i: (0, i))
    return call(
        functools.partial(f2_kernel, group.layout),
        (4,),
        [smem, smem, full(n2.shape), hbm, full(hb.shape)] + [hbm] * len(group.arrays),
        [sds((n, 4 * width), bf16), sds((n, 4 * width), bf16), *[sds((8, b, width), bf16)] * 4],
        [column, column, hbm, hbm, hbm, hbm],
        [pltpu.VMEM((32, b, width), bf16), pltpu.VMEM((n, width), f32), pltpu.VMEM((2, width, width), bf16), pltpu.VMEM((n, width), bf16),
         pltpu.SemaphoreType.DMA((32,)), pltpu.SemaphoreType.DMA(()), pltpu.SemaphoreType.DMA((2, 8))],
        2 * n * width * width * 8 * 2, 20 << 20,
        [group.slots, gpos, n2, cot, hb, *group.arrays],
    )


def compute_b1(n2, cot, gp, group, gpos):
    n, width = n2.shape
    b = width // NB
    chunk = n // 2 if n % 64 == 0 else n
    column = pl.BlockSpec((n, width), lambda i: (0, i))
    return call(
        functools.partial(b1_kernel, group.layout, chunk),
        (4,),
        [smem, smem, full(n2.shape), full(cot.shape), column] + [hbm] * len(group.arrays),
        [sds((n, 4 * width), bf16), sds((4, width), f32), sds((8, width), f32), *[sds((8, b, width), bf16)] * 4],
        [column, full((4, width)), full((8, width)), hbm, hbm, hbm, hbm],
        [pltpu.VMEM((32, b, width), bf16), pltpu.VMEM((n // chunk, chunk, width), f32), pltpu.VMEM((2, width, width), bf16),
         pltpu.SemaphoreType.DMA((32,)), pltpu.SemaphoreType.DMA((2, 8))],
        2 * n * width * width * 8 * 2, 20 << 20,
        [group.slots, gpos, n2, cot, gp, *group.arrays],
    )


def compute_b2(dh, cot, middle, vecs, triple, att, ga, gb, rows, length):
    n, width = cot.shape
    rb = 2 if rows % 2 == 0 else 1
    block = rb * length
    pairs = width // (2 * HD)
    b = width // NB
    tile = pl.BlockSpec((block, width), lambda i: (i, 0))
    wide = pl.BlockSpec((3, block, width), lambda i: (0, i, 0))
    return call(
        functools.partial(b2_kernel, ga.layout, gb.layout, rb, length),
        (rows // rb,),
        [smem, smem, pl.BlockSpec((block, 4 * width), lambda i: (i, 0)), tile, tile, full(vecs.shape), wide,
         pl.BlockSpec((rb * pairs, 2 * length, length), lambda i: (i, 0, 0))]
        + [hbm] * (len(ga.arrays) + len(gb.arrays)),
        [sds((n, width), f32), sds((n, width), bf16), sds((3, n, width), bf16), sds((8, width), f32)],
        [tile, tile, wide, full((8, width))],
        [pltpu.VMEM((NB, b, width), bf16), pltpu.VMEM((width, 4 * width), bf16), pltpu.VMEM((block, width), bf16),
         pltpu.SemaphoreType.DMA((NB,)), pltpu.SemaphoreType.DMA((32,))],
        2 * n * width * width * 10, 30 << 20,
        [ga.slots, gb.slots, dh, cot, middle, vecs, triple, att, *ga.arrays, *gb.arrays],
    )


def compute_ga(normed, attended, dt, dbr, gpos):
    n, width = normed.shape
    b = width // NB
    return call(
        ga_kernel,
        (4,),
        [smem, full(normed.shape), pl.BlockSpec((None, n, width), lambda i: (jnp.minimum(i, 2), 0, 0)), hbm, hbm],
        [*[sds((8, b, width), bf16)] * 4],
        [hbm, hbm, hbm, hbm],
        [pltpu.VMEM((n, width), bf16), pltpu.VMEM((n, width), bf16), pltpu.VMEM((2, width, width), bf16),
         pltpu.SemaphoreType.DMA((2,)), pltpu.SemaphoreType.DMA((2, 8))],
        2 * n * width * width * 4 * 2, 12 << 20,
        [gpos, normed, dt, attended, dbr],
    )


def compute_b4(tok, emb, dmid, dt, vecs, sums2, db_sum, group, rows, length):
    n, width = tok.shape
    rb = 2 if rows % 2 == 0 else 1
    block = rb * length
    b = width // NB
    lines = 8 * ((rows + 8 + 7) // 8)
    return call(
        functools.partial(b4_kernel, group.layout, rb, length),
        (rows // rb,),
        [smem, pl.BlockSpec((block, width), lambda i: (i, 0)), full(emb.shape), pl.BlockSpec((block, width), lambda i: (i, 0)),
         pl.BlockSpec((3, block, width), lambda i: (0, i, 0)), full(vecs.shape), full(sums2.shape), full(db_sum.shape)]
        + [hbm] * len(group.arrays),
        [sds((n, width), bf16), sds((lines, width), f32)],
        [pl.BlockSpec((block, width), lambda i: (i, 0)), full((lines, width))],
        [pltpu.VMEM((32, b, width), bf16), pltpu.SemaphoreType.DMA((32,))],
        2 * n * width * width * 3 * 2, 12 << 20,
        [group.slots, tok, emb, dmid, dt, vecs, sums2, db_sum, *group.arrays],
    )


def compute_f3(active, middle, vecs, group):
    n, width = middle.shape
    b = width // NB
    block = 256 if n % 256 == 0 else n
    return call(
        functools.partial(f3_kernel, group.layout),
        (n // block,),
        [smem, pl.BlockSpec((block, 4 * width), lambda i: (i, 0)), pl.BlockSpec((block, width), lambda i: (i, 0)), full(vecs.shape)]
        + [hbm] * len(group.arrays),
        sds((n, width), bf16),
        pl.BlockSpec((block, width), lambda i: (i, 0)),
        [pltpu.VMEM((32, b, width), bf16), pltpu.SemaphoreType.DMA((32,))],
        2 * n * width * width * 4 * 2, 12 << 20,
        [group.slots, active, middle, vecs, *group.arrays],
    )


def plain_groups(own_a, own_b, own_c, small):
    width = own_a.shape[2]
    slots = jnp.arange(32, dtype=jnp.int32)

    def group(whole):
        return Group([whole.reshape(32, width // NB, width)], [(0, 0, 32)], slots)

    a = lax.all_gather(own_a, "fsdp", axis=1, tiled=True)
    b = lax.all_gather(own_b, "fsdp", axis=1, tiled=True)
    c = lax.all_gather(own_c, "fsdp", axis=0, tiled=True)
    vec = [lax.all_gather(v, "fsdp", axis=0, tiled=True) for v in small]
    return group(a), group(b), group(c), jnp.stack(vec[:8]).astype(f32), vec[8].astype(f32).reshape(4, width)


def plain_scatter(keep_out, keep_own, send_out, send_own, rows_first=False):
    b, width = keep_out.shape[1:]
    g = [jnp.concatenate(v, axis=0).reshape(4, 4, b, width) for v in ((keep_out, keep_own), (send_out, send_own))]
    g = jnp.stack(g, axis=2).astype(f32)
    if rows_first:
        g = g.transpose(1, 2, 0, 3, 4).reshape(32 * b, width)
        return lax.psum(lax.psum_scatter(g, "fsdp", scatter_dimension=0, tiled=True), "dp")
    g = g.reshape(4, NB * b, width)
    return lax.psum(lax.psum_scatter(g, "fsdp", scatter_dimension=1, tiled=True), "dp")


def pick(stacked, i):
    return lax.dynamic_index_in_dim(stacked, i, axis=0, keepdims=False)


def xor_perm(n, k):
    return [(i, i ^ k) for i in range(n)]


def core_swap(v):
    return lax.ppermute(v, "fsdp", xor_perm(8, 1))


def x_swap(v):
    return lax.ppermute(v, "dp", xor_perm(4, 1))


def y_swap(v):
    return lax.ppermute(v, "dp", xor_perm(4, 2))


def diagonal_swap(v):
    return lax.ppermute(v, "dp", xor_perm(4, 3))


def z_shift(v, k):
    return lax.ppermute(v, "fsdp", [(i, (i + 2 * k) % 8) for i in range(8)])


def tie(values, after):
    return lax.optimization_barrier((values, after))[0]


def columns(v):
    return lax.all_to_all(jnp.broadcast_to(v[None], (4,) + v.shape), "dp", 0, 0, tiled=True)


quarter_major = [(e, 4 * q, 4) for q in range(4) for e in (0, 1)]


def grad_place(delta, k):
    half, high, low = k // 2, delta // 2, lax.rem(delta, 2)
    leaves, other = jnp.where(half == 0, low, high), jnp.where(half == 0, high, low)
    return (1 - leaves) * 8 + half * 4 + other * 2 + lax.rem(k, 2)


def fast_slots(z, c):
    table = []
    for q in range(4):
        for e in (0, 1):
            for k in range(4):
                table.append(q * NB + 2 * lax.rem(z - k + 4, 4) + (c ^ e))
    return jnp.stack(table).astype(jnp.int32)


def along_z(v):
    return [v] + [z_shift(v, k) for k in (1, 2, 3)]


def rows_of(got, first, count):
    return jnp.stack([g[first : first + count] for g in got])


def down_slots(z, c, quarters_in):
    table = []
    for e in (0, 1):
        for part in quarters_in:
            for k in range(4):
                table += [8 * lax.rem(z - k + 4, 4) + 4 * (c ^ e) + q for q in part]
    return jnp.stack(table).astype(jnp.int32)


def shard_order(e0, e1, z, c):
    pair = jnp.stack([jnp.where(c == 0, e0, e1), jnp.where(c == 0, e1, e0)], axis=1)
    got = jnp.stack([pick(pair, lax.rem(z - i + 4, 4)) for i in range(4)])
    return got.reshape((8,) + got.shape[2:])


def fast_small(got, width, rows):
    got = got.astype(f32)
    vecs = got[:, :8, : width // 8].transpose(1, 0, 2).reshape(8, width)
    hb = got[:, 8, : width // 2].reshape(4, width)
    ids = (got[:, 9, :rows] * 32.0 + got[:, 10, :rows]).astype(jnp.int32)
    return vecs, hb, ids


def plus(*values):
    return sum(v.astype(f32) for v in values).astype(bf16)


class Scatter:
    def __init__(self, keep_out, keep_own, send_out, send_own):
        self.keep = (keep_out, keep_own)
        self.got = (core_swap(send_out), core_swap(send_own))

    def split(self):
        self.out = [plus(self.keep[0][4 * i : 4 * i + 4], self.got[0][4 * i : 4 * i + 4]) for i in range(2)]

    def one(self):
        self.r1 = [x_swap(self.out[0]), y_swap(self.out[1])]

    def add_two(self):
        at = [slice(4 * i + 2, 4 * i + 4) for i in range(2)]
        self.on = [plus(self.keep[1][at[i]], self.got[1][at[i]], self.r1[i][2:]) for i in range(2)]

    def send_two(self):
        self.r2 = [y_swap(self.on[0]), x_swap(self.on[1])]

    def two(self):
        self.add_two()
        self.send_two()

    def three(self, after=()):
        at = [slice(4 * i, 4 * i + 2) for i in range(2)]
        halves = [plus(self.keep[1][at[i]], self.got[1][at[i]], self.r1[i][:2], self.r2[i]) for i in range(2)]
        self.h3 = [halves[k // 2][k % 2] for k in range(4)]
        last = tie(self.h3[1], after) if after else self.h3[1]
        self.r3 = [self.h3[0], z_shift(last, 1), z_shift(self.h3[2], 2), z_shift(self.h3[3], 3)]

    def total(self):
        return sum(p.astype(f32) for p in self.r3).astype(bf16)


def spread(mine):
    return [mine, x_swap(mine), y_swap(mine), diagonal_swap(mine)]


def quarters(got, d):
    got = jnp.stack(got)
    return [pick(got, d ^ q).astype(f32) for q in range(4)]


def per_device(
    fast, tokens, timesteps, segments, padding, cotangent, step_table,
    triple_weight, query_bias, value_bias, output_weight, output_bias,
    first_gain, first_shift, second_gain, second_shift,
    hidden_weight, hidden_bias, down_weight, down_bias,
):
    micro, local_rows, length, width = tokens.shape
    rows = micro * local_rows
    n = rows * length
    nd, nf = lax.axis_size("dp"), lax.axis_size("fsdp")
    d, f = lax.axis_index("dp"), lax.axis_index("fsdp")
    z, c = f // 2, lax.rem(f, 2)
    tok = tokens.reshape(n, width)
    cot = cotangent.reshape(n, width)
    seg = segments.reshape(rows, length).astype(f32)
    pad = padding.reshape(rows, length).astype(f32)

    ids = timesteps.reshape(rows)
    marks = jnp.broadcast_to(ids.astype(f32)[None, :], (nf, rows))
    steps = lax.iota(jnp.int32, step_table.shape[0])
    q4 = [triple_weight[:, i * width : (i + 1) * width] for i in range(3)] + [output_weight]
    h4 = [hidden_weight[:, i * width : (i + 1) * width] for i in range(4)]
    vec_args = (query_bias, value_bias, output_bias, first_gain, first_shift, second_gain, second_shift, down_bias)
    if fast:
        b = width // NB
        own_a = pick(jnp.stack(q4), d)
        own_b = pick(jnp.stack(h4), d)
        small = jnp.zeros((16, width), bf16)
        small = small.at[:8, : width // nf].set(jnp.stack(vec_args))
        small = small.at[8, : 4 * width // nf].set(hidden_bias)
        small = small.at[9:11, :rows].set(jnp.stack([ids // 32, lax.rem(ids, 32)]).astype(bf16))
        got = along_z(jnp.concatenate([own_a, small], axis=0))
        s0 = rows_of(got, 0, b)
        e0 = rows_of(got, b, 16)
        mine_a = columns(s0)
        got1 = along_z(tie(jnp.concatenate([own_b, down_weight[:b]], axis=0), got))
        vecs, hb, here = fast_small(shard_order(e0, core_swap(e0), z, c), width, rows)
        gpos = [grad_place(q ^ d, lax.rem(zf - z + 4, 4)) for q in range(4) for zf in range(4)] + [c]
        gpos = jnp.stack(gpos).astype(jnp.int32)
        slots = fast_slots(z, c)
        slots_c = down_slots(z, c, ((0,), (1, 2), (3,)))
    else:
        ga, gb, gc, vecs, hb = plain_groups(
            jnp.stack(q4), jnp.stack(h4), down_weight, vec_args + (hidden_bias,)
        )
        gpos = jnp.concatenate([jnp.arange(16, dtype=jnp.int32), jnp.zeros((1,), jnp.int32)])
        here = lax.all_gather(ids, "fsdp", axis=0, tiled=True)

    onehot = (here.reshape(nf * rows)[:, None] == steps[None, :]).astype(bf16)
    looked = jnp.dot(onehot, step_table, preferred_element_type=f32).astype(bf16)
    if fast:
        looked, seg, pad, vecs, hb, gpos, slots, slots_c, marks = lax.optimization_barrier(
            (looked.reshape(rows, width), seg, pad, vecs, hb, gpos, slots, slots_c, marks)
        )
        sent = jnp.pad(looked, ((0, 16 - rows), (0, 0)))
        got_e = [sent, z_shift(sent, 1), z_shift(sent, 2), z_shift(tie(sent, got1[3]), 3)]
        got_e = jnp.stack(got_e)
        mine_a, got1, got_e = lax.optimization_barrier((mine_a, got1, got_e))
        emb = shard_order(got_e, core_swap(got_e), z, c)[:, :rows].reshape(nf, nf, rows, width // nf)
        emb = pick(emb.transpose(1, 0, 2, 3), f)
    else:
        emb = lax.all_to_all(looked.reshape(nf, rows, width // nf), "fsdp", 0, 0, tiled=True)
    emb = emb.transpose(1, 0, 2).reshape(rows, width).astype(f32)

    if fast:
        flat = (16, b, width)
        mine_a = mine_a.reshape(flat)
        core_a = core_swap(mine_a)
        ga = Group([mine_a, core_a], quarter_major, slots)
        mine_b = columns(rows_of(got1, 0, b))
        c0 = rows_of(got1, b, b)
        got2 = along_z(tie(down_weight[b : 3 * b], got1))
        tok_in = tie(tok, (core_a, emb))
    else:
        tok_in = tok
    normed, triple, att, attended, middle, n2 = compute_f1(tok_in, emb, seg, pad, vecs, ga, rows, length)
    if fast:
        c0x = core_swap(c0)
        mine_b, n2, got2, c0x = lax.optimization_barrier((mine_b.reshape(flat), n2, got2, c0x))
        core_b = core_swap(mine_b)
        gb = Group([mine_b, core_b], quarter_major, slots)
        got3 = along_z(tie(down_weight[3 * b :], got2))
        c12 = jnp.stack(got2).reshape(8, b, width)
        n2, c12 = tie((n2, c12), core_b)
        c12x = core_swap(c12)
    active, gp, *grads_c = compute_f2(n2, cot, hb, gb, gpos)
    if fast:
        got3, c0x, c12x, gp, grads_c = lax.optimization_barrier((got3, c0x, c12x, gp, grads_c))
        c3 = jnp.stack(got3)
        gc = Group(
            [c0, c12, c3, c0x, c12x, core_swap(c3)],
            [(0, 0, 4), (1, 0, 8), (2, 0, 4), (3, 0, 4), (4, 0, 8), (5, 0, 4)],
            slots_c,
        )
        sc = Scatter(*grads_c)
        sc.split()
        gp, sc.out = lax.optimization_barrier((gp, sc.out))
        sc.one()
    dh, hb_sum, db_sum, *grads_b = compute_b1(n2, cot, gp, gc, gpos)
    if fast:
        dh, grads_b, sc.r1, sc.got = lax.optimization_barrier((dh, grads_b, sc.r1, sc.got))
        sc.two()
        sb = Scatter(*grads_b)
        sb.split()
        dh, sb.out = lax.optimization_barrier((dh, sb.out))
        sb.one()
    part = width // nf
    dmid, dbr, dt, sums2 = compute_b2(dh, cot, middle, vecs, triple, att, ga, gb, rows, length)
    if fast:
        dt, sb.r1, sc.r2, hb_sum = lax.optimization_barrier((dt, sb.r1, sc.r2, hb_sum))
        sb.two()
        sc.three()
    grads_a = compute_ga(normed, attended, dt, dbr, gpos)
    if fast:
        grads_a, sc.r3, sb.r2, dt = lax.optimization_barrier((grads_a, sc.r3, sb.r2, dt))
        sa = Scatter(*grads_a)
        sa.split()
        sb.three((sa.got[1],))
        dt, sa.out, active = lax.optimization_barrier((dt, sa.out, active))
        sa.one()
        mine_c = sc.total()
    input_grad, sums = compute_b4(tok, emb, dmid, dt, vecs, sums2, db_sum, ga, rows, length)
    if fast:
        hb_lanes = tie(hb_sum, sa.out).reshape(nf, 4 * part)
        sa.r1, sums, active, mine_c, hb_lanes, sb.r3 = lax.optimization_barrier(
            (sa.r1, sums, active, mine_c, hb_lanes, sb.r3)
        )
        sa.add_two()
        sums = tie(sums, sa.on)

    lines = sums.shape[0]
    if not fast:
        hb_lanes = hb_sum.reshape(nf, 4 * part)
    lanes = sums.reshape(lines, nf, part).transpose(1, 0, 2).reshape(nf, lines * part)
    payload = jnp.concatenate([lanes, hb_lanes, marks], axis=1)
    nt, end = rows * part, payload.shape[1] - rows
    if fast:
        sa.send_two()
        everyone = jnp.broadcast_to(payload[None], (nd,) + payload.shape).reshape(nd * nf, payload.shape[1])
        moved = lax.all_to_all(everyone, ("dp", "fsdp"), 0, 0, tiled=True)
        mine_b = sb.total()
        sa.r2, mine_b, mine_c, active = lax.optimization_barrier((sa.r2, mine_b, mine_c, active))
        sa.three()
        result = compute_f3(tie(active, sa.h3), middle, vecs, gc)
        mine_b, mine_c = tie((mine_b, mine_c), sa.h3)
        out_bc = columns(jnp.concatenate([mine_b, mine_c], axis=0))
    else:
        moved = lax.all_to_all(payload, "fsdp", 0, 0, tiled=True)
        moved = lax.all_gather(moved, "dp", axis=0, tiled=True)
    table_rows = moved[:, :nt].reshape(nd * nf * rows, part)
    all_ids = moved[:, end:].astype(jnp.int32).reshape(1, nd * nf * rows)
    vec_sums = jnp.sum(moved[:, nt:end], axis=0)
    if not fast:
        result = compute_f3(active, middle, vecs, gc)
    if fast:
        sa.r3, out_bc, moved, result = lax.optimization_barrier((sa.r3, out_bc, moved, result))
        out_a = quarters(spread(sa.total()), d)
        out_b = out_bc[:, :b].astype(f32)
        down_grad = out_bc[:, b:].astype(f32).reshape(4 * b, width)
    else:
        out_b = plain_scatter(*grads_b)
        out_a = plain_scatter(*grads_a)
        down_grad = plain_scatter(*grads_c, rows_first=True)
    hidden_grad = jnp.concatenate([out_b[i] for i in range(4)], axis=1)
    triple_grad = jnp.concatenate([out_a[i] for i in range(3)], axis=1)
    output_grad = out_a[3]
    all_hot = (steps[:, None] == all_ids).astype(f32)
    table_grad = jnp.dot(all_hot, table_rows, precision=highest)
    v = [vec_sums[i * part : (i + 1) * part] for i in (5, 6, 4, 0, 1, 2, 3, 7)]
    hidden_bias_grad = vec_sums[(lines - rows) * part :]
    shape = tokens.shape
    return (
        result.reshape(shape), input_grad.reshape(shape), table_grad, triple_grad, v[0], v[1], output_grad, v[2],
        v[3], v[4], v[5], v[6], hidden_grad, hidden_bias_grad, down_grad, v[7],
    )


def solution(mesh):
    fast = mesh.shape["dp"] == 4 and mesh.shape["fsdp"] == 8
    batch = ("dp", "fsdp")
    vec, mat, tab = P("fsdp"), P("fsdp", None), P(None, "fsdp")
    tokens_spec = P(None, batch, None, None)
    return jax.shard_map(
        functools.partial(per_device, fast),
        mesh=mesh,
        in_specs=(
            tokens_spec, P(None, batch), P(None, batch, None), P(None, batch, None), tokens_spec,
            tab, mat, vec, vec, mat, vec, vec, vec, vec, vec, mat, vec, mat, vec,
        ),
        out_specs=(
            tokens_spec, tokens_spec, tab, mat, vec, vec, mat, vec, vec, vec, vec, vec, mat, vec, mat, vec,
        ),
        check_vma=False,
    )
```

```python
import functools
import math

import jax
import jax.numpy as jnp
from jax import lax
from jax.experimental import pallas as pl
from jax.experimental.pallas import tpu as pltpu
from jax.sharding import PartitionSpec as P

HEADS = 12
HD = 64
EPS = 1e-05
MASKED = -1e30
SCALE = 1.0 / math.sqrt(HD)
GELU_C = math.sqrt(2.0 / math.pi)
GELU_A = 0.044715
VMEM_LIMIT = 55 * 1024 * 1024
highest = lax.Precision.HIGHEST
f32 = jnp.float32
bf16 = jnp.bfloat16

NB = 8


def mm(a, b):
    return lax.dot_general(a, b, (((1,), (0,)), ((), ())), preferred_element_type=f32)


def mm_nt(a, b):
    return lax.dot_general(a, b, (((1,), (1,)), ((), ())), preferred_element_type=f32)


def mm_tn(a, b):
    return lax.dot_general(a, b, (((0,), (0,)), ((), ())), preferred_element_type=f32)


def moments(v):
    average = jnp.mean(v, axis=-1, keepdims=True)
    centered = v - average
    variance = jnp.mean(centered * centered, axis=-1, keepdims=True)
    inv = lax.rsqrt(variance + EPS)
    return centered * inv, inv


def ln_back(e, xhat, inv):
    return (e - jnp.mean(e, -1, keepdims=True) - xhat * jnp.mean(e * xhat, -1, keepdims=True)) * inv


def start_blocks(slots_ref, pieces, layout, w_ref, sem, low=None):
    i = 0
    for piece, first, count in layout:
        for t in range(count):
            slot = slots_ref[i]
            if low is None:
                pltpu.make_async_copy(pieces[piece].at[first + t], w_ref.at[slot], sem.at[slot]).start()
            else:

                @pl.when(slot >= low)
                def _(piece=piece, at=first + t, slot=slot):
                    place = slot - low
                    pltpu.make_async_copy(pieces[piece].at[at], w_ref.at[place], sem.at[place]).start()

            i += 1


def start_wide(slots_ref, pieces, layout, w_ref, sem):
    width = w_ref.shape[0]
    b = width // NB
    i = 0
    for piece, first, count in layout:
        for t in range(count):
            slot = slots_ref[i]
            row = pl.multiple_of(lax.rem(slot, NB) * b, b)
            column = pl.multiple_of(slot // NB * width, width)
            place = w_ref.at[pl.ds(row, b), pl.ds(column, width)]
            pltpu.make_async_copy(pieces[piece].at[first + t], place, sem.at[slot]).start()
            i += 1


def wait_wide(w_ref, sem):
    width = w_ref.shape[0]
    b = width // NB
    place = w_ref.at[pl.ds(0, b), pl.ds(0, width)]
    for slot in range(32):
        pltpu.make_async_copy(place, place, sem.at[slot]).wait()


def wait_blocks(w_ref, sem, first, count):
    def one(t, carry):
        pltpu.make_async_copy(w_ref.at[first + t], w_ref.at[first + t], sem.at[first + t]).wait()
        return carry

    lax.fori_loop(0, count, one, 0)


def load_blocks(slots_ref, pieces, layout, w_ref, sem):
    start_blocks(slots_ref, pieces, layout, w_ref, sem)
    wait_blocks(w_ref, sem, 0, 32)


def square(w_ref, j):
    part = w_ref[NB * j : NB * (j + 1)]
    return part.reshape(part.shape[0] * part.shape[1], part.shape[2])


def send_blocks(gpos_ref, spots, buf_ref, even_rows, odd_rows, b, outs, sem):
    core = gpos_ref[16]
    keep_out, keep_own, send_out, send_own = outs
    for t, at in enumerate(spots):
        place = gpos_ref[at]
        idx = lax.rem(place, 8)
        for parity, row in ((0, even_rows[t]), (1, odd_rows[t])):
            for kept in (True, False):
                for low in (True, False):
                    ref = (keep_out if low else keep_own) if kept else (send_out if low else send_own)
                    mine = (core == parity) if kept else (core != parity)
                    region = (place < 8) if low else (place >= 8)

                    @pl.when(mine & region)
                    def _(ref=ref, row=row, idx=idx, which=2 * t + parity):
                        pltpu.make_async_copy(buf_ref.at[pl.ds(row, b)], ref.at[idx], sem.at[which]).start()


def drain_blocks(buf_ref, b, sem):
    for t in range(8):
        pltpu.make_async_copy(buf_ref.at[pl.ds(0, b)], buf_ref.at[pl.ds(0, b)], sem.at[t]).wait()


def half_mask(rows, width):
    lane = lax.broadcasted_iota(jnp.int32, (rows, width), 1)
    return lane < HD


def both(x2, first):
    zero = jnp.zeros_like(x2)
    return jnp.concatenate([jnp.where(first, x2, zero), jnp.where(first, zero, x2)], axis=0)


def residual_of(tok_ref, emb_ref, step, rb, length):
    parts = []
    for r in range(rb):
        rows = tok_ref[r * length : (r + 1) * length].astype(f32)
        parts.append(rows + emb_ref[pl.ds(step * rb + r, 1), :])
    return jnp.concatenate(parts, axis=0) if rb > 1 else parts[0]


def f1_kernel(layout, rb, length, slots, tok_ref, emb_ref, seg_ref, pad_ref, vec_ref, *rest):
    n = max(l[0] for l in layout) + 1
    pieces = rest[:n]
    normed_ref, triple_ref, att_ref, attended_ref, middle_ref, n2_ref, w_ref, sem = rest[n:]
    step = pl.program_id(0)

    @pl.when(step == 0)
    def _():
        load_blocks(slots, pieces, layout, w_ref, sem)

    x = residual_of(tok_ref, emb_ref, step, rb, length)
    xhat, _inv = moments(x)
    normed = (xhat * vec_ref[3:4, :] + vec_ref[4:5, :]).astype(bf16)
    normed_ref[...] = normed
    width = normed.shape[1]
    for q, row in ((0, 0), (1, None), (2, 1)):
        t = mm(normed, square(w_ref, q))
        if row is not None:
            t = t + vec_ref[row : row + 1, :]
        triple_ref[q] = t.astype(bf16)
    eye = lax.broadcasted_iota(jnp.int32, (length, length), 0) == lax.broadcasted_iota(
        jnp.int32, (length, length), 1
    )
    first = half_mask(length, 2 * HD)
    masks = []
    for r in range(rb):
        seg = jnp.broadcast_to(seg_ref[pl.ds(step * rb + r, 1), :], (length, length))
        pad = jnp.broadcast_to(pad_ref[pl.ds(step * rb + r, 1), :], (length, length))
        allowed = (seg == seg.T) & ((pad == 0.0) | eye)
        allowed = jnp.where(allowed, 1.0, 0.0)
        masks.append(jnp.concatenate([allowed, allowed], axis=0) > 0.5)
    pairs = width // (2 * HD)
    every = [(r, hp) for r in range(rb) for hp in range(pairs)]
    for start in range(0, len(every), 12):
        some = []
        for r, hp in every[start : start + 12]:
            rows = slice(r * length, (r + 1) * length)
            lanes = slice(hp * 2 * HD, (hp + 1) * 2 * HD)
            s = mm_nt(both(triple_ref[0, rows, lanes], first), triple_ref[1, rows, lanes]) * SCALE
            some.append((r, hp, rows, lanes, jnp.where(masks[r], s, MASKED)))
        done = []
        for r, hp, rows, lanes, s in some:
            e = jnp.exp(s - jnp.max(s, axis=-1, keepdims=True))
            p = (e / jnp.sum(e, axis=-1, keepdims=True)).astype(bf16)
            att_ref[r * pairs + hp] = p
            done.append((rows, lanes, p))
        for rows, lanes, p in done:
            wide = jnp.concatenate([p[:length], p[length:]], axis=1)
            attended_ref[rows, lanes] = mm(wide, both(triple_ref[2, rows, lanes], first)).astype(bf16)
    branch = mm(attended_ref[...], square(w_ref, 3)) + vec_ref[2:3, :]
    middle = x + branch
    middle_ref[...] = middle
    xhat2, _inv2 = moments(middle)
    n2_ref[...] = (xhat2 * vec_ref[5:6, :] + vec_ref[6:7, :]).astype(bf16)


def gelu_rows(h_ref, bias, active_ref, gp_ref, first, count):
    sub = 32
    for m in range(count // sub):
        at = slice(first + m * sub, first + (m + 1) * sub)
        v = h_ref[at] + bias
        v2 = v * v
        w = GELU_C * v
        cubic = w * v2
        t = jnp.tanh(w + cubic * GELU_A)
        half = 0.5 * t + 0.5
        active_ref[at] = (v * half).astype(bf16)
        steep = w + cubic * (3.0 * GELU_A)
        gp_ref[at] = (half + (half - half * t) * steep).astype(bf16)


def f2_kernel(layout, slots, gpos, n2_ref, cot_hbm, hb_ref, *rest):
    n = max(l[0] for l in layout) + 1
    pieces = rest[:n]
    active_ref, gp_ref = rest[n : n + 2]
    outs = rest[n + 2 : n + 6]
    w_ref, h_ref, g_ref, cot_ref, sem, cot_sem, out_sem = rest[n + 6 :]
    j = pl.program_id(0)
    load = pltpu.make_async_copy(cot_hbm, cot_ref, cot_sem)

    @pl.when(j == 0)
    def _():
        start_blocks(slots, pieces, layout, w_ref, sem)
        load.start()

    wait_blocks(w_ref, sem, j * NB, NB)
    tokens, width = n2_ref.shape
    b = width // NB
    bias = hb_ref[pl.ds(j, 1), :]
    slot = lax.rem(j, 2)

    @pl.when(j >= 2)
    def _():
        drain_blocks(g_ref.at[slot], b, out_sem.at[slot])

    part = w_ref[pl.ds(j * NB, NB)].reshape(width, width)
    half = tokens // 2
    h_ref[:half] = mm(n2_ref[:half], part)
    h_ref[half:] = mm(n2_ref[half:], part)
    gelu_rows(h_ref, bias, active_ref, gp_ref, 0, half)
    gelu_rows(h_ref, bias, active_ref, gp_ref, half, half)

    @pl.when(j == 0)
    def _():
        load.wait()

    g_ref[slot] = mm_tn(active_ref[...], cot_ref[...]).astype(bf16)
    spots = [q * 4 + j for q in range(4)]
    even_rows, odd_rows = [q * b for q in range(4)], [(4 + q) * b for q in range(4)]
    send_blocks(gpos, spots, g_ref.at[slot], even_rows, odd_rows, b, outs, out_sem.at[slot])

    @pl.when(j == 3)
    def _():
        drain_blocks(g_ref.at[0], b, out_sem.at[0])
        drain_blocks(g_ref.at[1], b, out_sem.at[1])


def b1_kernel(layout, chunk, slots, gpos, n2_ref, cot_ref, gp_ref, *rest):
    n = max(l[0] for l in layout) + 1
    pieces = rest[:n]
    dh_ref, hb_ref, db_ref = rest[n : n + 3]
    outs = rest[n + 3 : n + 7]
    w_ref, h_ref, g_ref, sem, out_sem = rest[n + 7 :]
    j = pl.program_id(0)
    tokens, width = n2_ref.shape
    b = width // NB
    slot = lax.rem(j, 2)

    @pl.when(j == 0)
    def _():
        start_blocks(slots, pieces, layout, w_ref, sem)
        db_ref[...] = jnp.zeros_like(db_ref)
        db_ref[0:1] = jnp.sum(cot_ref[...].astype(f32), axis=0, keepdims=True)
        hb_ref[...] = jnp.zeros_like(hb_ref)

    wait_blocks(w_ref, sem, j * NB, NB)
    w = w_ref[pl.ds(j * NB, NB)].reshape(width, width)
    sub = 32
    total = jnp.zeros((8, width), f32)
    for m in range(tokens // chunk):
        h_ref[m] = mm_nt(cot_ref[m * chunk : (m + 1) * chunk], w)
    for m in range(tokens // chunk):
        for s in range(chunk // sub):
            at = slice(m * chunk + s * sub, m * chunk + (s + 1) * sub)
            dh = (h_ref[m, s * sub : (s + 1) * sub] * gp_ref[at].astype(f32)).astype(bf16)
            dh_ref[at] = dh
            total = total + jnp.sum(dh.astype(f32).reshape(sub // 8, 8, width), axis=0)
    hb_ref[pl.ds(j, 1), :] = jnp.sum(total, axis=0, keepdims=True)

    @pl.when(j >= 2)
    def _():
        drain_blocks(g_ref.at[slot], b, out_sem.at[slot])

    g_ref[slot] = mm_tn(n2_ref[...], dh_ref[...]).astype(bf16)
    spots = [j * 4 + zf for zf in range(4)]
    even_rows, odd_rows = [2 * zf * b for zf in range(4)], [(2 * zf + 1) * b for zf in range(4)]
    send_blocks(gpos, spots, g_ref.at[slot], even_rows, odd_rows, b, outs, out_sem.at[slot])

    @pl.when(j == 3)
    def _():
        drain_blocks(g_ref.at[0], b, out_sem.at[0])
        drain_blocks(g_ref.at[1], b, out_sem.at[1])


def b2_kernel(
    layout_a, layout_b, rb, length, slots_a, slots_b,
    dh_ref, cot_ref, middle_ref, vec_ref, triple_ref, att_ref, *rest
):
    na = max(l[0] for l in layout_a) + 1
    nb = max(l[0] for l in layout_b) + 1
    pieces_a, pieces_b, rest = rest[:na], rest[na : na + nb], rest[na + nb :]
    dmid_ref, dbr_ref, dt_ref, sums_ref, wo_ref, wb_ref, datt_ref, sem_a, sem_b = rest
    width = cot_ref.shape[1]
    b = width // NB

    @pl.when(pl.program_id(0) == 0)
    def _():
        start_wide(slots_b, pieces_b, layout_b, wb_ref, sem_b)
        start_blocks(slots_a, pieces_a, layout_a, wo_ref, sem_a, 3 * NB)
        sums_ref[...] = jnp.zeros_like(sums_ref)
        wait_wide(wb_ref, sem_b)
        wait_blocks(wo_ref, sem_a, 0, NB)

    d_n2 = mm_nt(dh_ref[...], wb_ref[...])
    xhat, inv = moments(middle_ref[...])
    sums_ref[0:1] += jnp.sum(d_n2 * xhat, axis=0, keepdims=True)
    sums_ref[1:2] += jnp.sum(d_n2, axis=0, keepdims=True)
    d_middle = cot_ref[...].astype(f32) + ln_back(d_n2 * vec_ref[5:6, :], xhat, inv)
    dmid_ref[...] = d_middle
    d_branch = d_middle.astype(bf16)
    dbr_ref[...] = d_branch
    sums_ref[2:3] += jnp.sum(d_branch.astype(f32), axis=0, keepdims=True)

    datt_ref[...] = mm_nt(d_branch, wo_ref[...].reshape(width, width)).astype(bf16)
    first = half_mask(length, 2 * HD)
    pairs = width // (2 * HD)
    every = [(r, hp) for r in range(rb) for hp in range(pairs)]
    for start in range(0, len(every), 12):
        some = []
        for r, hp in every[start : start + 12]:
            rows = slice(r * length, (r + 1) * length)
            lanes = slice(hp * 2 * HD, (hp + 1) * 2 * HD)
            dos = both(datt_ref[rows, lanes], first)
            some.append((rows, lanes, dos, att_ref[r * pairs + hp], mm_nt(dos, triple_ref[2, rows, lanes])))
        slopes = []
        for rows, lanes, dos, p_low, d_a in some:
            dt_ref[2, rows, lanes] = mm_tn(p_low, dos).astype(bf16)
            p = p_low.astype(f32)
            inner = jnp.sum(p * d_a, axis=-1, keepdims=True)
            slopes.append((p * (d_a - inner)).astype(bf16))
        for (rows, lanes, dos, p_low, d_a), ds in zip(some, slopes):
            wide = jnp.concatenate([ds[:length], ds[length:]], axis=1)
            dt_ref[0, rows, lanes] = (mm(wide, both(triple_ref[1, rows, lanes], first)) * SCALE).astype(bf16)
            dt_ref[1, rows, lanes] = (mm_tn(ds, both(triple_ref[0, rows, lanes], first)) * SCALE).astype(bf16)
    sums_ref[3:4] += jnp.sum(dt_ref[0].astype(f32), axis=0, keepdims=True)
    sums_ref[4:5] += jnp.sum(dt_ref[2].astype(f32), axis=0, keepdims=True)


def ga_kernel(gpos, normed_ref, dt_ref, attended_hbm, dbr_hbm, *rest):
    outs = rest[:4]
    attended_ref, dbr_ref, g_ref, in_sem, out_sem = rest[4:]
    j = pl.program_id(0)
    width = normed_ref.shape[1]
    b = width // NB
    slot = lax.rem(j, 2)
    loads = [
        pltpu.make_async_copy(attended_hbm, attended_ref, in_sem.at[0]),
        pltpu.make_async_copy(dbr_hbm, dbr_ref, in_sem.at[1]),
    ]

    @pl.when(j == 0)
    def _():
        for cp in loads:
            cp.start()

    @pl.when(j >= 2)
    def _():
        drain_blocks(g_ref.at[slot], b, out_sem.at[slot])

    @pl.when(j < 3)
    def _():
        g_ref[slot] = mm_tn(normed_ref[...], dt_ref[...]).astype(bf16)

    @pl.when(j == 3)
    def _():
        for cp in loads:
            cp.wait()
        g_ref[slot] = mm_tn(attended_ref[...], dbr_ref[...]).astype(bf16)

    spots = [j * 4 + zf for zf in range(4)]
    even_rows, odd_rows = [2 * zf * b for zf in range(4)], [(2 * zf + 1) * b for zf in range(4)]
    send_blocks(gpos, spots, g_ref.at[slot], even_rows, odd_rows, b, outs, out_sem.at[slot])

    @pl.when(j == 3)
    def _():
        drain_blocks(g_ref.at[0], b, out_sem.at[0])
        drain_blocks(g_ref.at[1], b, out_sem.at[1])


def b4_kernel(layout, rb, length, slots, tok_ref, emb_ref, dmid_ref, dt_ref, vec_ref, sums2_ref, db_ref, *rest):
    n = max(l[0] for l in layout) + 1
    pieces = rest[:n]
    ig_ref, sums_ref, w_ref, sem = rest[n:]
    base = pl.num_programs(0) * rb
    step = pl.program_id(0)

    @pl.when(step == 0)
    def _():
        load_blocks(slots, pieces, layout, w_ref, sem)
        sums_ref[...] = jnp.zeros_like(sums_ref)
        sums_ref[pl.ds(base + 2, 5)] = sums2_ref[0:5]
        sums_ref[pl.ds(base + 7, 1)] = db_ref[0:1]

    d_n = mm_nt(dt_ref[0], square(w_ref, 0))
    for q in range(1, 3):
        d_n = d_n + mm_nt(dt_ref[q], square(w_ref, q))
    xhat, inv = moments(residual_of(tok_ref, emb_ref, step, rb, length))
    sums_ref[pl.ds(base, 1)] += jnp.sum(d_n * xhat, axis=0, keepdims=True)
    sums_ref[pl.ds(base + 1, 1)] += jnp.sum(d_n, axis=0, keepdims=True)
    d_start = dmid_ref[...] + ln_back(d_n * vec_ref[3:4, :], xhat, inv)
    ig_ref[...] = d_start.astype(bf16)
    for r in range(rb):
        sums_ref[pl.ds(step * rb + r, 1), :] = jnp.sum(d_start[r * length : (r + 1) * length], axis=0, keepdims=True)


def f3_kernel(layout, slots, act_ref, middle_ref, vec_ref, *rest):
    n = max(l[0] for l in layout) + 1
    pieces = rest[:n]
    out_ref, w_ref, sem = rest[n:]

    @pl.when(pl.program_id(0) == 0)
    def _():
        load_blocks(slots, pieces, layout, w_ref, sem)

    width = middle_ref.shape[1]
    acc = mm(act_ref[...], w_ref[...].reshape(4 * width, width))
    out_ref[...] = (middle_ref[...] + (acc + vec_ref[7:8, :])).astype(bf16)


def sds(shape, dtype):
    return jax.ShapeDtypeStruct(shape, dtype)


def full(shape):
    zeros = (0,) * len(shape)
    return pl.BlockSpec(shape, lambda i: zeros)


smem = pl.BlockSpec(memory_space=pltpu.SMEM)
hbm = pl.BlockSpec(memory_space=pl.ANY)


def call(kernel, grid, in_specs, out_shape, out_specs, scratch, flops, nbytes, args):
    return pl.pallas_call(
        kernel,
        grid=grid,
        in_specs=in_specs,
        out_shape=out_shape,
        out_specs=out_specs,
        scratch_shapes=scratch,
        compiler_params=pltpu.CompilerParams(
            dimension_semantics=("arbitrary",), vmem_limit_bytes=VMEM_LIMIT
        ),
        cost_estimate=pl.CostEstimate(flops=flops, bytes_accessed=nbytes, transcendentals=0),
    )(*args)


class Group:
    def __init__(self, arrays, layout, slots):
        self.arrays, self.layout, self.slots = arrays, layout, slots


def compute_f1(tok, emb, seg, pad, vecs, group, rows, length):
    n, width = tok.shape
    rb = 2 if rows % 2 == 0 else 1
    block = rb * length
    pairs = width // (2 * HD)
    b = width // NB
    return call(
        functools.partial(f1_kernel, group.layout, rb, length),
        (rows // rb,),
        [smem, pl.BlockSpec((block, width), lambda i: (i, 0)), full(emb.shape), full(seg.shape), full(pad.shape), full(vecs.shape)]
        + [hbm] * len(group.arrays),
        [sds((n, width), bf16), sds((3, n, width), bf16), sds((rows * pairs, 2 * length, length), bf16),
         sds((n, width), bf16), sds((n, width), f32), sds((n, width), bf16)],
        [pl.BlockSpec((block, width), lambda i: (i, 0)), pl.BlockSpec((3, block, width), lambda i: (0, i, 0)),
         pl.BlockSpec((rb * pairs, 2 * length, length), lambda i: (i, 0, 0)),
         pl.BlockSpec((block, width), lambda i: (i, 0)), pl.BlockSpec((block, width), lambda i: (i, 0)),
         pl.BlockSpec((block, width), lambda i: (i, 0))],
        [pltpu.VMEM((32, b, width), bf16), pltpu.SemaphoreType.DMA((32,))],
        2 * n * width * width * 4 * 3, 20 << 20,
        [group.slots, tok, emb, seg, pad, vecs, *group.arrays],
    )


def compute_f2(n2, cot, hb, group, gpos):
    n, width = n2.shape
    b = width // NB
    column = pl.BlockSpec((n, width), lambda i: (0, i))
    return call(
        functools.partial(f2_kernel, group.layout),
        (4,),
        [smem, smem, full(n2.shape), hbm, full(hb.shape)] + [hbm] * len(group.arrays),
        [sds((n, 4 * width), bf16), sds((n, 4 * width), bf16), *[sds((8, b, width), bf16)] * 4],
        [column, column, hbm, hbm, hbm, hbm],
        [pltpu.VMEM((32, b, width), bf16), pltpu.VMEM((n, width), f32), pltpu.VMEM((2, width, width), bf16), pltpu.VMEM((n, width), bf16),
         pltpu.SemaphoreType.DMA((32,)), pltpu.SemaphoreType.DMA(()), pltpu.SemaphoreType.DMA((2, 8))],
        2 * n * width * width * 8 * 2, 20 << 20,
        [group.slots, gpos, n2, cot, hb, *group.arrays],
    )


def compute_b1(n2, cot, gp, group, gpos):
    n, width = n2.shape
    b = width // NB
    chunk = n // 2 if n % 64 == 0 else n
    column = pl.BlockSpec((n, width), lambda i: (0, i))
    return call(
        functools.partial(b1_kernel, group.layout, chunk),
        (4,),
        [smem, smem, full(n2.shape), full(cot.shape), column] + [hbm] * len(group.arrays),
        [sds((n, 4 * width), bf16), sds((4, width), f32), sds((8, width), f32), *[sds((8, b, width), bf16)] * 4],
        [column, full((4, width)), full((8, width)), hbm, hbm, hbm, hbm],
        [pltpu.VMEM((32, b, width), bf16), pltpu.VMEM((n // chunk, chunk, width), f32), pltpu.VMEM((2, width, width), bf16),
         pltpu.SemaphoreType.DMA((32,)), pltpu.SemaphoreType.DMA((2, 8))],
        2 * n * width * width * 8 * 2, 20 << 20,
        [group.slots, gpos, n2, cot, gp, *group.arrays],
    )


def compute_b2(dh, cot, middle, vecs, triple, att, ga, gb, rows, length):
    n, width = cot.shape
    rb = 2 if rows % 2 == 0 else 1
    block = rb * length
    pairs = width // (2 * HD)
    b = width // NB
    tile = pl.BlockSpec((block, width), lambda i: (i, 0))
    wide = pl.BlockSpec((3, block, width), lambda i: (0, i, 0))
    return call(
        functools.partial(b2_kernel, ga.layout, gb.layout, rb, length),
        (rows // rb,),
        [smem, smem, pl.BlockSpec((block, 4 * width), lambda i: (i, 0)), tile, tile, full(vecs.shape), wide,
         pl.BlockSpec((rb * pairs, 2 * length, length), lambda i: (i, 0, 0))]
        + [hbm] * (len(ga.arrays) + len(gb.arrays)),
        [sds((n, width), f32), sds((n, width), bf16), sds((3, n, width), bf16), sds((8, width), f32)],
        [tile, tile, wide, full((8, width))],
        [pltpu.VMEM((NB, b, width), bf16), pltpu.VMEM((width, 4 * width), bf16), pltpu.VMEM((block, width), bf16),
         pltpu.SemaphoreType.DMA((NB,)), pltpu.SemaphoreType.DMA((32,))],
        2 * n * width * width * 10, 30 << 20,
        [ga.slots, gb.slots, dh, cot, middle, vecs, triple, att, *ga.arrays, *gb.arrays],
    )


def compute_ga(normed, attended, dt, dbr, gpos):
    n, width = normed.shape
    b = width // NB
    return call(
        ga_kernel,
        (4,),
        [smem, full(normed.shape), pl.BlockSpec((None, n, width), lambda i: (jnp.minimum(i, 2), 0, 0)), hbm, hbm],
        [*[sds((8, b, width), bf16)] * 4],
        [hbm, hbm, hbm, hbm],
        [pltpu.VMEM((n, width), bf16), pltpu.VMEM((n, width), bf16), pltpu.VMEM((2, width, width), bf16),
         pltpu.SemaphoreType.DMA((2,)), pltpu.SemaphoreType.DMA((2, 8))],
        2 * n * width * width * 4 * 2, 12 << 20,
        [gpos, normed, dt, attended, dbr],
    )


def compute_b4(tok, emb, dmid, dt, vecs, sums2, db_sum, group, rows, length):
    n, width = tok.shape
    rb = 2 if rows % 2 == 0 else 1
    block = rb * length
    b = width // NB
    lines = 8 * ((rows + 8 + 7) // 8)
    return call(
        functools.partial(b4_kernel, group.layout, rb, length),
        (rows // rb,),
        [smem, pl.BlockSpec((block, width), lambda i: (i, 0)), full(emb.shape), pl.BlockSpec((block, width), lambda i: (i, 0)),
         pl.BlockSpec((3, block, width), lambda i: (0, i, 0)), full(vecs.shape), full(sums2.shape), full(db_sum.shape)]
        + [hbm] * len(group.arrays),
        [sds((n, width), bf16), sds((lines, width), f32)],
        [pl.BlockSpec((block, width), lambda i: (i, 0)), full((lines, width))],
        [pltpu.VMEM((32, b, width), bf16), pltpu.SemaphoreType.DMA((32,))],
        2 * n * width * width * 3 * 2, 12 << 20,
        [group.slots, tok, emb, dmid, dt, vecs, sums2, db_sum, *group.arrays],
    )


def compute_f3(active, middle, vecs, group):
    n, width = middle.shape
    b = width // NB
    block = 256 if n % 256 == 0 else n
    return call(
        functools.partial(f3_kernel, group.layout),
        (n // block,),
        [smem, pl.BlockSpec((block, 4 * width), lambda i: (i, 0)), pl.BlockSpec((block, width), lambda i: (i, 0)), full(vecs.shape)]
        + [hbm] * len(group.arrays),
        sds((n, width), bf16),
        pl.BlockSpec((block, width), lambda i: (i, 0)),
        [pltpu.VMEM((32, b, width), bf16), pltpu.SemaphoreType.DMA((32,))],
        2 * n * width * width * 4 * 2, 12 << 20,
        [group.slots, active, middle, vecs, *group.arrays],
    )


def plain_groups(own_a, own_b, own_c, small):
    width = own_a.shape[2]
    slots = jnp.arange(32, dtype=jnp.int32)

    def group(whole):
        return Group([whole.reshape(32, width // NB, width)], [(0, 0, 32)], slots)

    a = lax.all_gather(own_a, "fsdp", axis=1, tiled=True)
    b = lax.all_gather(own_b, "fsdp", axis=1, tiled=True)
    c = lax.all_gather(own_c, "fsdp", axis=0, tiled=True)
    vec = [lax.all_gather(v, "fsdp", axis=0, tiled=True) for v in small]
    return group(a), group(b), group(c), jnp.stack(vec[:8]).astype(f32), vec[8].astype(f32).reshape(4, width)


def plain_scatter(keep_out, keep_own, send_out, send_own, rows_first=False):
    b, width = keep_out.shape[1:]
    g = [jnp.concatenate(v, axis=0).reshape(4, 4, b, width) for v in ((keep_out, keep_own), (send_out, send_own))]
    g = jnp.stack(g, axis=2).astype(f32)
    if rows_first:
        g = g.transpose(1, 2, 0, 3, 4).reshape(32 * b, width)
        return lax.psum(lax.psum_scatter(g, "fsdp", scatter_dimension=0, tiled=True), "dp")
    g = g.reshape(4, NB * b, width)
    return lax.psum(lax.psum_scatter(g, "fsdp", scatter_dimension=1, tiled=True), "dp")


def pick(stacked, i):
    return lax.dynamic_index_in_dim(stacked, i, axis=0, keepdims=False)


def xor_perm(n, k):
    return [(i, i ^ k) for i in range(n)]


def core_swap(v):
    return lax.ppermute(v, "fsdp", xor_perm(8, 1))


def x_swap(v):
    return lax.ppermute(v, "dp", xor_perm(4, 1))


def y_swap(v):
    return lax.ppermute(v, "dp", xor_perm(4, 2))


def diagonal_swap(v):
    return lax.ppermute(v, "dp", xor_perm(4, 3))


def z_shift(v, k):
    return lax.ppermute(v, "fsdp", [(i, (i + 2 * k) % 8) for i in range(8)])


def tie(values, after):
    return lax.optimization_barrier((values, after))[0]


def columns(v):
    return lax.all_to_all(jnp.broadcast_to(v[None], (4,) + v.shape), "dp", 0, 0, tiled=True)


quarter_major = [(e, 4 * q, 4) for q in range(4) for e in (0, 1)]


def grad_place(delta, k):
    half, high, low = k // 2, delta // 2, lax.rem(delta, 2)
    leaves, other = jnp.where(half == 0, low, high), jnp.where(half == 0, high, low)
    return (1 - leaves) * 8 + half * 4 + other * 2 + lax.rem(k, 2)


def fast_slots(z, c):
    table = []
    for q in range(4):
        for e in (0, 1):
            for k in range(4):
                table.append(q * NB + 2 * lax.rem(z - k + 4, 4) + (c ^ e))
    return jnp.stack(table).astype(jnp.int32)


def along_z(v):
    return [v] + [z_shift(v, k) for k in (1, 2, 3)]


def rows_of(got, first, count):
    return jnp.stack([g[first : first + count] for g in got])


def down_slots(z, c, quarters_in):
    table = []
    for e in (0, 1):
        for part in quarters_in:
            for k in range(4):
                table += [8 * lax.rem(z - k + 4, 4) + 4 * (c ^ e) + q for q in part]
    return jnp.stack(table).astype(jnp.int32)


def shard_order(e0, e1, z, c):
    pair = jnp.stack([jnp.where(c == 0, e0, e1), jnp.where(c == 0, e1, e0)], axis=1)
    got = jnp.stack([pick(pair, lax.rem(z - i + 4, 4)) for i in range(4)])
    return got.reshape((8,) + got.shape[2:])


def fast_small(got, width, rows):
    got = got.astype(f32)
    vecs = got[:, :8, : width // 8].transpose(1, 0, 2).reshape(8, width)
    hb = got[:, 8, : width // 2].reshape(4, width)
    ids = (got[:, 9, :rows] * 32.0 + got[:, 10, :rows]).astype(jnp.int32)
    return vecs, hb, ids


def plus(*values):
    return sum(v.astype(f32) for v in values).astype(bf16)


class Scatter:
    def __init__(self, keep_out, keep_own, send_out, send_own):
        self.keep = (keep_out, keep_own)
        self.got = (core_swap(send_out), core_swap(send_own))

    def split(self):
        self.out = [plus(self.keep[0][4 * i : 4 * i + 4], self.got[0][4 * i : 4 * i + 4]) for i in range(2)]

    def one(self):
        self.r1 = [x_swap(self.out[0]), y_swap(self.out[1])]

    def add_two(self):
        at = [slice(4 * i + 2, 4 * i + 4) for i in range(2)]
        self.on = [plus(self.keep[1][at[i]], self.got[1][at[i]], self.r1[i][2:]) for i in range(2)]

    def send_two(self):
        self.r2 = [y_swap(self.on[0]), x_swap(self.on[1])]

    def two(self):
        self.add_two()
        self.send_two()

    def three(self, after=()):
        at = [slice(4 * i, 4 * i + 2) for i in range(2)]
        halves = [plus(self.keep[1][at[i]], self.got[1][at[i]], self.r1[i][:2], self.r2[i]) for i in range(2)]
        self.h3 = [halves[k // 2][k % 2] for k in range(4)]
        last = tie(self.h3[1], after) if after else self.h3[1]
        self.r3 = [self.h3[0], z_shift(last, 1), z_shift(self.h3[2], 2), z_shift(self.h3[3], 3)]

    def total(self):
        return sum(p.astype(f32) for p in self.r3).astype(bf16)


def spread(mine):
    return [mine, x_swap(mine), y_swap(mine), diagonal_swap(mine)]


def quarters(got, d):
    got = jnp.stack(got)
    return [pick(got, d ^ q).astype(f32) for q in range(4)]


def per_device(
    fast, tokens, timesteps, segments, padding, cotangent, step_table,
    triple_weight, query_bias, value_bias, output_weight, output_bias,
    first_gain, first_shift, second_gain, second_shift,
    hidden_weight, hidden_bias, down_weight, down_bias,
):
    micro, local_rows, length, width = tokens.shape
    rows = micro * local_rows
    n = rows * length
    nd, nf = lax.axis_size("dp"), lax.axis_size("fsdp")
    d, f = lax.axis_index("dp"), lax.axis_index("fsdp")
    z, c = f // 2, lax.rem(f, 2)
    tok = tokens.reshape(n, width)
    cot = cotangent.reshape(n, width)
    seg = segments.reshape(rows, length).astype(f32)
    pad = padding.reshape(rows, length).astype(f32)

    ids = timesteps.reshape(rows)
    marks = jnp.broadcast_to(ids.astype(f32)[None, :], (nf, rows))
    steps = lax.iota(jnp.int32, step_table.shape[0])
    q4 = [triple_weight[:, i * width : (i + 1) * width] for i in range(3)] + [output_weight]
    h4 = [hidden_weight[:, i * width : (i + 1) * width] for i in range(4)]
    vec_args = (query_bias, value_bias, output_bias, first_gain, first_shift, second_gain, second_shift, down_bias)
    if fast:
        b = width // NB
        own_a = pick(jnp.stack(q4), d)
        own_b = pick(jnp.stack(h4), d)
        small = jnp.zeros((16, width), bf16)
        small = small.at[:8, : width // nf].set(jnp.stack(vec_args))
        small = small.at[8, : 4 * width // nf].set(hidden_bias)
        small = small.at[9:11, :rows].set(jnp.stack([ids // 32, lax.rem(ids, 32)]).astype(bf16))
        got = along_z(jnp.concatenate([own_a, small], axis=0))
        s0 = rows_of(got, 0, b)
        e0 = rows_of(got, b, 16)
        mine_a = columns(s0)
        got1 = along_z(tie(jnp.concatenate([own_b, down_weight[:b]], axis=0), got))
        vecs, hb, here = fast_small(shard_order(e0, core_swap(e0), z, c), width, rows)
        gpos = [grad_place(q ^ d, lax.rem(zf - z + 4, 4)) for q in range(4) for zf in range(4)] + [c]
        gpos = jnp.stack(gpos).astype(jnp.int32)
        slots = fast_slots(z, c)
        slots_c = down_slots(z, c, ((0,), (1, 2), (3,)))
    else:
        ga, gb, gc, vecs, hb = plain_groups(
            jnp.stack(q4), jnp.stack(h4), down_weight, vec_args + (hidden_bias,)
        )
        gpos = jnp.concatenate([jnp.arange(16, dtype=jnp.int32), jnp.zeros((1,), jnp.int32)])
        here = lax.all_gather(ids, "fsdp", axis=0, tiled=True)

    onehot = (here.reshape(nf * rows)[:, None] == steps[None, :]).astype(bf16)
    looked = jnp.dot(onehot, step_table, preferred_element_type=f32).astype(bf16)
    if fast:
        looked, seg, pad, vecs, hb, gpos, slots, slots_c, marks, own_c12 = lax.optimization_barrier(
            (looked.reshape(rows, width), seg, pad, vecs, hb, gpos, slots, slots_c, marks, down_weight[b : 3 * b])
        )
        sent = jnp.pad(looked, ((0, 16 - rows), (0, 0)))
        got_e = [sent, z_shift(sent, 1), z_shift(sent, 2), z_shift(tie(sent, got1[3]), 3)]
        got_e = jnp.stack(got_e)
        mine_a, got1, got_e = lax.optimization_barrier((mine_a, got1, got_e))
        emb = shard_order(got_e, core_swap(got_e), z, c)[:, :rows].reshape(nf, nf, rows, width // nf)
        emb = pick(emb.transpose(1, 0, 2, 3), f)
    else:
        emb = lax.all_to_all(looked.reshape(nf, rows, width // nf), "fsdp", 0, 0, tiled=True)
    emb = emb.transpose(1, 0, 2).reshape(rows, width).astype(f32)

    if fast:
        flat = (16, b, width)
        mine_a = mine_a.reshape(flat)
        core_a = core_swap(mine_a)
        ga = Group([mine_a, core_a], quarter_major, slots)
        mine_b = columns(rows_of(got1, 0, b))
        c0 = rows_of(got1, b, b)
        got2 = along_z(tie(own_c12, got1))
        tok_in = tie(tok, (core_a, emb))
    else:
        tok_in = tok
    normed, triple, att, attended, middle, n2 = compute_f1(tok_in, emb, seg, pad, vecs, ga, rows, length)
    if fast:
        c0x = core_swap(c0)
        mine_b, n2, got2, c0x = lax.optimization_barrier((mine_b.reshape(flat), n2, got2, c0x))
        core_b = core_swap(mine_b)
        gb = Group([mine_b, core_b], quarter_major, slots)
        got3 = along_z(tie(down_weight[3 * b :], got2))
        c12 = jnp.stack(got2).reshape(8, b, width)
        n2, c12 = tie((n2, c12), core_b)
        c12x = core_swap(c12)
    active, gp, *grads_c = compute_f2(n2, cot, hb, gb, gpos)
    if fast:
        got3, c0x, c12x, gp, grads_c = lax.optimization_barrier((got3, c0x, c12x, gp, grads_c))
        c3 = jnp.stack(got3)
        gc = Group(
            [c0, c12, c3, c0x, c12x, core_swap(c3)],
            [(0, 0, 4), (1, 0, 8), (2, 0, 4), (3, 0, 4), (4, 0, 8), (5, 0, 4)],
            slots_c,
        )
        sc = Scatter(*grads_c)
        sc.split()
        gp, sc.out = lax.optimization_barrier((gp, sc.out))
        sc.one()
    dh, hb_sum, db_sum, *grads_b = compute_b1(n2, cot, gp, gc, gpos)
    if fast:
        dh, grads_b, sc.r1, sc.got = lax.optimization_barrier((dh, grads_b, sc.r1, sc.got))
        sc.two()
        sb = Scatter(*grads_b)
        sb.split()
        dh, sb.out = lax.optimization_barrier((dh, sb.out))
        sb.one()
    part = width // nf
    dmid, dbr, dt, sums2 = compute_b2(dh, cot, middle, vecs, triple, att, ga, gb, rows, length)
    if fast:
        dt, sb.r1, sc.r2, hb_sum = lax.optimization_barrier((dt, sb.r1, sc.r2, hb_sum))
        sb.two()
        sc.three((sb.got[1],))
    grads_a = compute_ga(normed, attended, dt, dbr, gpos)
    if fast:
        grads_a, sc.r3, sb.r2, dt = lax.optimization_barrier((grads_a, sc.r3, sb.r2, dt))
        sa = Scatter(*grads_a)
        sa.split()
        sb.three((sa.got[1],))
        dt, sa.out, active = lax.optimization_barrier((dt, sa.out, active))
        sa.one()
        mine_c = sc.total()
    input_grad, sums = compute_b4(tok, emb, dmid, dt, vecs, sums2, db_sum, ga, rows, length)
    if fast:
        hb_lanes = tie(hb_sum, sa.out).reshape(nf, 4 * part)
        sa.r1, sums, active, mine_c, hb_lanes, sb.r3 = lax.optimization_barrier(
            (sa.r1, sums, active, mine_c, hb_lanes, sb.r3)
        )
        sa.add_two()
        sums = tie(sums, sa.on)

    lines = sums.shape[0]
    if not fast:
        hb_lanes = hb_sum.reshape(nf, 4 * part)
    lanes = sums.reshape(lines, nf, part).transpose(1, 0, 2).reshape(nf, lines * part)
    payload = jnp.concatenate([lanes, hb_lanes, marks], axis=1)
    nt, end = rows * part, payload.shape[1] - rows
    if fast:
        sa.send_two()
        everyone = jnp.broadcast_to(payload[None], (nd,) + payload.shape).reshape(nd * nf, payload.shape[1])
        moved = lax.all_to_all(everyone, ("dp", "fsdp"), 0, 0, tiled=True)
        mine_b = sb.total()
        sa.r2, mine_b, mine_c, active = lax.optimization_barrier((sa.r2, mine_b, mine_c, active))
        sa.three()
        result = compute_f3(tie(active, sa.h3), middle, vecs, gc)
        mine_b, mine_c = tie((mine_b, mine_c), sa.h3)
        out_bc = columns(jnp.concatenate([mine_b, mine_c], axis=0))
    else:
        moved = lax.all_to_all(payload, "fsdp", 0, 0, tiled=True)
        moved = lax.all_gather(moved, "dp", axis=0, tiled=True)
    table_rows = moved[:, :nt].reshape(nd * nf * rows, part)
    all_ids = moved[:, end:].astype(jnp.int32).reshape(1, nd * nf * rows)
    vec_sums = jnp.sum(moved[:, nt:end], axis=0)
    if not fast:
        result = compute_f3(active, middle, vecs, gc)
    if fast:
        sa.r3, out_bc, moved, result = lax.optimization_barrier((sa.r3, out_bc, moved, result))
        out_a = quarters(spread(sa.total()), d)
        out_b = out_bc[:, :b].astype(f32)
        down_grad = out_bc[:, b:].astype(f32).reshape(4 * b, width)
    else:
        out_b = plain_scatter(*grads_b)
        out_a = plain_scatter(*grads_a)
        down_grad = plain_scatter(*grads_c, rows_first=True)
    hidden_grad = jnp.concatenate([out_b[i] for i in range(4)], axis=1)
    triple_grad = jnp.concatenate([out_a[i] for i in range(3)], axis=1)
    output_grad = out_a[3]
    all_hot = (steps[:, None] == all_ids).astype(f32)
    table_grad = jnp.dot(all_hot, table_rows, precision=highest)
    v = [vec_sums[i * part : (i + 1) * part] for i in (5, 6, 4, 0, 1, 2, 3, 7)]
    hidden_bias_grad = vec_sums[(lines - rows) * part :]
    shape = tokens.shape
    return (
        result.reshape(shape), input_grad.reshape(shape), table_grad, triple_grad, v[0], v[1], output_grad, v[2],
        v[3], v[4], v[5], v[6], hidden_grad, hidden_bias_grad, down_grad, v[7],
    )


def solution(mesh):
    fast = mesh.shape["dp"] == 4 and mesh.shape["fsdp"] == 8
    batch = ("dp", "fsdp")
    vec, mat, tab = P("fsdp"), P("fsdp", None), P(None, "fsdp")
    tokens_spec = P(None, batch, None, None)
    return jax.shard_map(
        functools.partial(per_device, fast),
        mesh=mesh,
        in_specs=(
            tokens_spec, P(None, batch), P(None, batch, None), P(None, batch, None), tokens_spec,
            tab, mat, vec, vec, mat, vec, vec, vec, vec, vec, mat, vec, mat, vec,
        ),
        out_specs=(
            tokens_spec, tokens_spec, tab, mat, vec, vec, mat, vec, vec, vec, vec, vec, mat, vec, mat, vec,
        ),
        check_vma=False,
    )
```
